128 devices in a mesh: grp: 4 (over x_lo, core), slab: 32 (over y, z, x_hi).
Axes of the slice: x: 4 (x_hi: 2, x_lo: 2; x = x_hi * 2 + x_lo), y: 4, z: 4, core: 2. Of those that a mesh axis runs over, the one named last changes fastest.
Arguments:
- states: bfloat16 [128, 1024, 4096], P('grp', 'slab'), may hold values from -6 to 6
- core_density: float32 [1024, 4096], P('slab'), may hold values from 0.0015 to 0.032
- occupancy: int32 [128], P('grp'), may hold values from 1 to 8
Outputs:
- applied: bfloat16 [128, 1024, 4096], P('grp', 'slab')
- potential: float32 [1024, 4096], P('slab')
The draws below stay inside these ranges and needn't reach their ends.
All inputs are finite; a program needn't handle non-finite values.
Results may differ from the reference program's by a relative error of at most 0.005.
Values sent between devices are 32-bit elements; how exact they have to be, the bound alone decides.
A program may use at most 128 MiB of HBM per device.

```python
import math
import jax
import jax.numpy as jnp

NX = 64
NY = 64
OCC_DEN = 8
NS = 128
NZ = 1024
CELLS = 4096


def draw_core_density(key, part):
    first_key = jax.random.fold_in(key, 11)
    zpos = jnp.arange(NZ).astype(jnp.float32)
    layer = 0.004 * (1.0 + 1.5 * (1.0 + jnp.cos(2.0 * math.pi * 40.0 * zpos / NZ)))
    spread = jax.random.uniform(first_key, (NZ, CELLS), jnp.float32, math.log(0.5), math.log(2.0))
    core = layer[:, None] * jnp.exp(spread)
    return core.astype(jnp.float32)


def with_ends(entries, rng, low, high):
    place = [jax.random.randint(jax.random.fold_in(rng, axis), (), 0, length) for axis, length in enumerate(entries.shape)]
    main_axis = entries.shape.index(max(entries.shape))
    neighbour = place[:main_axis] + [(place[main_axis] + 1) % entries.shape[main_axis]] + place[main_axis + 1:]
    return entries.at[tuple(place)].set(low).at[tuple(neighbour)].set(high)


def shard_levels(stream_key, dims, shards, least, largest):
    level = 1.0
    for axis_at, parts in shards:
        draws = jax.random.uniform(jax.random.fold_in(jax.random.fold_in(stream_key, 6), axis_at), (parts,), jnp.float32, least / len(shards), largest / len(shards))
        level = level * jnp.repeat(jnp.exp(draws), dims[axis_at] // parts).reshape((-1,) + (1,) * (len(dims) - 1 - axis_at))
    return level


def gaussian(own_key, extent, deviation, limit, shards=(), kind=jnp.bfloat16):
    entries = jax.random.normal(own_key, extent, jnp.float32) * deviation
    if len(shards) > 0:
        entries = shard_levels(own_key, extent, shards, -0.22, 0.18) * entries
    return jnp.clip(entries, min=-limit, max=limit).astype(kind)


def setup_inputs(seed: int = 0) -> dict:
    keys = jax.random.split(jax.random.key(seed), 4)
    states = gaussian(keys[0], (NS, NZ, CELLS), 1.0, 6.0, ((0, 4), (1, 32)))
    core_density = draw_core_density(jax.random.fold_in(keys[3], 71), 0)
    occupancy = with_ends(jax.random.randint(keys[2], (NS,), 1, OCC_DEN + 1), jax.random.fold_in(keys[2], 1), 1, OCC_DEN).astype(jnp.int32)
    return dict(states=states, core_density=core_density, occupancy=occupancy)


grid_step = 0.5
valence_norm = 0.04

def energy(dens, sig):
    unif = -0.75 * (3.0 / math.pi) ** (1.0 / 3.0) * dens ** (4.0 / 3.0)
    reduced = sig / (4.0 * (3.0 * math.pi ** 2) ** (2.0 / 3.0) * dens ** (8.0 / 3.0))
    enhance = 1.0 + 0.804 - 0.804 / (1.0 + 0.2195149727645171 * reduced / 0.804)
    return unif * enhance

def total_energy(dens, sig):
    return jnp.sum(energy(dens, sig))

def fourth(field, axis):
    first = jnp.roll(field, 2, axis)
    second = jnp.roll(field, 1, axis)
    third = jnp.roll(field, -1, axis)
    fourth_part = jnp.roll(field, -2, axis)
    return (first - 8.0 * second + 8.0 * third - fourth_part) / (12.0 * grid_step)

def reference(states, core_density, occupancy):
    weight = valence_norm * occupancy.astype(jnp.float32) / (OCC_DEN * NS)
    wide = states.astype(jnp.float32)
    summed = jnp.einsum('s,szc->zc', weight, wide * wide)
    density = (core_density + summed).reshape(NZ, NX, NY)
    grad_z = fourth(density, 0)
    grad_x = fourth(density, 1)
    grad_y = fourth(density, 2)
    sigma = grad_x * grad_x + grad_y * grad_y + grad_z * grad_z
    d_dens, d_sig = jax.grad(total_energy, (0, 1))(density, sigma)
    flow_z = 2.0 * d_sig * grad_z
    flow_x = 2.0 * d_sig * grad_x
    flow_y = 2.0 * d_sig * grad_y
    divergence = fourth(flow_x, 1) + fourth(flow_y, 2) + fourth(flow_z, 0)
    potential = (d_dens - divergence).reshape(NZ, CELLS)
    applied = (potential[None] * wide).astype(jnp.bfloat16)
    return (applied, potential)
```

```python
import functools
import math

import jax
import jax.numpy as jnp
from jax import lax
from jax.experimental import pallas as pl
from jax.experimental.pallas import tpu as pltpu
from jax.sharding import PartitionSpec as P

MESH = pl.DeviceIdType.MESH

NX = 64
NY = 64
OCC_DEN = 8
LANES = 128

grid_step = 0.5
valence_norm = 0.04

kappa = 0.804
mu = 0.2195149727645171
exchange = -0.75 * (3.0 / math.pi) ** (1.0 / 3.0)
reduced_scale = 4.0 * (3.0 * math.pi**2) ** (2.0 / 3.0)
stencil_scale = 1.0 / (12.0 * grid_step)
u_scale = mu / kappa / reduced_scale * stencil_scale * stencil_scale
flow_scale = 2.0 * exchange * mu / reduced_scale * stencil_scale * stencil_scale
slope_scale = exchange * 4.0 / 3.0

CHUNKS = 8


def stencil(before2, before1, after1, after2):
    return (before2 - after2) + 8.0 * (after1 - before1)


def swap_halves(tile):
    return pltpu.roll(tile, 64, 1)


def along_y(tile, swapped, inner):
    before2 = pltpu.roll(jnp.where(inner >= NY - 2, swapped, tile), 2, 1)
    before1 = pltpu.roll(jnp.where(inner >= NY - 1, swapped, tile), 1, 1)
    after1 = pltpu.roll(jnp.where(inner < 1, swapped, tile), LANES - 1, 1)
    after2 = pltpu.roll(jnp.where(inner < 2, swapped, tile), LANES - 2, 1)
    return stencil(before2, before1, after1, after2)


def along_x(left, left_swapped, swapped, right, right_swapped, low):
    before1 = jnp.where(low, left_swapped, swapped)
    after1 = jnp.where(low, swapped, right_swapped)
    return stencil(left, before1, after1, right)


def along_z(tile):
    rows = tile.shape[0]
    return stencil(
        pltpu.roll(tile, 2, 0),
        pltpu.roll(tile, 1, 0),
        pltpu.roll(tile, rows - 1, 0),
        pltpu.roll(tile, rows - 2, 0),
    )


def potential_kernel(
    slabs,
    occ_ref,
    states_ref,
    core_ref,
    held_ref,
    pot_ref,
    part,
    from_core,
    chip_sum,
    from_chip,
    core_half,
    dens,
    above,
    below,
    flow_x,
    local,
    load_sem,
    core_sem,
    core_send,
    core_recv,
    chip_send,
    chip_recv,
    up_send,
    up_recv,
    down_send,
    down_recv,
    pot_send,
    pot_recv,
):
    s_dev, planes, cells = states_ref.shape
    half = planes // 2
    width = cells // CHUNKS
    tiles = width // LANES
    n_tiles = cells // LANES

    grp = lax.axis_index("grp")
    slab = lax.axis_index("slab")
    chip = grp // 2
    core = grp % 2
    core_peer = {"grp": chip * 2 + 1 - core, "slab": slab}
    chip_peer = {"grp": (1 - chip) * 2 + core, "slab": slab}
    up_peer = {
        "grp": (chip * (1 - core) + (1 - chip) * core) * 2 + 1 - core,
        "slab": (slab + core) % slabs,
    }
    down_peer = {
        "grp": (chip * core + (1 - chip) * (1 - core)) * 2 + 1 - core,
        "slab": (slab + slabs - 1 + core) % slabs,
    }
    slab_peer = {
        "grp": (1 - chip) * 2 + 1 - core,
        "slab": (slab + slabs - 1 + 2 * core) % slabs,
    }

    def cols(i):
        return pl.ds(pl.multiple_of(i * width, LANES), width)

    def load(i):
        return pltpu.make_async_copy(
            states_ref.at[:, :, cols(i)], held_ref.at[:, :, cols(i)], load_sem.at[i]
        )

    def remote(src, dst, send, recv, peer, i):
        return pltpu.make_async_remote_copy(
            src_ref=src,
            dst_ref=dst,
            send_sem=send.at[i],
            recv_sem=recv.at[i],
            device_id=peer,
            device_id_type=MESH,
        )

    def to_core(i):
        return remote(
            part.at[1 - core, :, cols(i)], from_core.at[:, cols(i)], core_send, core_recv, core_peer, i
        )

    def to_chip(i):
        return remote(chip_sum.at[:, cols(i)], from_chip.at[:, cols(i)], chip_send, chip_recv, chip_peer, i)

    def to_up(i):
        return remote(dens.at[pl.ds(half - 8, 8), cols(i)], below.at[:, cols(i)], up_send, up_recv, up_peer, i)

    def to_down(i):
        return remote(dens.at[pl.ds(0, 8), cols(i)], above.at[:, cols(i)], down_send, down_recv, down_peer, i)

    def own_rows():
        return pl.ds(pl.multiple_of(core * half, half), half)

    def to_pot(i):
        where = pot_ref.at[own_rows(), cols(i)]
        return remote(where, where, pot_send, pot_recv, core_peer, i)

    core_copy = pltpu.make_async_copy(core_ref.at[own_rows(), :], core_half, core_sem)
    for i in range(CHUNKS):
        load(i).start()
    core_copy.start()

    barrier = pltpu.get_barrier_semaphore()
    for peer in (core_peer, chip_peer, slab_peer):
        pl.semaphore_signal(barrier, inc=1, device_id=peer, device_id_type=MESH)

    weights = [
        occ_ref[s].astype(jnp.float32) * (valence_norm / (OCC_DEN * s_dev * 4))
        for s in range(s_dev)
    ]

    def density_part(i):
        def tile_step(t, carry):
            lanes = pl.ds(pl.multiple_of(i * width + t * LANES, LANES), LANES)
            total = jnp.zeros((planes, LANES), jnp.float32)
            for s in range(s_dev):
                wide = held_ref[s, :, lanes].astype(jnp.float32)
                total = total + (wide * weights[s]) * wide
            part[0, :, lanes] = total[:half]
            part[1, :, lanes] = total[half:]
            return carry

        lax.fori_loop(0, tiles, tile_step, 0)

    def chip_part(i):
        to_core(i).wait_recv()
        chip_sum[:, cols(i)] = part[core, :, cols(i)] + from_core[:, cols(i)]
        to_chip(i).start()

    for i in range(CHUNKS):
        load(i).wait()
        density_part(i)
        if i == 0:
            pl.semaphore_wait(barrier, 3)
        to_core(i).start()
        if i > 0:
            chip_part(i - 1)
    chip_part(CHUNKS - 1)
    core_copy.wait()

    lane = lax.broadcasted_iota(jnp.int32, (1, LANES), 1)
    inner = lane % NY
    low = lane < NY
    upper_row = lax.broadcasted_iota(jnp.int32, (8, LANES), 0) < 4

    def field(t):
        lanes = pl.ds(pl.multiple_of((t % n_tiles) * LANES, LANES), LANES)
        edge = jnp.where(upper_row, above[:, lanes], below[:, lanes])
        return jnp.concatenate([dens[:, lanes], edge], axis=0)

    def flow_step(t, carry):
        centre = field(t)
        left = field(t + n_tiles - 1)
        right = field(t + 1)
        swapped = swap_halves(centre)
        grad_x = along_x(left, swap_halves(left), swapped, right, swap_halves(right), low)
        grad_y = along_y(centre, swapped, inner)
        grad_z = along_z(centre)
        sigma = grad_x * grad_x + grad_y * grad_y + grad_z * grad_z
        root = jnp.exp2(jnp.log2(centre) * (-1.0 / 3.0))
        root2 = root * root
        root4 = root2 * root2
        share = 1.0 / (1.0 + u_scale * (sigma * (root4 * root4)))
        flow = flow_scale * (root4 * (share * share))
        d_dens = (slope_scale * (centre * root2)) * (
            (1.0 + kappa) + share * (2.0 * kappa * share - 3.0 * kappa)
        )
        flow_y = flow * grad_y
        div_y = along_y(flow_y[:half], swap_halves(flow_y[:half]), inner)
        div_z = along_z(flow * grad_z)[:half]
        lanes = pl.ds(pl.multiple_of((t % n_tiles) * LANES, LANES), LANES)
        flow_x[:, lanes] = (flow * grad_x)[:half]
        local[:, lanes] = d_dens[:half] - (div_y + div_z)
        return carry

    def pot_step(t, carry):
        def at(k):
            return flow_x[:, pl.ds(pl.multiple_of((k % n_tiles) * LANES, LANES), LANES)]

        lanes = pl.ds(pl.multiple_of((t % n_tiles) * LANES, LANES), LANES)
        left, centre, right = at(t + n_tiles - 1), at(t), at(t + 1)
        div_x = along_x(
            left, swap_halves(left), swap_halves(centre), right, swap_halves(right), low
        )
        pot_ref[own_rows(), lanes] = local[:, lanes] - div_x
        return carry

    for i in range(CHUNKS):
        to_chip(i).wait_recv()
        dens[:, cols(i)] = (chip_sum[:, cols(i)] + from_chip[:, cols(i)]) + core_half[:, cols(i)]
        to_up(i).start()
        to_down(i).start()

    for i in range(CHUNKS):
        to_up(i).wait_recv()
        to_down(i).wait_recv()

    lax.fori_loop(0, n_tiles, flow_step, 0)
    for i in range(CHUNKS):
        lax.fori_loop(i * tiles, (i + 1) * tiles, pot_step, 0)
        to_pot(i).start()
    for i in range(CHUNKS):
        to_core(i).wait_send()
        to_chip(i).wait_send()
        to_up(i).wait_send()
        to_down(i).wait_send()
        to_pot(i).wait()


def apply_kernel(held_ref, pot_ref, applied_ref, out_ref, staged, store_sem, pot_sem):
    s_dev, planes, cells = held_ref.shape
    width = cells // CHUNKS
    pot_copy = pltpu.make_async_copy(pot_ref, out_ref, pot_sem)
    pot_copy.start()

    def store(i):
        cols = pl.ds(i * width, width)
        return pltpu.make_async_copy(staged.at[:, :, cols], applied_ref.at[:, :, cols], store_sem.at[i])

    for i in range(CHUNKS):
        for t in range(width // LANES):
            lanes = pl.ds(i * width + t * LANES, LANES)
            pot = pot_ref[:, lanes]

            def state_step(s, carry):
                staged[s, :, lanes] = (held_ref[s, :, lanes].astype(jnp.float32) * pot).astype(jnp.bfloat16)
                return carry

            lax.fori_loop(0, s_dev, state_step, 0, unroll=8)
        store(i).start()
    for i in range(CHUNKS):
        store(i).wait()
    pot_copy.wait()


def body(slabs, states, core_density, occupancy):
    s_dev, planes, cells = states.shape
    half = planes // 2
    vmem = pl.BlockSpec(memory_space=pltpu.VMEM)
    anywhere = pl.BlockSpec(memory_space=pltpu.HBM)
    pair = pltpu.SemaphoreType.DMA((CHUNKS,))
    states = pltpu.with_memory_space_constraint(states, pltpu.HBM)
    core_density = pltpu.with_memory_space_constraint(core_density, pltpu.HBM)
    held, pot = pl.pallas_call(
        functools.partial(potential_kernel, slabs),
        out_shape=(
            pltpu.VMEM((s_dev, planes, cells), jnp.bfloat16),
            pltpu.VMEM((planes, cells), jnp.float32),
        ),
        in_specs=[pl.BlockSpec(memory_space=pltpu.SMEM), anywhere, anywhere],
        out_specs=(vmem, vmem),
        scratch_shapes=[
            pltpu.VMEM((2, half, cells), jnp.float32),
            pltpu.VMEM((half, cells), jnp.float32),
            pltpu.VMEM((half, cells), jnp.float32),
            pltpu.VMEM((half, cells), jnp.float32),
            pltpu.VMEM((half, cells), jnp.float32),
            pltpu.VMEM((half, cells), jnp.float32),
            pltpu.VMEM((8, cells), jnp.float32),
            pltpu.VMEM((8, cells), jnp.float32),
            pltpu.VMEM((half, cells), jnp.float32),
            pltpu.VMEM((half, cells), jnp.float32),
            pair,
            pltpu.SemaphoreType.DMA,
        ]
        + [pair] * 10,
        compiler_params=pltpu.CompilerParams(
            collective_id=0, has_side_effects=True, vmem_limit_bytes=24 * 1024 * 1024
        ),
        name="potential",
    )(occupancy, states, core_density)
    return pl.pallas_call(
        apply_kernel,
        out_shape=(
            jax.ShapeDtypeStruct((s_dev, planes, cells), jnp.bfloat16),
            jax.ShapeDtypeStruct((planes, cells), jnp.float32),
        ),
        in_specs=[vmem, vmem],
        out_specs=(anywhere, anywhere),
        scratch_shapes=[
            pltpu.VMEM((s_dev, planes, cells), jnp.bfloat16),
            pair,
            pltpu.SemaphoreType.DMA,
        ],
        compiler_params=pltpu.CompilerParams(vmem_limit_bytes=32 * 1024 * 1024),
        name="apply",
    )(held, pot)


def solution(mesh):
    placed = (P("grp", "slab", None), P("slab", None), P("grp"))
    return jax.shard_map(
        functools.partial(body, mesh.shape["slab"]),
        mesh=mesh,
        in_specs=placed,
        out_specs=(P("grp", "slab", None), P("slab", None)),
        check_vma=False,
    )
```

```python
import functools
import math

import jax
import jax.numpy as jnp
from jax import lax
from jax.experimental import pallas as pl
from jax.experimental.pallas import tpu as pltpu
from jax.sharding import PartitionSpec as P

MESH = pl.DeviceIdType.MESH

NX = 64
NY = 64
OCC_DEN = 8
LANES = 128

grid_step = 0.5
valence_norm = 0.04

kappa = 0.804
mu = 0.2195149727645171
exchange = -0.75 * (3.0 / math.pi) ** (1.0 / 3.0)
reduced_scale = 4.0 * (3.0 * math.pi**2) ** (2.0 / 3.0)
stencil_scale = 1.0 / (12.0 * grid_step)
u_scale = mu / kappa / reduced_scale * stencil_scale * stencil_scale
flow_scale = 2.0 * exchange * mu / reduced_scale * stencil_scale * stencil_scale
slope_scale = exchange * 4.0 / 3.0

CHUNKS = 8


def stencil(before2, before1, after1, after2):
    return (before2 - after2) + 8.0 * (after1 - before1)


def swap_halves(tile):
    return pltpu.roll(tile, 64, 1)


def along_y(tile, swapped, inner):
    before2 = pltpu.roll(jnp.where(inner >= NY - 2, swapped, tile), 2, 1)
    before1 = pltpu.roll(jnp.where(inner >= NY - 1, swapped, tile), 1, 1)
    after1 = pltpu.roll(jnp.where(inner < 1, swapped, tile), LANES - 1, 1)
    after2 = pltpu.roll(jnp.where(inner < 2, swapped, tile), LANES - 2, 1)
    return stencil(before2, before1, after1, after2)


def along_x(left, left_swapped, swapped, right, right_swapped, low):
    before1 = jnp.where(low, left_swapped, swapped)
    after1 = jnp.where(low, swapped, right_swapped)
    return stencil(left, before1, after1, right)


def along_z(tile):
    rows = tile.shape[0]
    return stencil(
        pltpu.roll(tile, 2, 0),
        pltpu.roll(tile, 1, 0),
        pltpu.roll(tile, rows - 1, 0),
        pltpu.roll(tile, rows - 2, 0),
    )


def potential_kernel(
    slabs,
    occ_ref,
    states_ref,
    core_ref,
    held_ref,
    pot_ref,
    part,
    from_core,
    chip_sum,
    from_chip,
    core_half,
    dens,
    above,
    below,
    flow_x,
    local,
    load_sem,
    core_sem,
    core_send,
    core_recv,
    chip_send,
    chip_recv,
    up_send,
    up_recv,
    down_send,
    down_recv,
    pot_send,
    pot_recv,
):
    s_dev, planes, cells = states_ref.shape
    half = planes // 2
    width = cells // CHUNKS
    tiles = width // LANES
    n_tiles = cells // LANES

    grp = lax.axis_index("grp")
    slab = lax.axis_index("slab")
    chip = grp // 2
    core = grp % 2
    core_peer = {"grp": chip * 2 + 1 - core, "slab": slab}
    chip_peer = {"grp": (1 - chip) * 2 + core, "slab": slab}
    up_peer = {
        "grp": (chip * (1 - core) + (1 - chip) * core) * 2 + 1 - core,
        "slab": (slab + core) % slabs,
    }
    down_peer = {
        "grp": (chip * core + (1 - chip) * (1 - core)) * 2 + 1 - core,
        "slab": (slab + slabs - 1 + core) % slabs,
    }
    slab_peer = {
        "grp": (1 - chip) * 2 + 1 - core,
        "slab": (slab + slabs - 1 + 2 * core) % slabs,
    }

    def cols(i):
        return pl.ds(pl.multiple_of(i * width, LANES), width)

    def load(i):
        return pltpu.make_async_copy(
            states_ref.at[:, :, cols(i)], held_ref.at[:, :, cols(i)], load_sem.at[i]
        )

    def remote(src, dst, send, recv, peer, i):
        return pltpu.make_async_remote_copy(
            src_ref=src,
            dst_ref=dst,
            send_sem=send.at[i],
            recv_sem=recv.at[i],
            device_id=peer,
            device_id_type=MESH,
        )

    def to_core(i):
        return remote(
            part.at[1 - core, :, cols(i)], from_core.at[:, cols(i)], core_send, core_recv, core_peer, i
        )

    def to_chip(i):
        return remote(chip_sum.at[:, cols(i)], from_chip.at[:, cols(i)], chip_send, chip_recv, chip_peer, i)

    def to_up(i):
        return remote(dens.at[pl.ds(half - 8, 8), cols(i)], below.at[:, cols(i)], up_send, up_recv, up_peer, i)

    def to_down(i):
        return remote(dens.at[pl.ds(0, 8), cols(i)], above.at[:, cols(i)], down_send, down_recv, down_peer, i)

    def own_rows():
        return pl.ds(pl.multiple_of(core * half, half), half)

    def to_pot(i):
        where = pot_ref.at[own_rows(), cols(i)]
        return remote(where, where, pot_send, pot_recv, core_peer, i)

    core_copy = pltpu.make_async_copy(core_ref.at[own_rows(), :], core_half, core_sem)
    for i in range(CHUNKS):
        load(i).start()
    core_copy.start()

    barrier = pltpu.get_barrier_semaphore()
    for peer in (core_peer, chip_peer, slab_peer):
        pl.semaphore_signal(barrier, inc=1, device_id=peer, device_id_type=MESH)

    weights = [
        occ_ref[s].astype(jnp.float32) * (valence_norm / (OCC_DEN * s_dev * 4))
        for s in range(s_dev)
    ]

    def density_part(i):
        def tile_step(t, carry):
            lanes = pl.ds(pl.multiple_of(i * width + t * 2 * LANES, LANES), 2 * LANES)
            total = jnp.zeros((planes, 2 * LANES), jnp.float32)
            for s in range(s_dev):
                wide = held_ref[s, :, lanes].astype(jnp.float32)
                total = total + (wide * weights[s]) * wide
            part[0, :, lanes] = total[:half]
            part[1, :, lanes] = total[half:]
            return carry

        lax.fori_loop(0, tiles // 2, tile_step, 0)

    def chip_part(i):
        to_core(i).wait_recv()
        chip_sum[:, cols(i)] = part[core, :, cols(i)] + from_core[:, cols(i)]
        to_chip(i).start()

    for i in range(CHUNKS):
        load(i).wait()
        density_part(i)
        if i == 0:
            pl.semaphore_wait(barrier, 3)
        to_core(i).start()
        if i > 0:
            chip_part(i - 1)
    chip_part(CHUNKS - 1)
    core_copy.wait()

    lane = lax.broadcasted_iota(jnp.int32, (1, LANES), 1)
    inner = lane % NY
    low = lane < NY
    upper_row = lax.broadcasted_iota(jnp.int32, (8, LANES), 0) < 4

    def field(t):
        lanes = pl.ds(pl.multiple_of((t % n_tiles) * LANES, LANES), LANES)
        edge = jnp.where(upper_row, above[:, lanes], below[:, lanes])
        return jnp.concatenate([dens[:, lanes], edge], axis=0)

    def flow_step(t, carry):
        centre = field(t)
        left = field(t + n_tiles - 1)
        right = field(t + 1)
        swapped = swap_halves(centre)
        grad_x = along_x(left, swap_halves(left), swapped, right, swap_halves(right), low)
        grad_y = along_y(centre, swapped, inner)
        grad_z = along_z(centre)
        sigma = grad_x * grad_x + grad_y * grad_y + grad_z * grad_z
        root = jnp.exp2(jnp.log2(centre) * (-1.0 / 3.0))
        root2 = root * root
        root4 = root2 * root2
        share = 1.0 / (1.0 + u_scale * (sigma * (root4 * root4)))
        flow = flow_scale * (root4 * (share * share))
        d_dens = (slope_scale * (centre * root2)) * (
            (1.0 + kappa) + share * (2.0 * kappa * share - 3.0 * kappa)
        )
        flow_y = flow * grad_y
        div_y = along_y(flow_y[:half], swap_halves(flow_y[:half]), inner)
        div_z = along_z(flow * grad_z)[:half]
        lanes = pl.ds(pl.multiple_of((t % n_tiles) * LANES, LANES), LANES)
        flow_x[:, lanes] = (flow * grad_x)[:half]
        local[:, lanes] = d_dens[:half] - (div_y + div_z)
        return carry

    def pot_step(t, carry):
        def at(k):
            return flow_x[:, pl.ds(pl.multiple_of((k % n_tiles) * LANES, LANES), LANES)]

        lanes = pl.ds(pl.multiple_of((t % n_tiles) * LANES, LANES), LANES)
        left, centre, right = at(t + n_tiles - 1), at(t), at(t + 1)
        div_x = along_x(
            left, swap_halves(left), swap_halves(centre), right, swap_halves(right), low
        )
        pot_ref[own_rows(), lanes] = local[:, lanes] - div_x
        return carry

    for i in range(CHUNKS):
        to_chip(i).wait_recv()
        dens[:, cols(i)] = (chip_sum[:, cols(i)] + from_chip[:, cols(i)]) + core_half[:, cols(i)]
        to_up(i).start()
        to_down(i).start()

    for i in range(CHUNKS):
        to_up(i).wait_recv()
        to_down(i).wait_recv()

    lax.fori_loop(0, n_tiles, flow_step, 0, unroll=8)
    for i in range(CHUNKS):
        lax.fori_loop(i * tiles, (i + 1) * tiles, pot_step, 0, unroll=True)
        to_pot(i).start()
    for i in range(CHUNKS):
        to_core(i).wait_send()
        to_chip(i).wait_send()
        to_up(i).wait_send()
        to_down(i).wait_send()
        to_pot(i).wait()


def apply_kernel(held_ref, pot_ref, applied_ref, out_ref, staged, store_sem, pot_sem):
    s_dev, planes, cells = held_ref.shape
    width = cells // CHUNKS
    pot_copy = pltpu.make_async_copy(pot_ref, out_ref, pot_sem)
    pot_copy.start()

    def store(i):
        cols = pl.ds(i * width, width)
        return pltpu.make_async_copy(staged.at[:, :, cols], applied_ref.at[:, :, cols], store_sem.at[i])

    for i in range(CHUNKS):
        cols = pl.ds(i * width, width)
        pot = pot_ref[:, cols].astype(jnp.bfloat16)

        def state_step(s, carry):
            staged[s, :, cols] = held_ref[s, :, cols] * pot
            return carry

        lax.fori_loop(0, s_dev, state_step, 0, unroll=8)
        store(i).start()
    for i in range(CHUNKS):
        store(i).wait()
    pot_copy.wait()


def body(slabs, states, core_density, occupancy):
    s_dev, planes, cells = states.shape
    half = planes // 2
    vmem = pl.BlockSpec(memory_space=pltpu.VMEM)
    anywhere = pl.BlockSpec(memory_space=pltpu.HBM)
    pair = pltpu.SemaphoreType.DMA((CHUNKS,))
    states = pltpu.with_memory_space_constraint(states, pltpu.HBM)
    core_density = pltpu.with_memory_space_constraint(core_density, pltpu.HBM)
    held, pot = pl.pallas_call(
        functools.partial(potential_kernel, slabs),
        out_shape=(
            pltpu.VMEM((s_dev, planes, cells), jnp.bfloat16),
            pltpu.VMEM((planes, cells), jnp.float32),
        ),
        in_specs=[pl.BlockSpec(memory_space=pltpu.SMEM), anywhere, anywhere],
        out_specs=(vmem, vmem),
        scratch_shapes=[
            pltpu.VMEM((2, half, cells), jnp.float32),
            pltpu.VMEM((half, cells), jnp.float32),
            pltpu.VMEM((half, cells), jnp.float32),
            pltpu.VMEM((half, cells), jnp.float32),
            pltpu.VMEM((half, cells), jnp.float32),
            pltpu.VMEM((half, cells), jnp.float32),
            pltpu.VMEM((8, cells), jnp.float32),
            pltpu.VMEM((8, cells), jnp.float32),
            pltpu.VMEM((half, cells), jnp.float32),
            pltpu.VMEM((half, cells), jnp.float32),
            pair,
            pltpu.SemaphoreType.DMA,
        ]
        + [pair] * 10,
        compiler_params=pltpu.CompilerParams(
            collective_id=0, has_side_effects=True, vmem_limit_bytes=24 * 1024 * 1024
        ),
        name="potential",
    )(occupancy, states, core_density)
    return pl.pallas_call(
        apply_kernel,
        out_shape=(
            jax.ShapeDtypeStruct((s_dev, planes, cells), jnp.bfloat16),
            jax.ShapeDtypeStruct((planes, cells), jnp.float32),
        ),
        in_specs=[vmem, vmem],
        out_specs=(anywhere, anywhere),
        scratch_shapes=[
            pltpu.VMEM((s_dev, planes, cells), jnp.bfloat16),
            pair,
            pltpu.SemaphoreType.DMA,
        ],
        compiler_params=pltpu.CompilerParams(vmem_limit_bytes=32 * 1024 * 1024),
        name="apply",
    )(held, pot)


def solution(mesh):
    placed = (P("grp", "slab", None), P("slab", None), P("grp"))
    return jax.shard_map(
        functools.partial(body, mesh.shape["slab"]),
        mesh=mesh,
        in_specs=placed,
        out_specs=(P("grp", "slab", None), P("slab", None)),
        check_vma=False,
    )
```

```python
import functools
import math

import jax
import jax.numpy as jnp
from jax import lax
from jax.experimental import pallas as pl
from jax.experimental.pallas import tpu as pltpu
from jax.sharding import PartitionSpec as P

MESH = pl.DeviceIdType.MESH

NX = 64
NY = 64
OCC_DEN = 8
LANES = 128

grid_step = 0.5
valence_norm = 0.04

kappa = 0.804
mu = 0.2195149727645171
exchange = -0.75 * (3.0 / math.pi) ** (1.0 / 3.0)
reduced_scale = 4.0 * (3.0 * math.pi**2) ** (2.0 / 3.0)
stencil_scale = 1.0 / (12.0 * grid_step)
u_scale = mu / kappa / reduced_scale * stencil_scale * stencil_scale
flow_scale = 2.0 * exchange * mu / reduced_scale * stencil_scale * stencil_scale
slope_scale = exchange * 4.0 / 3.0

CHUNKS = 4
STEP = 4 * LANES
STORES = 8


def stencil(before2, before1, after1, after2):
    return (before2 - after2) + 8.0 * (after1 - before1)


def swap_halves(tile):
    return pltpu.roll(tile, 64, 1)


def along_y(tile, swapped, inner):
    before2 = pltpu.roll(jnp.where(inner >= NY - 2, swapped, tile), 2, 1)
    before1 = pltpu.roll(jnp.where(inner >= NY - 1, swapped, tile), 1, 1)
    after1 = pltpu.roll(jnp.where(inner < 1, swapped, tile), LANES - 1, 1)
    after2 = pltpu.roll(jnp.where(inner < 2, swapped, tile), LANES - 2, 1)
    return stencil(before2, before1, after1, after2)


def along_x(left, left_swapped, swapped, right, right_swapped, low):
    before1 = jnp.where(low, left_swapped, swapped)
    after1 = jnp.where(low, swapped, right_swapped)
    return stencil(left, before1, after1, right)


def along_z(tile):
    rows = tile.shape[0]
    return stencil(
        pltpu.roll(tile, 2, 0),
        pltpu.roll(tile, 1, 0),
        pltpu.roll(tile, rows - 1, 0),
        pltpu.roll(tile, rows - 2, 0),
    )


def potential_kernel(
    slabs,
    occ_hbm,
    states_ref,
    core_ref,
    held_ref,
    pot_ref,
    occ_ref,
    part,
    from_core,
    chip_sum,
    from_chip,
    core_half,
    dens,
    inner_in,
    edge_out,
    edge_in,
    outer,
    flow_x,
    local,
    load_sem,
    misc_sem,
    group_sem,
    slab_sem,
    core_send,
    core_recv,
    chip_send,
    chip_recv,
    inner_send,
    inner_recv,
    edge_send,
    edge_recv,
    pot_send,
    pot_recv,
):
    s_dev, planes, cells = states_ref.shape
    half = planes // 2
    width = cells // CHUNKS
    n_tiles = cells // LANES

    grp = lax.axis_index("grp")
    slab = lax.axis_index("slab")
    chip = grp // 2
    core = grp % 2
    core_peer = {"grp": chip * 2 + 1 - core, "slab": slab}
    chip_peer = {"grp": (1 - chip) * 2 + core, "slab": slab}
    cross_peer = {"grp": (1 - chip) * 2 + 1 - core, "slab": slab}
    beyond = (slab + slabs - 1 + 2 * core) % slabs
    edge_chips = (chip, 1 - chip)

    def cols(i):
        return pl.ds(pl.multiple_of(i * width, LANES), width)

    def load(h, i):
        where = (slice(None), pl.ds(h * half, half), cols(i))
        return pltpu.make_async_copy(states_ref.at[where], held_ref.at[where], load_sem.at[h * CHUNKS + i])

    def remote(src, dst, send, recv, peer):
        return pltpu.make_async_remote_copy(
            src_ref=src, dst_ref=dst, send_sem=send, recv_sem=recv, device_id=peer, device_id_type=MESH
        )

    def to_core(i):
        return remote(
            part.at[1 - core, :, cols(i)], from_core.at[:, cols(i)], core_send.at[i], core_recv.at[i], core_peer
        )

    def to_chip(i):
        return remote(
            chip_sum.at[:, cols(i)], from_chip.at[:, cols(i)], chip_send.at[i], chip_recv.at[i], chip_peer
        )

    def to_edge(k):
        peer = {"grp": edge_chips[k] * 2 + 1 - core, "slab": beyond}
        return remote(edge_out, edge_in.at[chip], edge_send.at[k], edge_recv.at[chip], peer)

    def from_edge(k):
        return remote(edge_out, edge_in.at[k], edge_send.at[k], edge_recv.at[k], core_peer)

    def to_inner(i):
        rows = pl.ds(pl.multiple_of((1 - core) * 8, 8), 8)
        return remote(
            dens.at[rows, cols(i)], inner_in.at[:, cols(i)], inner_send.at[i], inner_recv.at[i], core_peer
        )

    def own_rows():
        return pl.ds(pl.multiple_of(core * half, half), half)

    def to_pot(i):
        where = pot_ref.at[own_rows(), cols(i)]
        return remote(where, where, pot_send.at[i], pot_recv.at[i], core_peer)

    occ_copy = pltpu.make_async_copy(occ_hbm, occ_ref, misc_sem.at[0])
    occ_copy.start()
    for h in (1, 0):
        for i in range(CHUNKS):
            load(h, i).start()
    core_copy = pltpu.make_async_copy(core_ref.at[own_rows(), :], core_half, misc_sem.at[1])
    core_copy.start()

    barrier = pltpu.get_barrier_semaphore()

    def greet(peer):
        pl.semaphore_signal(barrier, inc=1, device_id=peer, device_id_type=MESH)

    @pl.when(core == 0)
    def _():
        greet(chip_peer)
        greet({"grp": 1, "slab": beyond})
        greet({"grp": 3, "slab": beyond})

    @pl.when(core == 1)
    def _():
        greet(core_peer)
        greet(cross_peer)
        greet({"grp": 1, "slab": beyond})
        greet({"grp": 3, "slab": beyond})

    occ_copy.wait()
    weights = [
        occ_ref[s].astype(jnp.float32) * (valence_norm / (OCC_DEN * s_dev * 4))
        for s in range(s_dev)
    ]

    def density_part(h, i):
        load(h, i).wait()

        def tile_step(t, carry):
            lanes = pl.ds(pl.multiple_of(i * width + t * STEP, STEP), STEP)
            total = jnp.zeros((half, STEP), jnp.float32)
            for s in range(s_dev):
                wide = held_ref[s, h * half : (h + 1) * half, lanes].astype(jnp.float32)
                total = total + (wide * weights[s]) * wide
            part[h, :, lanes] = total
            return carry

        lax.fori_loop(0, width // STEP, tile_step, 0)

    for i in range(CHUNKS):
        density_part(1, i)

    @pl.when(core == 0)
    def _():
        pl.semaphore_wait(barrier, 3)
        pl.semaphore_signal(group_sem, inc=1, device_id=core_peer, device_id_type=MESH)
        for i in range(CHUNKS):
            to_core(i).start()

    for i in range(CHUNKS):
        density_part(0, i)
        if i == CHUNKS - 2:

            @pl.when(core == 1)
            def _():
                pl.semaphore_wait(group_sem, 1)
                for j in range(CHUNKS - 1):
                    to_core(j).start()

    @pl.when(core == 1)
    def _():
        to_core(CHUNKS - 1).start()

    core_copy.wait()
    first_rows = lax.broadcasted_iota(jnp.int32, (8, LANES), 0) < 4
    with_core = (1 - chip).astype(jnp.float32)
    is_low = core == 0

    for i in range(CHUNKS):
        to_core(i).wait_recv()
        chip_sum[:, cols(i)] = (part[core, :, cols(i)] + from_core[:, cols(i)]) + with_core * core_half[:, cols(i)]
        to_chip(i).start()

    edge_rows = pl.ds(pl.multiple_of(core * 8, 8), 8)
    for t in range(n_tiles // 2):
        front = chip_sum[edge_rows, t * LANES : (t + 1) * LANES]
        back = chip_sum[edge_rows, cells // 2 + t * LANES : cells // 2 + (t + 1) * LANES]
        front_turned, back_turned = pltpu.roll(front, 4, 0), pltpu.roll(back, 4, 0)
        low_edge = jnp.where(first_rows, front, back_turned)
        high_edge = jnp.where(first_rows, front_turned, back)
        edge_out[:, t * LANES : (t + 1) * LANES] = jnp.where(is_low, low_edge, high_edge)

    @pl.when(core == 1)
    def _():
        pl.semaphore_wait(barrier, 4)
        pl.semaphore_signal(slab_sem, inc=1, device_id=core_peer, device_id_type=MESH)

    @pl.when(core == 0)
    def _():
        pl.semaphore_wait(slab_sem, 1)

    for k in range(2):
        to_edge(k).start()

    for i in range(CHUNKS):
        to_chip(i).wait_recv()
        dens[:, cols(i)] = chip_sum[:, cols(i)] + from_chip[:, cols(i)]
        to_inner(i).start()

    for k in range(2):
        from_edge(k).wait_recv()
    for t in range(n_tiles // 2):
        lanes = slice(t * LANES, (t + 1) * LANES)
        both = edge_in[0, :, lanes] + edge_in[1, :, lanes]
        turned = pltpu.roll(both, 4, 0)
        outer[:, t * LANES : (t + 1) * LANES] = jnp.where(first_rows, both, turned)
        outer[:, cells // 2 + t * LANES : cells // 2 + (t + 1) * LANES] = jnp.where(first_rows, turned, both)
    for i in range(CHUNKS):
        to_inner(i).wait_recv()

    lane = lax.broadcasted_iota(jnp.int32, (1, LANES), 1)
    inner = lane % NY
    low = lane < NY
    inner_rows = jnp.where(is_low, first_rows.astype(jnp.int32), 1 - first_rows.astype(jnp.int32)) == 1

    def field(t):
        lanes = pl.ds(pl.multiple_of((t % n_tiles) * LANES, LANES), LANES)
        edge = jnp.where(inner_rows, inner_in[:, lanes], outer[:, lanes])
        return jnp.concatenate([dens[:, lanes], edge], axis=0)

    def flow_step(t, carry):
        centre = field(t)
        left = field(t + n_tiles - 1)
        right = field(t + 1)
        swapped = swap_halves(centre)
        grad_x = along_x(left, swap_halves(left), swapped, right, swap_halves(right), low)
        grad_y = along_y(centre, swapped, inner)
        grad_z = along_z(centre)
        sigma = grad_x * grad_x + grad_y * grad_y + grad_z * grad_z
        root = jnp.exp2(jnp.log2(centre) * (-1.0 / 3.0))
        root2 = root * root
        root4 = root2 * root2
        share = 1.0 / (1.0 + u_scale * (sigma * (root4 * root4)))
        flow = flow_scale * (root4 * (share * share))
        d_dens = (slope_scale * (centre * root2)) * (
            (1.0 + kappa) + share * (2.0 * kappa * share - 3.0 * kappa)
        )
        flow_y = flow * grad_y
        div_y = along_y(flow_y[:half], swap_halves(flow_y[:half]), inner)
        div_z = along_z(flow * grad_z)[:half]
        lanes = pl.ds(pl.multiple_of((t % n_tiles) * LANES, LANES), LANES)
        flow_x[:, lanes] = (flow * grad_x)[:half]
        local[:, lanes] = d_dens[:half] - (div_y + div_z)
        return carry

    def pot_step(t, carry):
        def at(k):
            return flow_x[:, pl.ds(pl.multiple_of((k % n_tiles) * LANES, LANES), LANES)]

        lanes = pl.ds(pl.multiple_of((t % n_tiles) * LANES, LANES), LANES)
        left, centre, right = at(t + n_tiles - 1), at(t), at(t + 1)
        div_x = along_x(
            left, swap_halves(left), swap_halves(centre), right, swap_halves(right), low
        )
        pot_ref[own_rows(), lanes] = local[:, lanes] - div_x
        return carry

    lax.fori_loop(0, n_tiles, flow_step, 0, unroll=8)
    tiles = width // LANES
    for i in range(CHUNKS):
        lax.fori_loop(i * tiles, (i + 1) * tiles, pot_step, 0, unroll=True)
        to_pot(i).start()
    for i in range(CHUNKS):
        to_core(i).wait_send()
        to_chip(i).wait_send()
        to_inner(i).wait_send()
        to_pot(i).wait()
    for k in range(2):
        to_edge(k).wait_send()


def apply_kernel(held_ref, pot_ref, applied_ref, out_ref, staged, store_sem, pot_sem):
    s_dev, planes, cells = held_ref.shape
    width = cells // STORES
    pot_copy = pltpu.make_async_copy(pot_ref, out_ref, pot_sem)
    pot_copy.start()

    def store(i):
        cols = pl.ds(i * width, width)
        return pltpu.make_async_copy(staged.at[:, :, cols], applied_ref.at[:, :, cols], store_sem.at[i])

    for i in range(STORES):
        cols = pl.ds(i * width, width)
        pot = pot_ref[:, cols].astype(jnp.bfloat16)

        def state_step(s, carry):
            staged[s, :, cols] = held_ref[s, :, cols] * pot
            return carry

        lax.fori_loop(0, s_dev, state_step, 0, unroll=8)
        store(i).start()
    for i in range(STORES):
        store(i).wait()
    pot_copy.wait()


def body(slabs, states, core_density, occupancy):
    s_dev, planes, cells = states.shape
    half = planes // 2
    vmem = pl.BlockSpec(memory_space=pltpu.VMEM)
    hbm = pl.BlockSpec(memory_space=pltpu.HBM)
    states = pltpu.with_memory_space_constraint(states, pltpu.HBM)
    core_density = pltpu.with_memory_space_constraint(core_density, pltpu.HBM)
    occupancy = pltpu.with_memory_space_constraint(occupancy, pltpu.HBM)

    def rows(count):
        return pltpu.VMEM((count, cells), jnp.float32)

    def sems(count):
        return pltpu.SemaphoreType.DMA((count,))

    held, pot = pl.pallas_call(
        functools.partial(potential_kernel, slabs),
        out_shape=(
            pltpu.VMEM((s_dev, planes, cells), jnp.bfloat16),
            pltpu.VMEM((planes, cells), jnp.float32),
        ),
        in_specs=[hbm, hbm, hbm],
        out_specs=(vmem, vmem),
        scratch_shapes=[
            pltpu.SMEM((s_dev,), jnp.int32),
            pltpu.VMEM((2, half, cells), jnp.float32),
            rows(half),
            rows(half),
            rows(half),
            rows(half),
            rows(half),
            rows(8),
            pltpu.VMEM((8, cells // 2), jnp.float32),
            pltpu.VMEM((2, 8, cells // 2), jnp.float32),
            rows(8),
            rows(half),
            rows(half),
            sems(2 * CHUNKS),
            sems(2),
            pltpu.SemaphoreType.REGULAR,
            pltpu.SemaphoreType.REGULAR,
        ]
        + [sems(CHUNKS)] * 6
        + [sems(2)] * 2
        + [sems(CHUNKS)] * 2,
        compiler_params=pltpu.CompilerParams(
            collective_id=0, has_side_effects=True, vmem_limit_bytes=24 * 1024 * 1024
        ),
        name="potential",
    )(occupancy, states, core_density)
    return pl.pallas_call(
        apply_kernel,
        out_shape=(
            jax.ShapeDtypeStruct((s_dev, planes, cells), jnp.bfloat16),
            jax.ShapeDtypeStruct((planes, cells), jnp.float32),
        ),
        in_specs=[vmem, vmem],
        out_specs=(hbm, hbm),
        scratch_shapes=[
            pltpu.VMEM((s_dev, planes, cells), jnp.bfloat16),
            sems(STORES),
            pltpu.SemaphoreType.DMA,
        ],
        compiler_params=pltpu.CompilerParams(vmem_limit_bytes=32 * 1024 * 1024),
        name="apply",
    )(held, pot)


def solution(mesh):
    placed = (P("grp", "slab", None), P("slab", None), P("grp"))
    return jax.shard_map(
        functools.partial(body, mesh.shape["slab"]),
        mesh=mesh,
        in_specs=placed,
        out_specs=(P("grp", "slab", None), P("slab", None)),
        check_vma=False,
    )
```

```python
import functools
import math

import jax
import jax.numpy as jnp
from jax import lax
from jax.experimental import pallas as pl
from jax.experimental.pallas import tpu as pltpu
from jax.sharding import PartitionSpec as P

MESH = pl.DeviceIdType.MESH

NX = 64
NY = 64
OCC_DEN = 8
LANES = 128

grid_step = 0.5
valence_norm = 0.04

kappa = 0.804
mu = 0.2195149727645171
exchange = -0.75 * (3.0 / math.pi) ** (1.0 / 3.0)
reduced_scale = 4.0 * (3.0 * math.pi**2) ** (2.0 / 3.0)
stencil_scale = 1.0 / (12.0 * grid_step)
u_scale = mu / kappa / reduced_scale * stencil_scale * stencil_scale
flow_scale = 2.0 * exchange * mu / reduced_scale * stencil_scale * stencil_scale
slope_scale = exchange * 4.0 / 3.0

CHUNKS = 4
STEP = 4 * LANES
STORES = 8


def stencil(before2, before1, after1, after2):
    return (before2 - after2) + 8.0 * (after1 - before1)


def swap_halves(tile):
    return pltpu.roll(tile, 64, 1)


def along_y(tile, swapped, inner):
    before2 = pltpu.roll(jnp.where(inner >= NY - 2, swapped, tile), 2, 1)
    before1 = pltpu.roll(jnp.where(inner >= NY - 1, swapped, tile), 1, 1)
    after1 = pltpu.roll(jnp.where(inner < 1, swapped, tile), LANES - 1, 1)
    after2 = pltpu.roll(jnp.where(inner < 2, swapped, tile), LANES - 2, 1)
    return stencil(before2, before1, after1, after2)


def along_x(left, left_swapped, swapped, right, right_swapped, low):
    before1 = jnp.where(low, left_swapped, swapped)
    after1 = jnp.where(low, swapped, right_swapped)
    return stencil(left, before1, after1, right)


def along_z(tile):
    rows = tile.shape[0]
    return stencil(
        pltpu.roll(tile, 2, 0),
        pltpu.roll(tile, 1, 0),
        pltpu.roll(tile, rows - 1, 0),
        pltpu.roll(tile, rows - 2, 0),
    )


def potential_kernel(
    slabs,
    occ_hbm,
    states_ref,
    core_ref,
    held_ref,
    pot_ref,
    occ_ref,
    part,
    from_core,
    chip_sum,
    from_chip,
    core_half,
    dens,
    inner_in,
    edge_out,
    edge_in,
    outer,
    flow_x,
    local,
    load_sem,
    misc_sem,
    group_sem,
    slab_sem,
    core_send,
    core_recv,
    chip_send,
    chip_recv,
    inner_send,
    inner_recv,
    edge_send,
    edge_recv,
    pot_send,
    pot_recv,
):
    s_dev, planes, cells = states_ref.shape
    half = planes // 2
    width = cells // CHUNKS
    n_tiles = cells // LANES

    grp = lax.axis_index("grp")
    slab = lax.axis_index("slab")
    chip = grp // 2
    upper = 1 - grp % 2
    core_peer = {"grp": chip * 2 + upper, "slab": slab}
    chip_peer = {"grp": (1 - chip) * 2 + 1 - upper, "slab": slab}
    cross_peer = {"grp": (1 - chip) * 2 + upper, "slab": slab}
    beyond = (slab + slabs - 1 + 2 * upper) % slabs
    wrapped = slab % 8 == 0
    edge_chips = (chip, 1 - chip)

    def cols(i):
        return pl.ds(pl.multiple_of(i * width, LANES), width)

    def load(h, i):
        where = (slice(None), pl.ds(h * half, half), cols(i))
        return pltpu.make_async_copy(states_ref.at[where], held_ref.at[where], load_sem.at[h * CHUNKS + i])

    def remote(src, dst, send, recv, peer):
        return pltpu.make_async_remote_copy(
            src_ref=src, dst_ref=dst, send_sem=send, recv_sem=recv, device_id=peer, device_id_type=MESH
        )

    def to_core(i):
        return remote(
            part.at[1 - upper, :, cols(i)], from_core.at[:, cols(i)], core_send.at[i], core_recv.at[i], core_peer
        )

    def to_chip(i):
        return remote(
            chip_sum.at[:, cols(i)], from_chip.at[:, cols(i)], chip_send.at[i], chip_recv.at[i], chip_peer
        )

    def to_edge(k):
        peer = {"grp": edge_chips[k] * 2 + upper, "slab": beyond}
        return remote(edge_out, edge_in.at[chip], edge_send.at[k], edge_recv.at[chip], peer)

    def from_edge(k):
        return remote(edge_out, edge_in.at[k], edge_send.at[k], edge_recv.at[k], core_peer)

    def to_inner(i):
        rows = pl.ds(pl.multiple_of((1 - upper) * 8, 8), 8)
        return remote(
            dens.at[rows, cols(i)], inner_in.at[:, cols(i)], inner_send.at[i], inner_recv.at[i], core_peer
        )

    def own_rows():
        return pl.ds(pl.multiple_of(upper * half, half), half)

    def to_pot(i):
        where = pot_ref.at[own_rows(), cols(i)]
        return remote(where, where, pot_send.at[i], pot_recv.at[i], core_peer)

    occ_copy = pltpu.make_async_copy(occ_hbm, occ_ref, misc_sem.at[0])
    occ_copy.start()
    for h in (1, 0):
        for i in range(CHUNKS):
            load(h, i).start()
    core_copy = pltpu.make_async_copy(core_ref.at[own_rows(), :], core_half, misc_sem.at[1])
    core_copy.start()

    barrier = pltpu.get_barrier_semaphore()

    def greet(peer):
        pl.semaphore_signal(barrier, inc=1, device_id=peer, device_id_type=MESH)

    @pl.when(upper == 0)
    def _():
        greet(chip_peer)
        greet({"grp": 0, "slab": beyond})
        greet({"grp": 2, "slab": beyond})

    @pl.when(upper == 1)
    def _():
        greet(core_peer)
        greet(cross_peer)
        greet({"grp": 0, "slab": beyond})
        greet({"grp": 2, "slab": beyond})

    occ_copy.wait()
    weights = [
        occ_ref[s].astype(jnp.float32) * (valence_norm / (OCC_DEN * s_dev * 4))
        for s in range(s_dev)
    ]

    def density_part(h, i):
        load(h, i).wait()

        def tile_step(t, carry):
            lanes = pl.ds(pl.multiple_of(i * width + t * STEP, STEP), STEP)
            total = jnp.zeros((half, STEP), jnp.float32)
            for s in range(s_dev):
                wide = held_ref[s, h * half : (h + 1) * half, lanes].astype(jnp.float32)
                total = total + (wide * weights[s]) * wide
            part[h, :, lanes] = total
            return carry

        lax.fori_loop(0, width // STEP, tile_step, 0)

    first_rows = lax.broadcasted_iota(jnp.int32, (8, LANES), 0) < 4
    with_core = (1 - chip).astype(jnp.float32)
    is_low = upper == 0

    def sum_chip():
        core_copy.wait()
        for i in range(CHUNKS):
            to_core(i).wait_recv()
            chip_sum[:, cols(i)] = (part[upper, :, cols(i)] + from_core[:, cols(i)]) + with_core * core_half[:, cols(i)]

        edge_rows = pl.ds(pl.multiple_of(upper * 8, 8), 8)

        def pack(t, carry):
            lanes = pl.ds(pl.multiple_of(t * LANES, LANES), LANES)
            front = chip_sum[edge_rows, lanes]
            back = chip_sum[edge_rows, pl.ds(pl.multiple_of(cells // 2 + t * LANES, LANES), LANES)]
            front_turned, back_turned = pltpu.roll(front, 4, 0), pltpu.roll(back, 4, 0)
            low_edge = jnp.where(first_rows, front, back_turned)
            high_edge = jnp.where(first_rows, front_turned, back)
            edge_out[:, lanes] = jnp.where(is_low, low_edge, high_edge)
            return carry

        lax.fori_loop(0, n_tiles // 2, pack, 0, unroll=4)

    def send_chip():
        for i in range(CHUNKS):
            to_chip(i).start()

    def send_edges():
        for k in range(2):
            to_edge(k).start()

    def meet_slabs():
        pl.semaphore_wait(barrier, 4)
        pl.semaphore_signal(slab_sem, inc=1, device_id=core_peer, device_id_type=MESH)

    for i in range(CHUNKS):
        density_part(1, i)

    @pl.when(upper == 0)
    def _():
        pl.semaphore_wait(barrier, 3)
        pl.semaphore_signal(group_sem, inc=1, device_id=core_peer, device_id_type=MESH)
        for i in range(CHUNKS):
            to_core(i).start()

    for i in range(CHUNKS - 1):
        density_part(0, i)

    @pl.when(upper == 1)
    def _():
        pl.semaphore_wait(group_sem, 1)
        for i in range(CHUNKS - 1):
            to_core(i).start()
        sum_chip()

        @pl.when(jnp.logical_not(wrapped))
        def _():
            meet_slabs()
            send_edges()

        send_chip()

    density_part(0, CHUNKS - 1)

    @pl.when(upper == 1)
    def _():
        to_core(CHUNKS - 1).start()

    @pl.when(upper == 0)
    def _():
        sum_chip()

        @pl.when(jnp.logical_not(wrapped))
        def _():
            pl.semaphore_wait(slab_sem, 1)
            send_edges()

        send_chip()

    @pl.when(wrapped & (upper == 1))
    def _():
        meet_slabs()
        send_edges()

    @pl.when(wrapped & (upper == 0))
    def _():
        pl.semaphore_wait(slab_sem, 1)
        send_edges()

    for i in range(CHUNKS):
        to_chip(i).wait_recv()
        dens[:, cols(i)] = chip_sum[:, cols(i)] + from_chip[:, cols(i)]
        to_inner(i).start()

    for k in range(2):
        from_edge(k).wait_recv()
    for t in range(n_tiles // 2):
        lanes = slice(t * LANES, (t + 1) * LANES)
        both = edge_in[0, :, lanes] + edge_in[1, :, lanes]
        turned = pltpu.roll(both, 4, 0)
        outer[:, t * LANES : (t + 1) * LANES] = jnp.where(first_rows, both, turned)
        outer[:, cells // 2 + t * LANES : cells // 2 + (t + 1) * LANES] = jnp.where(first_rows, turned, both)
    for i in range(CHUNKS):
        to_inner(i).wait_recv()

    lane = lax.broadcasted_iota(jnp.int32, (1, LANES), 1)
    inner = lane % NY
    low = lane < NY
    inner_rows = jnp.where(is_low, first_rows.astype(jnp.int32), 1 - first_rows.astype(jnp.int32)) == 1

    def field(t):
        lanes = pl.ds(pl.multiple_of((t % n_tiles) * LANES, LANES), LANES)
        edge = jnp.where(inner_rows, inner_in[:, lanes], outer[:, lanes])
        return jnp.concatenate([dens[:, lanes], edge], axis=0)

    def flow_step(t, carry):
        centre = field(t)
        left = field(t + n_tiles - 1)
        right = field(t + 1)
        swapped = swap_halves(centre)
        grad_x = along_x(left, swap_halves(left), swapped, right, swap_halves(right), low)
        grad_y = along_y(centre, swapped, inner)
        grad_z = along_z(centre)
        sigma = grad_x * grad_x + grad_y * grad_y + grad_z * grad_z
        root = jnp.exp2(jnp.log2(centre) * (-1.0 / 3.0))
        root2 = root * root
        root4 = root2 * root2
        share = 1.0 / (1.0 + u_scale * (sigma * (root4 * root4)))
        flow = flow_scale * (root4 * (share * share))
        d_dens = (slope_scale * (centre * root2)) * (
            (1.0 + kappa) + share * (2.0 * kappa * share - 3.0 * kappa)
        )
        flow_y = flow * grad_y
        div_y = along_y(flow_y[:half], swap_halves(flow_y[:half]), inner)
        div_z = along_z(flow * grad_z)[:half]
        lanes = pl.ds(pl.multiple_of((t % n_tiles) * LANES, LANES), LANES)
        flow_x[:, lanes] = (flow * grad_x)[:half]
        local[:, lanes] = d_dens[:half] - (div_y + div_z)
        return carry

    def pot_step(t, carry):
        def at(k):
            return flow_x[:, pl.ds(pl.multiple_of((k % n_tiles) * LANES, LANES), LANES)]

        lanes = pl.ds(pl.multiple_of((t % n_tiles) * LANES, LANES), LANES)
        left, centre, right = at(t + n_tiles - 1), at(t), at(t + 1)
        div_x = along_x(
            left, swap_halves(left), swap_halves(centre), right, swap_halves(right), low
        )
        pot_ref[own_rows(), lanes] = local[:, lanes] - div_x
        return carry

    lax.fori_loop(0, n_tiles, flow_step, 0, unroll=8)
    tiles = width // LANES
    for i in range(CHUNKS):
        lax.fori_loop(i * tiles, (i + 1) * tiles, pot_step, 0, unroll=True)
        to_pot(i).start()
    for i in range(CHUNKS):
        to_core(i).wait_send()
        to_chip(i).wait_send()
        to_inner(i).wait_send()
        to_pot(i).wait()
    for k in range(2):
        to_edge(k).wait_send()


def apply_kernel(held_ref, pot_ref, applied_ref, out_ref, staged, store_sem, pot_sem):
    s_dev, planes, cells = held_ref.shape
    width = cells // STORES
    pot_copy = pltpu.make_async_copy(pot_ref, out_ref, pot_sem)
    pot_copy.start()

    def store(i):
        cols = pl.ds(i * width, width)
        return pltpu.make_async_copy(staged.at[:, :, cols], applied_ref.at[:, :, cols], store_sem.at[i])

    for i in range(STORES):
        cols = pl.ds(i * width, width)
        pot = pot_ref[:, cols].astype(jnp.bfloat16)

        def state_step(s, carry):
            staged[s, :, cols] = held_ref[s, :, cols] * pot
            return carry

        lax.fori_loop(0, s_dev, state_step, 0, unroll=8)
        store(i).start()
    for i in range(STORES):
        store(i).wait()
    pot_copy.wait()


def body(slabs, states, core_density, occupancy):
    s_dev, planes, cells = states.shape
    half = planes // 2
    vmem = pl.BlockSpec(memory_space=pltpu.VMEM)
    hbm = pl.BlockSpec(memory_space=pltpu.HBM)
    states = pltpu.with_memory_space_constraint(states, pltpu.HBM)
    core_density = pltpu.with_memory_space_constraint(core_density, pltpu.HBM)
    occupancy = pltpu.with_memory_space_constraint(occupancy, pltpu.HBM)

    def rows(count):
        return pltpu.VMEM((count, cells), jnp.float32)

    def sems(count):
        return pltpu.SemaphoreType.DMA((count,))

    held, pot = pl.pallas_call(
        functools.partial(potential_kernel, slabs),
        out_shape=(
            pltpu.VMEM((s_dev, planes, cells), jnp.bfloat16),
            pltpu.VMEM((planes, cells), jnp.float32),
        ),
        in_specs=[hbm, hbm, hbm],
        out_specs=(vmem, vmem),
        scratch_shapes=[
            pltpu.SMEM((s_dev,), jnp.int32),
            pltpu.VMEM((2, half, cells), jnp.float32),
            rows(half),
            rows(half),
            rows(half),
            rows(half),
            rows(half),
            rows(8),
            pltpu.VMEM((8, cells // 2), jnp.float32),
            pltpu.VMEM((2, 8, cells // 2), jnp.float32),
            rows(8),
            rows(half),
            rows(half),
            sems(2 * CHUNKS),
            sems(2),
            pltpu.SemaphoreType.REGULAR,
            pltpu.SemaphoreType.REGULAR,
        ]
        + [sems(CHUNKS)] * 6
        + [sems(2)] * 2
        + [sems(CHUNKS)] * 2,
        compiler_params=pltpu.CompilerParams(
            collective_id=0, has_side_effects=True, vmem_limit_bytes=24 * 1024 * 1024
        ),
        name="potential",
    )(occupancy, states, core_density)
    return pl.pallas_call(
        apply_kernel,
        out_shape=(
            jax.ShapeDtypeStruct((s_dev, planes, cells), jnp.bfloat16),
            jax.ShapeDtypeStruct((planes, cells), jnp.float32),
        ),
        in_specs=[vmem, vmem],
        out_specs=(hbm, hbm),
        scratch_shapes=[
            pltpu.VMEM((s_dev, planes, cells), jnp.bfloat16),
            sems(STORES),
            pltpu.SemaphoreType.DMA,
        ],
        compiler_params=pltpu.CompilerParams(vmem_limit_bytes=32 * 1024 * 1024),
        name="apply",
    )(held, pot)


def solution(mesh):
    placed = (P("grp", "slab", None), P("slab", None), P("grp"))
    return jax.shard_map(
        functools.partial(body, mesh.shape["slab"]),
        mesh=mesh,
        in_specs=placed,
        out_specs=(P("grp", "slab", None), P("slab", None)),
        check_vma=False,
    )
```

```python
import functools
import math

import jax
import jax.numpy as jnp
from jax import lax
from jax.experimental import pallas as pl
from jax.experimental.pallas import tpu as pltpu
from jax.sharding import PartitionSpec as P

MESH = pl.DeviceIdType.MESH

NX = 64
NY = 64
OCC_DEN = 8
LANES = 128

grid_step = 0.5
valence_norm = 0.04

kappa = 0.804
mu = 0.2195149727645171
exchange = -0.75 * (3.0 / math.pi) ** (1.0 / 3.0)
reduced_scale = 4.0 * (3.0 * math.pi**2) ** (2.0 / 3.0)
stencil_scale = 1.0 / (12.0 * grid_step)
u_scale = mu / kappa / reduced_scale * stencil_scale * stencil_scale
flow_scale = 2.0 * exchange * mu / reduced_scale * stencil_scale * stencil_scale
slope_scale = exchange * 4.0 / 3.0

CHUNKS = 4
STEP = 4 * LANES
SPAN = 32
FAR_SPAN = 32
NEAR_SPAN = 16
STORES = 8


def stencil(before2, before1, after1, after2):
    return (before2 - after2) + 8.0 * (after1 - before1)


def swap_halves(tile):
    return pltpu.roll(tile, 64, 1)


def along_y(tile, swapped, inner):
    before2 = pltpu.roll(jnp.where(inner >= NY - 2, swapped, tile), 2, 1)
    before1 = pltpu.roll(jnp.where(inner >= NY - 1, swapped, tile), 1, 1)
    after1 = pltpu.roll(jnp.where(inner < 1, swapped, tile), LANES - 1, 1)
    after2 = pltpu.roll(jnp.where(inner < 2, swapped, tile), LANES - 2, 1)
    return stencil(before2, before1, after1, after2)


def along_x(left, left_swapped, swapped, right, right_swapped, low):
    before1 = jnp.where(low, left_swapped, swapped)
    after1 = jnp.where(low, swapped, right_swapped)
    return stencil(left, before1, after1, right)


def along_z(tile):
    rows = tile.shape[0]
    return stencil(
        pltpu.roll(tile, 2, 0),
        pltpu.roll(tile, 1, 0),
        pltpu.roll(tile, rows - 1, 0),
        pltpu.roll(tile, rows - 2, 0),
    )


def potential_kernel(
    slabs,
    occ_hbm,
    states_ref,
    core_ref,
    held_ref,
    pot_ref,
    occ_ref,
    part,
    from_core,
    chip_sum,
    from_chip,
    core_half,
    dens,
    inner_in,
    edge_out,
    edge_in,
    outer,
    flow_x,
    local,
    near_rest,
    near_z,
    load_sem,
    misc_sem,
    group_sem,
    slab_sem,
    core_send,
    core_recv,
    chip_send,
    chip_recv,
    inner_send,
    inner_recv,
    edge_send,
    edge_recv,
    pot_send,
    pot_recv,
):
    s_dev, planes, cells = states_ref.shape
    half = planes // 2
    width = cells // CHUNKS
    n_tiles = cells // LANES

    grp = lax.axis_index("grp")
    slab = lax.axis_index("slab")
    chip = grp // 2
    upper = 1 - grp % 2
    core_peer = {"grp": chip * 2 + upper, "slab": slab}
    chip_peer = {"grp": (1 - chip) * 2 + 1 - upper, "slab": slab}
    cross_peer = {"grp": (1 - chip) * 2 + upper, "slab": slab}
    beyond = (slab + slabs - 1 + 2 * upper) % slabs
    wrapped = slab % 8 == 0
    edge_chips = (chip, 1 - chip)

    def cols(i):
        return pl.ds(pl.multiple_of(i * width, LANES), width)

    def load(h, i):
        where = (slice(None), pl.ds(h * half, half), cols(i))
        return pltpu.make_async_copy(states_ref.at[where], held_ref.at[where], load_sem.at[h * CHUNKS + i])

    def remote(src, dst, send, recv, peer):
        return pltpu.make_async_remote_copy(
            src_ref=src, dst_ref=dst, send_sem=send, recv_sem=recv, device_id=peer, device_id_type=MESH
        )

    def to_core(i):
        return remote(
            part.at[1 - upper, :, cols(i)], from_core.at[:, cols(i)], core_send.at[i], core_recv.at[i], core_peer
        )

    def to_chip(i):
        return remote(
            chip_sum.at[:, cols(i)], from_chip.at[:, cols(i)], chip_send.at[i], chip_recv.at[i], chip_peer
        )

    def to_edge(k):
        peer = {"grp": edge_chips[k] * 2 + upper, "slab": beyond}
        return remote(edge_out, edge_in.at[chip], edge_send.at[k], edge_recv.at[chip], peer)

    def from_edge(k):
        return remote(edge_out, edge_in.at[k], edge_send.at[k], edge_recv.at[k], core_peer)

    def shifted(i):
        return pl.ds(pl.multiple_of(i * width + LANES, LANES), width)

    def to_inner(i):
        rows = pl.ds(pl.multiple_of((1 - upper) * 8, 8), 8)
        return remote(
            dens.at[rows, shifted(i)], inner_in.at[:, shifted(i)], inner_send.at[i], inner_recv.at[i], core_peer
        )

    def own_rows():
        return pl.ds(pl.multiple_of(upper * half, half), half)

    near_out = pl.ds(pl.multiple_of(upper * 24, 8), 8)
    far_out = pl.ds(pl.multiple_of(8 + upper * 8, 8), 8)

    def to_pot(i):
        span = NEAR_SPAN * LANES
        where = pot_ref.at[near_out, pl.ds(pl.multiple_of(i * span, LANES), span)]
        return remote(where, where, pot_send.at[i], pot_recv.at[i], core_peer)

    def to_pot_far():
        where = pot_ref.at[far_out, :]
        return remote(where, where, pot_send.at[CHUNKS], pot_recv.at[CHUNKS], core_peer)

    occ_copy = pltpu.make_async_copy(occ_hbm, occ_ref, misc_sem.at[0])
    occ_copy.start()
    for h in (1, 0):
        for i in range(CHUNKS):
            load(h, i).start()
    core_copy = pltpu.make_async_copy(core_ref.at[own_rows(), :], core_half, misc_sem.at[1])
    core_copy.start()

    barrier = pltpu.get_barrier_semaphore()

    def greet(peer):
        pl.semaphore_signal(barrier, inc=1, device_id=peer, device_id_type=MESH)

    @pl.when(upper == 0)
    def _():
        greet(chip_peer)
        greet({"grp": 0, "slab": beyond})
        greet({"grp": 2, "slab": beyond})

    @pl.when(upper == 1)
    def _():
        greet(core_peer)
        greet(cross_peer)
        greet({"grp": 0, "slab": beyond})
        greet({"grp": 2, "slab": beyond})

    occ_copy.wait()
    weights = [
        occ_ref[s].astype(jnp.float32) * (valence_norm / (OCC_DEN * s_dev * 4))
        for s in range(s_dev)
    ]

    def density_part(h, i):
        load(h, i).wait()

        def tile_step(t, carry):
            lanes = pl.ds(pl.multiple_of(i * width + t * STEP, STEP), STEP)
            total = jnp.zeros((half, STEP), jnp.float32)
            for s in range(s_dev):
                wide = held_ref[s, h * half : (h + 1) * half, lanes].astype(jnp.float32)
                total = total + (wide * weights[s]) * wide
            part[h, :, lanes] = total
            return carry

        lax.fori_loop(0, width // STEP, tile_step, 0)

    first_rows = lax.broadcasted_iota(jnp.int32, (8, LANES), 0) < 4
    with_core = (1 - chip).astype(jnp.float32)
    is_low = upper == 0

    def sum_chip():
        core_copy.wait()
        for i in range(CHUNKS):
            to_core(i).wait_recv()
            chip_sum[:, cols(i)] = (part[upper, :, cols(i)] + from_core[:, cols(i)]) + with_core * core_half[:, cols(i)]

        edge_rows = pl.ds(pl.multiple_of(upper * 8, 8), 8)

        def pack(t, carry):
            lanes = pl.ds(pl.multiple_of(t * LANES, LANES), LANES)
            front = chip_sum[edge_rows, lanes]
            back = chip_sum[edge_rows, pl.ds(pl.multiple_of(cells // 2 + t * LANES, LANES), LANES)]
            front_turned, back_turned = pltpu.roll(front, 4, 0), pltpu.roll(back, 4, 0)
            low_edge = jnp.where(first_rows, front, back_turned)
            high_edge = jnp.where(first_rows, front_turned, back)
            edge_out[:, lanes] = jnp.where(is_low, low_edge, high_edge)
            return carry

        lax.fori_loop(0, n_tiles // 2, pack, 0, unroll=4)

    def send_chip():
        for i in range(CHUNKS):
            to_chip(i).start()

    def send_edges():
        for k in range(2):
            to_edge(k).start()

    def meet_slabs():
        pl.semaphore_wait(barrier, 4)
        pl.semaphore_signal(slab_sem, inc=1, device_id=core_peer, device_id_type=MESH)

    for i in range(CHUNKS):
        density_part(1, i)

    @pl.when(upper == 0)
    def _():
        pl.semaphore_wait(barrier, 3)
        pl.semaphore_signal(group_sem, inc=1, device_id=core_peer, device_id_type=MESH)
        for i in range(CHUNKS):
            to_core(i).start()

    for i in range(CHUNKS - 1):
        density_part(0, i)

    @pl.when(upper == 1)
    def _():
        pl.semaphore_wait(group_sem, 1)
        for i in range(CHUNKS - 1):
            to_core(i).start()
        sum_chip()

        @pl.when(jnp.logical_not(wrapped))
        def _():
            meet_slabs()
            send_edges()

        send_chip()

    density_part(0, CHUNKS - 1)

    @pl.when(upper == 1)
    def _():
        to_core(CHUNKS - 1).start()

    @pl.when(upper == 0)
    def _():
        sum_chip()

        @pl.when(jnp.logical_not(wrapped))
        def _():
            pl.semaphore_wait(slab_sem, 1)
            send_edges()

        send_chip()

    @pl.when(wrapped & (upper == 1))
    def _():
        meet_slabs()
        send_edges()

    @pl.when(wrapped & (upper == 0))
    def _():
        pl.semaphore_wait(slab_sem, 1)
        send_edges()

    lane = lax.broadcasted_iota(jnp.int32, (1, LANES), 1)
    inner = lane % NY
    low = lane < NY
    row = lax.broadcasted_iota(jnp.int32, (8, LANES), 0)
    own_four = jnp.where(is_low, row, 7 - row) < 4
    own_two = jnp.where(is_low, row, 7 - row) < 2
    near = pl.ds(pl.multiple_of(upper * 8, 8), 8)
    far = pl.ds(pl.multiple_of((1 - upper) * 8, 8), 8)

    tiles = width // LANES
    reach = (tiles + 2) * LANES
    last = n_tiles * LANES
    first_copy, last_copy = slice(last + LANES, last + 2 * LANES), slice(0, LANES)
    first_tile, last_tile = slice(LANES, 2 * LANES), slice(last, last + LANES)

    def at(j):
        return slice(j * LANES, (j + 1) * LANES)

    def total(i):
        to_chip(i).wait_recv()
        dens[:, shifted(i)] = chip_sum[:, cols(i)] + from_chip[:, cols(i)]
        to_inner(i).start()

    def flows(fields, turned, j):
        centre = fields[j]
        grad_x = along_x(fields[j - 1], turned[j - 1], turned[j], fields[j + 1], turned[j + 1], low)
        grad_y = along_y(centre, turned[j], inner)
        grad_z = along_z(centre)
        sigma = grad_x * grad_x + grad_y * grad_y + grad_z * grad_z
        root = jnp.exp2(jnp.log2(centre) * (-1.0 / 3.0))
        root2 = root * root
        root4 = root2 * root2
        share = 1.0 / (1.0 + u_scale * (sigma * (root4 * root4)))
        flow = flow_scale * (root4 * (share * share))
        d_dens = (slope_scale * (centre * root2)) * (
            (1.0 + kappa) + share * (2.0 * kappa * share - 3.0 * kappa)
        )
        return flow * grad_x, flow * grad_y, flow * grad_z, d_dens

    def first_pass(where, count):
        window = [ref.at[:, where] for ref in (dens, inner_in, flow_x, local, near_rest, near_z)]
        dens_w, inner_w, flow_w, local_w, rest_w, z_w = window
        fields = [jnp.concatenate([dens_w[:, at(j)], inner_w[:, at(j)]], axis=0) for j in range(count + 2)]
        turned = [swap_halves(f) for f in fields]
        for j in range(1, count + 1):
            part_x, part_y, part_z, d_dens = flows(fields, turned, j)
            part_y = part_y[:half]
            rest = d_dens[:half] - along_y(part_y, swap_halves(part_y), inner)
            flow_w[:, at(j)] = part_x[:half]
            local_w[:, at(j)] = rest - along_z(part_z)[:half]
            rest_w[:, at(j)] = jnp.where(is_low, rest[:8], rest[8:])
            z_w[:, at(j)] = jnp.where(is_low, part_z[:8], part_z[8:half])

    def second_pass(g, carry):
        where = pl.ds(pl.multiple_of(g * SPAN * LANES, LANES), (SPAN + 2) * LANES)
        dens_w, flow_w, local_w = (ref.at[near, where] for ref in (dens, flow_x, local))
        outer_w, rest_w, z_w = (ref.at[:, where] for ref in (outer, near_rest, near_z))
        fields = [
            jnp.where(own_four, outer_w[:, at(j)], pltpu.roll(dens_w[:, at(j)], 4, 0)) for j in range(SPAN + 2)
        ]
        turned = [swap_halves(f) for f in fields]
        for j in range(1, SPAN + 1):
            part_x, part_y, part_z, d_dens = flows(fields, turned, j)
            rest = d_dens - along_y(part_y, swap_halves(part_y), inner)
            rest = jnp.where(own_two, pltpu.roll(rest, 4, 0), rest_w[:, at(j)])
            old_z = z_w[:, at(j)]
            row_z = jnp.where(
                first_rows,
                pltpu.roll(jnp.where(is_low, part_z, old_z), 6, 0),
                pltpu.roll(jnp.where(is_low, old_z, part_z), 2, 0),
            )
            div_z = along_z(row_z)
            div_z = jnp.where(is_low, pltpu.roll(div_z, 6, 0), pltpu.roll(div_z, 2, 0))
            local_w[:, at(j)] = jnp.where(own_four, rest - div_z, local_w[:, at(j)])
            flow_w[:, at(j)] = jnp.where(own_two, pltpu.roll(part_x, 4, 0), flow_w[:, at(j)])
        return carry

    def finish(rows, out_rows, g, span):
        where = pl.ds(pl.multiple_of(g * span * LANES, LANES), (span + 2) * LANES)
        flow_w, local_w = flow_x.at[rows, where], local.at[rows, where]
        out_w = pot_ref.at[out_rows, pl.ds(pl.multiple_of(g * span * LANES, LANES), span * LANES)]
        fields = [flow_w[:, at(j)] for j in range(span + 2)]
        turned = [swap_halves(f) for f in fields]
        for j in range(1, span + 1):
            div_x = along_x(fields[j - 1], turned[j - 1], turned[j], fields[j + 1], turned[j + 1], low)
            out_w[:, at(j - 1)] = local_w[:, at(j)] - div_x

    def finish_far(g, carry):
        finish(far, far_out, g, FAR_SPAN)
        return carry

    def finish_near(g, carry):
        finish(near, near_out, g, NEAR_SPAN)
        to_pot(g).start()
        return carry

    def wrap(ref, rows):
        ref[rows, first_copy] = ref[rows, first_tile]
        ref[rows, last_copy] = ref[rows, last_tile]

    everything = slice(None)
    total(0)
    dens[:, first_copy] = dens[:, first_tile]
    total(1)
    to_inner(0).wait_recv()
    inner_in[:, first_copy] = inner_in[:, first_tile]
    first_pass(pl.ds(LANES, tiles * LANES), tiles - 2)

    def follow(i, carry):
        @pl.when(i < CHUNKS)
        def _():
            total(i)

        to_inner(i - 1).wait_recv()
        first_pass(pl.ds(pl.multiple_of((i - 1) * width - LANES, LANES), reach), tiles)
        return carry

    lax.fori_loop(2, CHUNKS + 1, follow, 0)
    dens[:, last_copy] = dens[:, last_tile]
    inner_in[:, last_copy] = inner_in[:, last_tile]
    first_pass(pl.ds(last - LANES, 3 * LANES), 1)
    first_pass(pl.ds(0, 3 * LANES), 1)
    wrap(flow_x, everything)
    lax.fori_loop(0, n_tiles // FAR_SPAN, finish_far, 0)
    to_pot_far().start()
    for k in range(2):
        from_edge(k).wait_recv()

    for t in range(n_tiles // 2):
        both = edge_in[0, :, at(t)] + edge_in[1, :, at(t)]
        turned = pltpu.roll(both, 4, 0)
        outer[:, at(t + 1)] = jnp.where(first_rows, both, turned)
        outer[:, at(t + 1 + n_tiles // 2)] = jnp.where(first_rows, turned, both)
    wrap(outer, everything)
    lax.fori_loop(0, n_tiles // SPAN, second_pass, 0)
    wrap(flow_x, near)
    lax.fori_loop(0, n_tiles // NEAR_SPAN, finish_near, 0)
    for i in range(CHUNKS):
        to_core(i).wait_send()
        to_chip(i).wait_send()
        to_inner(i).wait_send()
    for i in range(n_tiles // NEAR_SPAN):
        to_pot(i).wait()
    to_pot_far().wait()
    for k in range(2):
        to_edge(k).wait_send()


def apply_kernel(held_ref, pot_ref, applied_ref, out_ref, staged, store_sem, pot_sem):
    s_dev, planes, cells = held_ref.shape
    width = cells // STORES
    pot_copy = pltpu.make_async_copy(pot_ref, out_ref, pot_sem)
    pot_copy.start()

    def store(i):
        cols = pl.ds(i * width, width)
        return pltpu.make_async_copy(staged.at[:, :, cols], applied_ref.at[:, :, cols], store_sem.at[i])

    for i in range(STORES):
        cols = pl.ds(i * width, width)
        pot = pot_ref[:, cols].astype(jnp.bfloat16)

        def state_step(s, carry):
            staged[s, :, cols] = held_ref[s, :, cols] * pot
            return carry

        lax.fori_loop(0, s_dev, state_step, 0, unroll=8)
        store(i).start()
    for i in range(STORES):
        store(i).wait()
    pot_copy.wait()


def body(slabs, states, core_density, occupancy):
    s_dev, planes, cells = states.shape
    half = planes // 2
    vmem = pl.BlockSpec(memory_space=pltpu.VMEM)
    hbm = pl.BlockSpec(memory_space=pltpu.HBM)
    states = pltpu.with_memory_space_constraint(states, pltpu.HBM)
    core_density = pltpu.with_memory_space_constraint(core_density, pltpu.HBM)
    occupancy = pltpu.with_memory_space_constraint(occupancy, pltpu.HBM)

    def rows(count):
        return pltpu.VMEM((count, cells), jnp.float32)

    def wide(count):
        return pltpu.VMEM((count, cells + 2 * LANES), jnp.float32)

    def sems(count):
        return pltpu.SemaphoreType.DMA((count,))

    held, pot = pl.pallas_call(
        functools.partial(potential_kernel, slabs),
        out_shape=(
            pltpu.VMEM((s_dev, planes, cells), jnp.bfloat16),
            pltpu.VMEM((planes, cells), jnp.float32),
        ),
        in_specs=[hbm, hbm, hbm],
        out_specs=(vmem, vmem),
        scratch_shapes=[
            pltpu.SMEM((s_dev,), jnp.int32),
            pltpu.VMEM((2, half, cells), jnp.float32),
            rows(half),
            rows(half),
            rows(half),
            rows(half),
            wide(half),
            wide(8),
            pltpu.VMEM((8, cells // 2), jnp.float32),
            pltpu.VMEM((2, 8, cells // 2), jnp.float32),
            wide(8),
            wide(half),
            wide(half),
            wide(8),
            wide(8),
            sems(2 * CHUNKS),
            sems(2),
            pltpu.SemaphoreType.REGULAR,
            pltpu.SemaphoreType.REGULAR,
        ]
        + [sems(CHUNKS)] * 6
        + [sems(2)] * 2
        + [sems(CHUNKS + 1)] * 2,
        compiler_params=pltpu.CompilerParams(
            collective_id=0, has_side_effects=True, vmem_limit_bytes=24 * 1024 * 1024
        ),
        name="potential",
    )(occupancy, states, core_density)
    return pl.pallas_call(
        apply_kernel,
        out_shape=(
            jax.ShapeDtypeStruct((s_dev, planes, cells), jnp.bfloat16),
            jax.ShapeDtypeStruct((planes, cells), jnp.float32),
        ),
        in_specs=[vmem, vmem],
        out_specs=(hbm, hbm),
        scratch_shapes=[
            pltpu.VMEM((s_dev, planes, cells), jnp.bfloat16),
            sems(STORES),
            pltpu.SemaphoreType.DMA,
        ],
        compiler_params=pltpu.CompilerParams(vmem_limit_bytes=32 * 1024 * 1024),
        name="apply",
    )(held, pot)


def solution(mesh):
    placed = (P("grp", "slab", None), P("slab", None), P("grp"))
    return jax.shard_map(
        functools.partial(body, mesh.shape["slab"]),
        mesh=mesh,
        in_specs=placed,
        out_specs=(P("grp", "slab", None), P("slab", None)),
        check_vma=False,
    )
```

```python
import functools
import math

import jax
import jax.numpy as jnp
from jax import lax
from jax.experimental import pallas as pl
from jax.experimental.pallas import tpu as pltpu
from jax.sharding import PartitionSpec as P

MESH = pl.DeviceIdType.MESH

NX = 64
NY = 64
OCC_DEN = 8
LANES = 128

grid_step = 0.5
valence_norm = 0.04

kappa = 0.804
mu = 0.2195149727645171
exchange = -0.75 * (3.0 / math.pi) ** (1.0 / 3.0)
reduced_scale = 4.0 * (3.0 * math.pi**2) ** (2.0 / 3.0)
stencil_scale = 1.0 / (12.0 * grid_step)
u_scale = mu / kappa / reduced_scale * stencil_scale * stencil_scale
flow_scale = 2.0 * exchange * mu / reduced_scale * stencil_scale * stencil_scale
slope_scale = exchange * 4.0 / 3.0

CHUNKS = 4
STEP = 4 * LANES
GATE = 2
SPAN = 32
FAR_SPAN = 32
NEAR_SPAN = 16
STORES = 8


def stencil(before2, before1, after1, after2):
    return (before2 - after2) + 8.0 * (after1 - before1)


def swap_halves(tile):
    return pltpu.roll(tile, 64, 1)


def along_y(tile, swapped, inner):
    before2 = pltpu.roll(jnp.where(inner >= NY - 2, swapped, tile), 2, 1)
    before1 = pltpu.roll(jnp.where(inner >= NY - 1, swapped, tile), 1, 1)
    after1 = pltpu.roll(jnp.where(inner < 1, swapped, tile), LANES - 1, 1)
    after2 = pltpu.roll(jnp.where(inner < 2, swapped, tile), LANES - 2, 1)
    return stencil(before2, before1, after1, after2)


def along_x(left, left_swapped, swapped, right, right_swapped, low):
    before1 = jnp.where(low, left_swapped, swapped)
    after1 = jnp.where(low, swapped, right_swapped)
    return stencil(left, before1, after1, right)


def along_z(tile):
    rows = tile.shape[0]
    return stencil(
        pltpu.roll(tile, 2, 0),
        pltpu.roll(tile, 1, 0),
        pltpu.roll(tile, rows - 1, 0),
        pltpu.roll(tile, rows - 2, 0),
    )


def potential_kernel(
    slabs,
    occ_hbm,
    states_ref,
    core_ref,
    held_ref,
    pot_ref,
    occ_ref,
    part,
    from_core,
    chip_sum,
    from_chip,
    core_half,
    dens,
    inner_in,
    edge_out,
    edge_in,
    outer,
    flow_x,
    local,
    near_rest,
    near_z,
    load_sem,
    misc_sem,
    group_sem,
    slab_sem,
    sent,
    core_recv,
    chip_recv,
    inner_recv,
    edge_recv,
    pot_recv,
):
    s_dev, planes, cells = states_ref.shape
    half = planes // 2
    width = cells // CHUNKS
    n_tiles = cells // LANES

    grp = lax.axis_index("grp")
    slab = lax.axis_index("slab")
    chip = grp // 2
    upper = 1 - grp % 2
    core_peer = {"grp": chip * 2 + upper, "slab": slab}
    chip_peer = {"grp": (1 - chip) * 2 + 1 - upper, "slab": slab}
    cross_peer = {"grp": (1 - chip) * 2 + upper, "slab": slab}
    beyond = (slab + slabs - 1 + 2 * upper) % slabs
    wrapped = slab % 8 == 0
    rushed = (slab % 8 == 7) & (upper == 1)
    edge_chips = (chip, 1 - chip)

    def cols(i):
        return pl.ds(pl.multiple_of(i * width, LANES), width)

    def load(h, i):
        where = (slice(None), pl.ds(h * half, half), cols(i))
        return pltpu.make_async_copy(states_ref.at[where], held_ref.at[where], load_sem.at[h * CHUNKS + i])

    def remote(src, dst, send, recv, peer):
        return pltpu.make_async_remote_copy(
            src_ref=src, dst_ref=dst, send_sem=send, recv_sem=recv, device_id=peer, device_id_type=MESH
        )

    def to_core(i):
        return remote(
            part.at[1 - upper, :, cols(i)], from_core.at[:, cols(i)], sent.at[1], core_recv.at[i], core_peer
        )

    def to_chip(i):
        return remote(
            chip_sum.at[:, cols(i)], from_chip.at[:, cols(i)], sent.at[2], chip_recv.at[i], chip_peer
        )

    def edge_cols(m):
        return slice(m * width, (m + 1) * width)

    def to_edge(m, k):
        peer = {"grp": edge_chips[k] * 2 + upper, "slab": beyond}
        out = edge_out.at[:, edge_cols(m)]
        return remote(out, edge_in.at[chip, :, edge_cols(m)], sent.at[0], edge_recv.at[2 * m + chip], peer)

    def from_edge(m, k):
        out = edge_out.at[:, edge_cols(m)]
        return remote(out, edge_in.at[k, :, edge_cols(m)], sent.at[0], edge_recv.at[2 * m + k], core_peer)

    def shifted(i):
        return pl.ds(pl.multiple_of(i * width + LANES, LANES), width)

    def to_inner(i):
        rows = pl.ds(pl.multiple_of((1 - upper) * 8, 8), 8)
        return remote(
            dens.at[rows, shifted(i)], inner_in.at[:, shifted(i)], sent.at[3], inner_recv.at[i], core_peer
        )

    def own_rows():
        return pl.ds(pl.multiple_of(upper * half, half), half)

    near_out = pl.ds(pl.multiple_of(upper * 24, 8), 8)
    far_out = pl.ds(pl.multiple_of(8 + upper * 8, 8), 8)

    def to_pot(i):
        span = NEAR_SPAN * LANES
        where = pot_ref.at[near_out, pl.ds(pl.multiple_of(i * span, LANES), span)]
        return remote(where, where, sent.at[4], pot_recv.at[i], core_peer)

    def to_pot_far():
        where = pot_ref.at[far_out, :]
        return remote(where, where, sent.at[5], pot_recv.at[CHUNKS], core_peer)

    barrier = pltpu.get_barrier_semaphore()

    def greet(peer):
        pl.semaphore_signal(barrier, inc=1, device_id=peer, device_id_type=MESH)

    @pl.when(upper == 0)
    def _():
        greet(chip_peer)
        greet({"grp": 0, "slab": beyond})
        greet({"grp": 2, "slab": beyond})

    @pl.when(upper == 1)
    def _():
        greet(core_peer)
        greet(cross_peer)
        greet({"grp": 0, "slab": beyond})
        greet({"grp": 2, "slab": beyond})

    occ_copy = pltpu.make_async_copy(occ_hbm, occ_ref, misc_sem.at[0])
    occ_copy.start()
    for i in range(CHUNKS):
        load(1, i).start()
    core_copy = pltpu.make_async_copy(core_ref.at[own_rows(), :], core_half, misc_sem.at[1])
    core_copy.start()
    for i in range(CHUNKS):
        load(0, i).start()

    occ_copy.wait()
    weights = [
        occ_ref[s].astype(jnp.float32) * (valence_norm / (OCC_DEN * s_dev * 4))
        for s in range(s_dev)
    ]

    def density_part(h, i):
        load(h, i).wait()

        def tile_step(t, carry):
            lanes = pl.ds(pl.multiple_of(i * width + t * STEP, STEP), STEP)
            total = jnp.zeros((half, STEP), jnp.float32)
            for s in range(s_dev):
                wide = held_ref[s, h * half : (h + 1) * half, lanes].astype(jnp.float32)
                total = total + (wide * weights[s]) * wide
            part[h, :, lanes] = total
            return carry

        lax.fori_loop(0, width // STEP, tile_step, 0)

    first_rows = lax.broadcasted_iota(jnp.int32, (8, LANES), 0) < 4
    with_core = (1 - chip).astype(jnp.float32)
    is_low = upper == 0

    def sum_chip(i):
        to_core(i).wait_recv()
        chip_sum[:, cols(i)] = (part[upper, :, cols(i)] + from_core[:, cols(i)]) + with_core * core_half[:, cols(i)]

    def pack(m):
        edge_rows = pl.ds(pl.multiple_of(upper * 8, 8), 8)
        for t in range(width // LANES):
            here = 2 * m * width + t * LANES
            front = chip_sum[edge_rows, here : here + LANES]
            back = chip_sum[edge_rows, here + width : here + width + LANES]
            front_turned, back_turned = pltpu.roll(front, 4, 0), pltpu.roll(back, 4, 0)
            low_edge = jnp.where(first_rows, front, back_turned)
            high_edge = jnp.where(first_rows, front_turned, back)
            edge_out[:, m * width + t * LANES : m * width + (t + 1) * LANES] = jnp.where(is_low, low_edge, high_edge)

    def send_edges(m):
        for k in range(2):
            to_edge(m, k).start()

    def meet_slabs():
        @pl.when(upper == 1)
        def _():
            pl.semaphore_wait(barrier, 4)
            pl.semaphore_signal(slab_sem, inc=1, device_id=core_peer, device_id_type=MESH)

        @pl.when(upper == 0)
        def _():
            pl.semaphore_wait(slab_sem, 1)

    def sum_and_send(m):
        for i in (2 * m, 2 * m + 1):
            sum_chip(i)
        pack(m)

        @pl.when(jnp.logical_not(wrapped))
        def _():
            if m == 0:
                meet_slabs()
            send_edges(m)

        @pl.when(jnp.logical_not(rushed))
        def _():
            for i in (2 * m, 2 * m + 1):
                to_chip(i).start()

        if m == 1:

            @pl.when(rushed)
            def _():
                for i in range(CHUNKS):
                    to_chip(i).start()

    for i in range(CHUNKS):
        density_part(1, i)
        if i == GATE:

            @pl.when(upper == 0)
            def _():
                pl.semaphore_wait(barrier, 3)
                pl.semaphore_signal(group_sem, inc=1, device_id=core_peer, device_id_type=MESH)
                for j in range(GATE):
                    to_core(j).start()

        if i >= GATE:

            @pl.when(upper == 0)
            def _():
                to_core(i).start()

    core_copy.wait()
    for i in range(CHUNKS):
        if i % 2 == 0:
            @pl.when(upper == 1)
            def _():
                if i == 0:
                    pl.semaphore_wait(group_sem, 1)
                sum_and_send(i // 2)
        density_part(0, i)

        @pl.when(upper == 1)
        def _():
            to_core(i).start()

    @pl.when(upper == 0)
    def _():
        for m in range(2):
            sum_and_send(m)

    @pl.when(wrapped)
    def _():
        meet_slabs()
        for m in range(2):
            send_edges(m)

    lane = lax.broadcasted_iota(jnp.int32, (1, LANES), 1)
    inner = lane % NY
    low = lane < NY
    row = lax.broadcasted_iota(jnp.int32, (8, LANES), 0)
    own_four = jnp.where(is_low, row, 7 - row) < 4
    own_two = jnp.where(is_low, row, 7 - row) < 2
    near = pl.ds(pl.multiple_of(upper * 8, 8), 8)
    far = pl.ds(pl.multiple_of((1 - upper) * 8, 8), 8)

    tiles = width // LANES
    reach = (tiles + 2) * LANES
    last = n_tiles * LANES
    first_copy, last_copy = slice(last + LANES, last + 2 * LANES), slice(0, LANES)
    first_tile, last_tile = slice(LANES, 2 * LANES), slice(last, last + LANES)

    def at(j):
        return slice(j * LANES, (j + 1) * LANES)

    def total(i):
        to_chip(i).wait_recv()
        dens[:, shifted(i)] = chip_sum[:, cols(i)] + from_chip[:, cols(i)]
        to_inner(i).start()

    def flows(fields, turned, j):
        centre = fields[j]
        grad_x = along_x(fields[j - 1], turned[j - 1], turned[j], fields[j + 1], turned[j + 1], low)
        grad_y = along_y(centre, turned[j], inner)
        grad_z = along_z(centre)
        sigma = grad_x * grad_x + grad_y * grad_y + grad_z * grad_z
        root = jnp.exp2(jnp.log2(centre) * (-1.0 / 3.0))
        root2 = root * root
        root4 = root2 * root2
        share = 1.0 / (1.0 + u_scale * (sigma * (root4 * root4)))
        flow = flow_scale * (root4 * (share * share))
        d_dens = (slope_scale * (centre * root2)) * (
            (1.0 + kappa) + share * (2.0 * kappa * share - 3.0 * kappa)
        )
        return flow * grad_x, flow * grad_y, flow * grad_z, d_dens

    def first_pass(start, count):
        where = [at(t % n_tiles + 1) for t in range(start - 1, start + count + 1)]
        fields = [jnp.concatenate([dens[:, w], inner_in[:, w]], axis=0) for w in where]
        turned = [swap_halves(f) for f in fields]
        for j in range(1, count + 1):
            part_x, part_y, part_z, d_dens = flows(fields, turned, j)
            part_y = part_y[:half]
            rest = d_dens[:half] - along_y(part_y, swap_halves(part_y), inner)
            flow_x[:, where[j]] = part_x[:half]
            local[:, where[j]] = rest - along_z(part_z)[:half]
            near_rest[:, where[j]] = jnp.where(is_low, rest[:8], rest[8:])
            near_z[:, where[j]] = jnp.where(is_low, part_z[:8], part_z[8:half])

    def second_pass(g, carry):
        where = pl.ds(pl.multiple_of(g * SPAN * LANES, LANES), (SPAN + 2) * LANES)
        dens_w, flow_w, local_w = (ref.at[near, where] for ref in (dens, flow_x, local))
        outer_w, rest_w, z_w = (ref.at[:, where] for ref in (outer, near_rest, near_z))
        fields = [
            jnp.where(own_four, outer_w[:, at(j)], pltpu.roll(dens_w[:, at(j)], 4, 0)) for j in range(SPAN + 2)
        ]
        turned = [swap_halves(f) for f in fields]
        for j in range(1, SPAN + 1):
            part_x, part_y, part_z, d_dens = flows(fields, turned, j)
            rest = d_dens - along_y(part_y, swap_halves(part_y), inner)
            rest = jnp.where(own_two, pltpu.roll(rest, 4, 0), rest_w[:, at(j)])
            old_z = z_w[:, at(j)]
            row_z = jnp.where(
                first_rows,
                pltpu.roll(jnp.where(is_low, part_z, old_z), 6, 0),
                pltpu.roll(jnp.where(is_low, old_z, part_z), 2, 0),
            )
            div_z = along_z(row_z)
            div_z = jnp.where(is_low, pltpu.roll(div_z, 6, 0), pltpu.roll(div_z, 2, 0))
            local_w[:, at(j)] = jnp.where(own_four, rest - div_z, local_w[:, at(j)])
            flow_w[:, at(j)] = jnp.where(own_two, pltpu.roll(part_x, 4, 0), flow_w[:, at(j)])
        return carry

    def finish(rows, out_rows, g, span):
        where = pl.ds(pl.multiple_of(g * span * LANES, LANES), (span + 2) * LANES)
        flow_w, local_w = flow_x.at[rows, where], local.at[rows, where]
        out_w = pot_ref.at[out_rows, pl.ds(pl.multiple_of(g * span * LANES, LANES), span * LANES)]
        fields = [flow_w[:, at(j)] for j in range(span + 2)]
        turned = [swap_halves(f) for f in fields]
        for j in range(1, span + 1):
            div_x = along_x(fields[j - 1], turned[j - 1], turned[j], fields[j + 1], turned[j + 1], low)
            out_w[:, at(j - 1)] = local_w[:, at(j)] - div_x

    def finish_far(g, carry):
        finish(far, far_out, g, FAR_SPAN)
        return carry

    def finish_near(g, carry):
        finish(near, near_out, g, NEAR_SPAN)
        to_pot(g).start()
        return carry

    def wrap(ref, rows):
        ref[rows, first_copy] = ref[rows, first_tile]
        ref[rows, last_copy] = ref[rows, last_tile]

    everything = slice(None)
    total(0)
    total(1)
    to_inner(0).wait_recv()
    first_pass(1, tiles - 2)
    for i in range(1, CHUNKS - 1):
        total(i + 1)
        to_inner(i).wait_recv()
        first_pass(i * tiles - 1, tiles)
    to_inner(CHUNKS - 1).wait_recv()
    first_pass((CHUNKS - 1) * tiles - 1, tiles + 2)
    wrap(flow_x, everything)
    wrap(dens, near)
    lax.fori_loop(0, n_tiles // FAR_SPAN, finish_far, 0)
    to_pot_far().start()
    for m in range(2):
        for k in range(2):
            from_edge(m, k).wait_recv()

    for m in range(2):
        for t in range(tiles):
            both = edge_in[0, :, at(m * tiles + t)] + edge_in[1, :, at(m * tiles + t)]
            turned = pltpu.roll(both, 4, 0)
            outer[:, at(2 * m * tiles + t + 1)] = jnp.where(first_rows, both, turned)
            outer[:, at((2 * m + 1) * tiles + t + 1)] = jnp.where(first_rows, turned, both)
    wrap(outer, everything)
    lax.fori_loop(0, n_tiles // SPAN, second_pass, 0)
    wrap(flow_x, near)
    lax.fori_loop(0, n_tiles // NEAR_SPAN, finish_near, 0)
    for i in range(n_tiles // NEAR_SPAN):
        to_pot(i).wait_recv()
    to_pot_far().wait_recv()
    kinds = (
        edge_in,
        from_core,
        from_chip,
        inner_in.at[:, pl.ds(LANES, cells)],
        pot_ref.at[near_out, :],
        pot_ref.at[far_out, :],
    )
    for kind, ref in enumerate(kinds):
        remote(ref, ref, sent.at[kind], edge_recv.at[0], core_peer).wait_send()


def apply_kernel(held_ref, pot_ref, applied_ref, out_ref, staged, store_sem, pot_sem):
    s_dev, planes, cells = held_ref.shape
    width = cells // STORES
    pot_copy = pltpu.make_async_copy(pot_ref, out_ref, pot_sem)
    pot_copy.start()

    def store(i):
        cols = pl.ds(i * width, width)
        return pltpu.make_async_copy(staged.at[:, :, cols], applied_ref.at[:, :, cols], store_sem.at[i])

    for i in range(STORES):
        cols = pl.ds(i * width, width)
        pot = pot_ref[:, cols].astype(jnp.bfloat16)

        def state_step(s, carry):
            staged[s, :, cols] = held_ref[s, :, cols] * pot
            return carry

        lax.fori_loop(0, s_dev, state_step, 0, unroll=8)
        store(i).start()
    for i in range(STORES):
        store(i).wait()
    pot_copy.wait()


def body(slabs, states, core_density, occupancy):
    s_dev, planes, cells = states.shape
    half = planes // 2
    vmem = pl.BlockSpec(memory_space=pltpu.VMEM)
    hbm = pl.BlockSpec(memory_space=pltpu.HBM)
    states = pltpu.with_memory_space_constraint(states, pltpu.HBM)
    core_density = pltpu.with_memory_space_constraint(core_density, pltpu.HBM)
    occupancy = pltpu.with_memory_space_constraint(occupancy, pltpu.HBM)

    def rows(count):
        return pltpu.VMEM((count, cells), jnp.float32)

    def wide(count):
        return pltpu.VMEM((count, cells + 2 * LANES), jnp.float32)

    def sems(count):
        return pltpu.SemaphoreType.DMA((count,))

    held, pot = pl.pallas_call(
        functools.partial(potential_kernel, slabs),
        out_shape=(
            pltpu.VMEM((s_dev, planes, cells), jnp.bfloat16),
            pltpu.VMEM((planes, cells), jnp.float32),
        ),
        in_specs=[hbm, hbm, hbm],
        out_specs=(vmem, vmem),
        scratch_shapes=[
            pltpu.SMEM((s_dev,), jnp.int32),
            pltpu.VMEM((2, half, cells), jnp.float32),
            rows(half),
            rows(half),
            rows(half),
            rows(half),
            wide(half),
            wide(8),
            pltpu.VMEM((8, cells // 2), jnp.float32),
            pltpu.VMEM((2, 8, cells // 2), jnp.float32),
            wide(8),
            wide(half),
            wide(half),
            wide(8),
            wide(8),
            sems(2 * CHUNKS),
            sems(2),
            pltpu.SemaphoreType.REGULAR,
            pltpu.SemaphoreType.REGULAR,
        ]
        + [sems(6), sems(CHUNKS), sems(CHUNKS), sems(CHUNKS), sems(4), sems(CHUNKS + 1)],
        compiler_params=pltpu.CompilerParams(
            collective_id=0, has_side_effects=True, vmem_limit_bytes=24 * 1024 * 1024
        ),
        name="potential",
    )(occupancy, states, core_density)
    return pl.pallas_call(
        apply_kernel,
        out_shape=(
            jax.ShapeDtypeStruct((s_dev, planes, cells), jnp.bfloat16),
            jax.ShapeDtypeStruct((planes, cells), jnp.float32),
        ),
        in_specs=[vmem, vmem],
        out_specs=(hbm, hbm),
        scratch_shapes=[
            pltpu.VMEM((s_dev, planes, cells), jnp.bfloat16),
            sems(STORES),
            pltpu.SemaphoreType.DMA,
        ],
        compiler_params=pltpu.CompilerParams(vmem_limit_bytes=32 * 1024 * 1024),
        name="apply",
    )(held, pot)


def solution(mesh):
    placed = (P("grp", "slab", None), P("slab", None), P("grp"))
    return jax.shard_map(
        functools.partial(body, mesh.shape["slab"]),
        mesh=mesh,
        in_specs=placed,
        out_specs=(P("grp", "slab", None), P("slab", None)),
        check_vma=False,
    )
```

```python
import functools
import math

import jax
import jax.numpy as jnp
from jax import lax
from jax.experimental import pallas as pl
from jax.experimental.pallas import tpu as pltpu
from jax.sharding import PartitionSpec as P

MESH = pl.DeviceIdType.MESH

NX = 64
NY = 64
OCC_DEN = 8
LANES = 128

grid_step = 0.5
valence_norm = 0.04

kappa = 0.804
mu = 0.2195149727645171
exchange = -0.75 * (3.0 / math.pi) ** (1.0 / 3.0)
reduced_scale = 4.0 * (3.0 * math.pi**2) ** (2.0 / 3.0)
stencil_scale = 1.0 / (12.0 * grid_step)
u_scale = mu / kappa / reduced_scale * stencil_scale * stencil_scale
flow_scale = 2.0 * exchange * mu / reduced_scale * stencil_scale * stencil_scale
slope_scale = exchange * 4.0 / 3.0

CHUNKS = 4
STEP = 4 * LANES
GATE = 2
PARTS = ((2, 12), (14, 18), (0, 2))
STORES = 8


def stencil(before2, before1, after1, after2):
    return (before2 - after2) + 8.0 * (after1 - before1)


def swap_halves(tile):
    return pltpu.roll(tile, 64, 1)


def along_y(tile, swapped, inner):
    before2 = pltpu.roll(jnp.where(inner >= NY - 2, swapped, tile), 2, 1)
    before1 = pltpu.roll(jnp.where(inner >= NY - 1, swapped, tile), 1, 1)
    after1 = pltpu.roll(jnp.where(inner < 1, swapped, tile), LANES - 1, 1)
    after2 = pltpu.roll(jnp.where(inner < 2, swapped, tile), LANES - 2, 1)
    return stencil(before2, before1, after1, after2)


def along_x(left, left_swapped, swapped, right, right_swapped, low):
    before1 = jnp.where(low, left_swapped, swapped)
    after1 = jnp.where(low, swapped, right_swapped)
    return stencil(left, before1, after1, right)


def along_z(tile):
    rows = tile.shape[0]
    return stencil(
        pltpu.roll(tile, 2, 0),
        pltpu.roll(tile, 1, 0),
        pltpu.roll(tile, rows - 1, 0),
        pltpu.roll(tile, rows - 2, 0),
    )


def potential_kernel(
    slabs,
    occ_hbm,
    states_ref,
    core_ref,
    held_ref,
    pot_ref,
    occ_ref,
    part,
    from_core,
    chip_sum,
    from_chip,
    core_half,
    dens,
    inner_in,
    edge_out,
    edge_in,
    outer,
    flow_x,
    local,
    near_rest,
    near_z,
    load_sem,
    misc_sem,
    group_sem,
    slab_sem,
    sent,
    core_recv,
    chip_recv,
    inner_recv,
    edge_recv,
    pot_recv,
):
    s_dev, planes, cells = states_ref.shape
    half = planes // 2
    width = cells // CHUNKS
    n_tiles = cells // LANES

    grp = lax.axis_index("grp")
    slab = lax.axis_index("slab")
    chip = grp // 2
    upper = 1 - grp % 2
    core_peer = {"grp": chip * 2 + upper, "slab": slab}
    chip_peer = {"grp": (1 - chip) * 2 + 1 - upper, "slab": slab}
    cross_peer = {"grp": (1 - chip) * 2 + upper, "slab": slab}
    beyond = (slab + slabs - 1 + 2 * upper) % slabs
    wrapped = slab % 8 == 0
    rushed = (slab % 8 == 7) & (upper == 1)
    edge_chips = (chip, 1 - chip)

    near = pl.ds(pl.multiple_of(upper * 8, 8), 8)
    far = pl.ds(pl.multiple_of((1 - upper) * 8, 8), 8)

    def cols(i):
        return pl.ds(pl.multiple_of(i * width, LANES), width)

    def load(h, i):
        where = (slice(None), pl.ds(h * half, half), cols(i))
        return pltpu.make_async_copy(states_ref.at[where], held_ref.at[where], load_sem.at[h * CHUNKS + i])

    def remote(src, dst, send, recv, peer):
        return pltpu.make_async_remote_copy(
            src_ref=src, dst_ref=dst, send_sem=send, recv_sem=recv, device_id=peer, device_id_type=MESH
        )

    def to_core(i):
        return remote(
            part.at[1 - upper, :, cols(i)], from_core.at[:, cols(i)], sent.at[1], core_recv.at[i], core_peer
        )

    def to_chip(rows, i):
        tile_at = (rows, cols(i))
        which = i + CHUNKS * (rows is near)
        return remote(chip_sum.at[tile_at], from_chip.at[tile_at], sent.at[2], chip_recv.at[which], chip_peer)

    def edge_cols(m):
        return slice(m * width, (m + 1) * width)

    def to_edge(m, k):
        peer = {"grp": edge_chips[k] * 2 + upper, "slab": beyond}
        out = edge_out.at[:, edge_cols(m)]
        return remote(out, edge_in.at[chip, :, edge_cols(m)], sent.at[0], edge_recv.at[2 * m + chip], peer)

    def from_edge(m, k):
        out = edge_out.at[:, edge_cols(m)]
        return remote(out, edge_in.at[k, :, edge_cols(m)], sent.at[0], edge_recv.at[2 * m + k], core_peer)

    def shifted(i):
        return pl.ds(pl.multiple_of(i * width + LANES, LANES), width)

    def to_inner(i):
        return remote(
            dens.at[far, shifted(i)], inner_in.at[:, shifted(i)], sent.at[3], inner_recv.at[i], core_peer
        )

    def own_rows():
        return pl.ds(pl.multiple_of(upper * half, half), half)

    near_out = pl.ds(pl.multiple_of(upper * 24, 8), 8)
    far_out = pl.ds(pl.multiple_of(8 + upper * 8, 8), 8)

    def to_pot(i):
        start, count = PARTS[i]
        where = pot_ref.at[near_out, pl.ds(start * LANES, count * LANES)]
        return remote(where, where, sent.at[4], pot_recv.at[i], core_peer)

    def to_pot_far():
        where = pot_ref.at[far_out, :]
        return remote(where, where, sent.at[5], pot_recv.at[CHUNKS], core_peer)

    barrier = pltpu.get_barrier_semaphore()

    def greet(peer):
        pl.semaphore_signal(barrier, inc=1, device_id=peer, device_id_type=MESH)

    @pl.when(upper == 0)
    def _():
        greet(chip_peer)
        greet({"grp": 0, "slab": beyond})
        greet({"grp": 2, "slab": beyond})

    @pl.when(upper == 1)
    def _():
        greet(core_peer)
        greet(cross_peer)
        greet({"grp": 0, "slab": beyond})
        greet({"grp": 2, "slab": beyond})

    occ_copy = pltpu.make_async_copy(occ_hbm, occ_ref, misc_sem.at[0])
    occ_copy.start()
    for i in range(CHUNKS):
        load(1, i).start()
    core_copy = pltpu.make_async_copy(core_ref.at[own_rows(), :], core_half, misc_sem.at[1])
    core_copy.start()
    for i in range(CHUNKS):
        load(0, i).start()

    occ_copy.wait()
    weights = [
        occ_ref[s].astype(jnp.float32) * (valence_norm / (OCC_DEN * s_dev * 4))
        for s in range(s_dev)
    ]

    def density_part(h, i):
        load(h, i).wait()

        def tile_step(t, carry):
            lanes = pl.ds(pl.multiple_of(i * width + t * STEP, STEP), STEP)
            total = jnp.zeros((half, STEP), jnp.float32)
            for s in range(s_dev):
                wide = held_ref[s, h * half : (h + 1) * half, lanes].astype(jnp.float32)
                total = total + (wide * weights[s]) * wide
            part[h, :, lanes] = total
            return carry

        lax.fori_loop(0, width // STEP, tile_step, 0)

    first_rows = lax.broadcasted_iota(jnp.int32, (8, LANES), 0) < 4
    with_core = (1 - chip).astype(jnp.float32)
    is_low = upper == 0

    def sum_chip(i):
        to_core(i).wait_recv()
        chip_sum[:, cols(i)] = (part[upper, :, cols(i)] + from_core[:, cols(i)]) + with_core * core_half[:, cols(i)]

    def pack(m):
        edge_rows = pl.ds(pl.multiple_of(upper * 8, 8), 8)
        for t in range(width // LANES):
            here = 2 * m * width + t * LANES
            front = chip_sum[edge_rows, here : here + LANES]
            back = chip_sum[edge_rows, here + width : here + width + LANES]
            front_turned, back_turned = pltpu.roll(front, 4, 0), pltpu.roll(back, 4, 0)
            low_edge = jnp.where(first_rows, front, back_turned)
            high_edge = jnp.where(first_rows, front_turned, back)
            edge_out[:, m * width + t * LANES : m * width + (t + 1) * LANES] = jnp.where(is_low, low_edge, high_edge)

    def send_edges(m):
        for k in range(2):
            to_edge(m, k).start()

    def meet_slabs():
        @pl.when(upper == 1)
        def _():
            pl.semaphore_wait(barrier, 4)
            pl.semaphore_signal(slab_sem, inc=1, device_id=core_peer, device_id_type=MESH)

        @pl.when(upper == 0)
        def _():
            pl.semaphore_wait(slab_sem, 1)

    def sum_and_send(m):
        for i in (2 * m, 2 * m + 1):
            sum_chip(i)
        pack(m)

        @pl.when(jnp.logical_not(wrapped))
        def _():
            if m == 0:
                meet_slabs()
            send_edges(m)

        @pl.when(jnp.logical_not(rushed))
        def _():
            for i in (2 * m, 2 * m + 1):
                to_chip(far, i).start()

        if m == 1:

            @pl.when(rushed)
            def _():
                for i in range(CHUNKS):
                    to_chip(far, i).start()

            for i in range(CHUNKS):
                to_chip(near, i).start()

    for i in range(CHUNKS):
        density_part(1, i)
        if i == GATE:

            @pl.when(upper == 0)
            def _():
                pl.semaphore_wait(barrier, 3)
                pl.semaphore_signal(group_sem, inc=1, device_id=core_peer, device_id_type=MESH)
                for j in range(GATE):
                    to_core(j).start()

        if i >= GATE:

            @pl.when(upper == 0)
            def _():
                to_core(i).start()

    core_copy.wait()
    for i in range(CHUNKS):
        if i % 2 == 0:
            @pl.when(upper == 1)
            def _():
                if i == 0:
                    pl.semaphore_wait(group_sem, 1)
                sum_and_send(i // 2)
        density_part(0, i)

        @pl.when(upper == 1)
        def _():
            to_core(i).start()

    @pl.when(upper == 0)
    def _():
        for m in range(2):
            sum_and_send(m)

    @pl.when(wrapped)
    def _():
        meet_slabs()
        for m in range(2):
            send_edges(m)

    lane = lax.broadcasted_iota(jnp.int32, (1, LANES), 1)
    inner = lane % NY
    low = lane < NY
    row = lax.broadcasted_iota(jnp.int32, (8, LANES), 0)
    own_four = jnp.where(is_low, row, 7 - row) < 4
    own_two = jnp.where(is_low, row, 7 - row) < 2

    tiles = width // LANES

    def at(j):
        return slice(j * LANES, (j + 1) * LANES)

    def total(rows, i):
        to_chip(rows, i).wait_recv()
        dens[rows, shifted(i)] = chip_sum[rows, cols(i)] + from_chip[rows, cols(i)]

    def flows(fields, turned, j):
        centre = fields[j]
        grad_x = along_x(fields[j - 1], turned[j - 1], turned[j], fields[j + 1], turned[j + 1], low)
        grad_y = along_y(centre, turned[j], inner)
        grad_z = along_z(centre)
        sigma = grad_x * grad_x + grad_y * grad_y + grad_z * grad_z
        root = jnp.exp2(jnp.log2(centre) * (-1.0 / 3.0))
        root2 = root * root
        root4 = root2 * root2
        share = 1.0 / (1.0 + u_scale * (sigma * (root4 * root4)))
        flow = flow_scale * (root4 * (share * share))
        d_dens = (slope_scale * (centre * root2)) * (
            (1.0 + kappa) + share * (2.0 * kappa * share - 3.0 * kappa)
        )
        return flow * grad_x, flow * grad_y, flow * grad_z, d_dens

    def first_pass(start, count):
        where = [at(t % n_tiles + 1) for t in range(start - 1, start + count + 1)]
        fields = [jnp.concatenate([dens[:, w], inner_in[:, w]], axis=0) for w in where]
        turned = [swap_halves(f) for f in fields]
        for j in range(1, count + 1):
            part_x, part_y, part_z, d_dens = flows(fields, turned, j)
            part_y = part_y[:half]
            rest = d_dens[:half] - along_y(part_y, swap_halves(part_y), inner)
            flow_x[:, where[j]] = part_x[:half]
            local[:, where[j]] = rest - along_z(part_z)[:half]
            near_rest[:, where[j]] = jnp.where(is_low, rest[:8], rest[8:])
            near_z[:, where[j]] = jnp.where(is_low, part_z[:8], part_z[8:half])

    def second_pass(start, count):
        where = [at(t % n_tiles + 1) for t in range(start - 1, start + count + 1)]
        fields = [jnp.where(own_four, outer[:, w], pltpu.roll(dens[near, w], 4, 0)) for w in where]
        turned = [swap_halves(f) for f in fields]
        for j in range(1, count + 1):
            part_x, part_y, part_z, d_dens = flows(fields, turned, j)
            rest = d_dens - along_y(part_y, swap_halves(part_y), inner)
            rest = jnp.where(own_two, pltpu.roll(rest, 4, 0), near_rest[:, where[j]])
            old_z = near_z[:, where[j]]
            row_z = jnp.where(
                first_rows,
                pltpu.roll(jnp.where(is_low, part_z, old_z), 6, 0),
                pltpu.roll(jnp.where(is_low, old_z, part_z), 2, 0),
            )
            div_z = along_z(row_z)
            div_z = jnp.where(is_low, pltpu.roll(div_z, 6, 0), pltpu.roll(div_z, 2, 0))
            local[near, where[j]] = jnp.where(own_four, rest - div_z, local[near, where[j]])
            flow_x[near, where[j]] = jnp.where(own_two, pltpu.roll(part_x, 4, 0), flow_x[near, where[j]])

    def finish(rows, out_rows, start, count):
        where = [at(t % n_tiles + 1) for t in range(start - 1, start + count + 1)]
        fields = [flow_x[rows, w] for w in where]
        turned = [swap_halves(f) for f in fields]
        for j in range(1, count + 1):
            div_x = along_x(fields[j - 1], turned[j - 1], turned[j], fields[j + 1], turned[j + 1], low)
            pot_ref[out_rows, at((start + j - 1) % n_tiles)] = local[rows, where[j]] - div_x

    def unpack(m):
        for k in range(2):
            from_edge(m, k).wait_recv()
        for t in range(tiles):
            both = edge_in[0, :, at(m * tiles + t)] + edge_in[1, :, at(m * tiles + t)]
            turned = pltpu.roll(both, 4, 0)
            outer[:, at(2 * m * tiles + t + 1)] = jnp.where(first_rows, both, turned)
            outer[:, at((2 * m + 1) * tiles + t + 1)] = jnp.where(first_rows, turned, both)

    for i in range(CHUNKS):
        total(far, i)
        to_inner(i).start()
    for i in range(CHUNKS):
        total(near, i)
        to_inner(i).wait_recv()
        if i == 0:
            first_pass(1, tiles - 2)
        elif i < CHUNKS - 1:
            first_pass(i * tiles - 1, tiles)
        else:
            first_pass(i * tiles - 1, tiles + 2)
    finish(far, far_out, 0, n_tiles)
    to_pot_far().start()
    unpack(0)
    second_pass(1, 2 * tiles - 2)
    finish(near, near_out, *PARTS[0])
    to_pot(0).start()
    unpack(1)
    second_pass(2 * tiles - 1, 2 * tiles + 2)
    for i in (1, 2):
        finish(near, near_out, *PARTS[i])
        to_pot(i).start()
    for i in range(len(PARTS)):
        to_pot(i).wait_recv()
    to_pot_far().wait_recv()
    kinds = (
        edge_in,
        from_core,
        from_chip,
        inner_in.at[:, pl.ds(LANES, cells)],
        pot_ref.at[near_out, :],
        pot_ref.at[far_out, :],
    )
    for kind, ref in enumerate(kinds):
        remote(ref, ref, sent.at[kind], edge_recv.at[0], core_peer).wait_send()


def apply_kernel(held_ref, pot_ref, applied_ref, out_ref, staged, store_sem, pot_sem):
    s_dev, planes, cells = held_ref.shape
    width = cells // STORES
    pot_copy = pltpu.make_async_copy(pot_ref, out_ref, pot_sem)
    pot_copy.start()

    def store(i):
        cols = pl.ds(i * width, width)
        return pltpu.make_async_copy(staged.at[:, :, cols], applied_ref.at[:, :, cols], store_sem.at[i])

    for i in range(STORES):
        cols = pl.ds(i * width, width)
        pot = pot_ref[:, cols].astype(jnp.bfloat16)

        def state_step(s, carry):
            staged[s, :, cols] = held_ref[s, :, cols] * pot
            return carry

        lax.fori_loop(0, s_dev, state_step, 0, unroll=8)
        store(i).start()
    for i in range(STORES):
        store(i).wait()
    pot_copy.wait()


def body(slabs, states, core_density, occupancy):
    s_dev, planes, cells = states.shape
    half = planes // 2
    vmem = pl.BlockSpec(memory_space=pltpu.VMEM)
    hbm = pl.BlockSpec(memory_space=pltpu.HBM)
    states = pltpu.with_memory_space_constraint(states, pltpu.HBM)
    core_density = pltpu.with_memory_space_constraint(core_density, pltpu.HBM)
    occupancy = pltpu.with_memory_space_constraint(occupancy, pltpu.HBM)

    def rows(count):
        return pltpu.VMEM((count, cells), jnp.float32)

    def wide(count):
        return pltpu.VMEM((count, cells + 2 * LANES), jnp.float32)

    def sems(count):
        return pltpu.SemaphoreType.DMA((count,))

    held, pot = pl.pallas_call(
        functools.partial(potential_kernel, slabs),
        out_shape=(
            pltpu.VMEM((s_dev, planes, cells), jnp.bfloat16),
            pltpu.VMEM((planes, cells), jnp.float32),
        ),
        in_specs=[hbm, hbm, hbm],
        out_specs=(vmem, vmem),
        scratch_shapes=[
            pltpu.SMEM((s_dev,), jnp.int32),
            pltpu.VMEM((2, half, cells), jnp.float32),
            rows(half),
            rows(half),
            rows(half),
            rows(half),
            wide(half),
            wide(8),
            pltpu.VMEM((8, cells // 2), jnp.float32),
            pltpu.VMEM((2, 8, cells // 2), jnp.float32),
            wide(8),
            wide(half),
            wide(half),
            wide(8),
            wide(8),
            sems(2 * CHUNKS),
            sems(2),
            pltpu.SemaphoreType.REGULAR,
            pltpu.SemaphoreType.REGULAR,
        ]
        + [sems(6), sems(CHUNKS), sems(2 * CHUNKS), sems(CHUNKS), sems(4), sems(CHUNKS + 1)],
        compiler_params=pltpu.CompilerParams(
            collective_id=0, has_side_effects=True, vmem_limit_bytes=24 * 1024 * 1024
        ),
        name="potential",
    )(occupancy, states, core_density)
    return pl.pallas_call(
        apply_kernel,
        out_shape=(
            jax.ShapeDtypeStruct((s_dev, planes, cells), jnp.bfloat16),
            jax.ShapeDtypeStruct((planes, cells), jnp.float32),
        ),
        in_specs=[vmem, vmem],
        out_specs=(hbm, hbm),
        scratch_shapes=[
            pltpu.VMEM((s_dev, planes, cells), jnp.bfloat16),
            sems(STORES),
            pltpu.SemaphoreType.DMA,
        ],
        compiler_params=pltpu.CompilerParams(vmem_limit_bytes=32 * 1024 * 1024),
        name="apply",
    )(held, pot)


def solution(mesh):
    placed = (P("grp", "slab", None), P("slab", None), P("grp"))
    return jax.shard_map(
        functools.partial(body, mesh.shape["slab"]),
        mesh=mesh,
        in_specs=placed,
        out_specs=(P("grp", "slab", None), P("slab", None)),
        check_vma=False,
    )
```

```python
import functools
import math

import jax
import jax.numpy as jnp
from jax import lax
from jax.experimental import pallas as pl
from jax.experimental.pallas import tpu as pltpu
from jax.sharding import PartitionSpec as P

MESH = pl.DeviceIdType.MESH

NX = 64
NY = 64
OCC_DEN = 8
LANES = 128

grid_step = 0.5
valence_norm = 0.04

kappa = 0.804
mu = 0.2195149727645171
exchange = -0.75 * (3.0 / math.pi) ** (1.0 / 3.0)
reduced_scale = 4.0 * (3.0 * math.pi**2) ** (2.0 / 3.0)
stencil_scale = 1.0 / (12.0 * grid_step)
u_scale = mu / kappa / reduced_scale * stencil_scale * stencil_scale
flow_scale = 2.0 * exchange * mu / reduced_scale * stencil_scale * stencil_scale
slope_scale = exchange * 4.0 / 3.0

CHUNKS = 4
STEP = 4 * LANES
LOADS = 8
GATE = 2
PARTS = ((2, 12), (14, 18), (0, 2))
STORES = 8


def stencil(before2, before1, after1, after2):
    return (before2 - after2) + 8.0 * (after1 - before1)


def swap_halves(tile):
    return pltpu.roll(tile, 64, 1)


def along_y(tile, swapped, inner):
    before2 = pltpu.roll(jnp.where(inner >= NY - 2, swapped, tile), 2, 1)
    before1 = pltpu.roll(jnp.where(inner >= NY - 1, swapped, tile), 1, 1)
    after1 = pltpu.roll(jnp.where(inner < 1, swapped, tile), LANES - 1, 1)
    after2 = pltpu.roll(jnp.where(inner < 2, swapped, tile), LANES - 2, 1)
    return stencil(before2, before1, after1, after2)


def along_x(left, left_swapped, swapped, right, right_swapped, low):
    before1 = jnp.where(low, left_swapped, swapped)
    after1 = jnp.where(low, swapped, right_swapped)
    return stencil(left, before1, after1, right)


def along_z(tile):
    rows = tile.shape[0]
    return stencil(
        pltpu.roll(tile, 2, 0),
        pltpu.roll(tile, 1, 0),
        pltpu.roll(tile, rows - 1, 0),
        pltpu.roll(tile, rows - 2, 0),
    )


def potential_kernel(
    slabs,
    occ_hbm,
    states_ref,
    core_ref,
    held_ref,
    pot_ref,
    occ_ref,
    part,
    from_core,
    chip_sum,
    from_chip,
    core_half,
    dens,
    inner_in,
    edge_out,
    edge_in,
    outer,
    flow_x,
    local,
    near_rest,
    near_z,
    load_sem,
    misc_sem,
    group_sem,
    slab_sem,
    sent,
    core_recv,
    chip_recv,
    inner_recv,
    edge_recv,
    pot_recv,
):
    s_dev, planes, cells = states_ref.shape
    half = planes // 2
    width = cells // CHUNKS
    n_tiles = cells // LANES

    grp = lax.axis_index("grp")
    slab = lax.axis_index("slab")
    chip = grp // 2
    upper = 1 - grp % 2
    core_peer = {"grp": chip * 2 + upper, "slab": slab}
    chip_peer = {"grp": (1 - chip) * 2 + 1 - upper, "slab": slab}
    cross_peer = {"grp": (1 - chip) * 2 + upper, "slab": slab}
    beyond = (slab + slabs - 1 + 2 * upper) % slabs
    wrapped = slab % 8 == 0
    rushed = (slab % 8 == 7) & (upper == 1)
    edge_chips = (0, 1)

    near = pl.ds(pl.multiple_of(upper * 8, 8), 8)
    far = pl.ds(pl.multiple_of((1 - upper) * 8, 8), 8)

    def cols(i):
        return pl.ds(pl.multiple_of(i * width, LANES), width)

    def load(h, i):
        where = (slice(None), pl.ds(h * half, half), pl.ds(pl.multiple_of(i * STEP, STEP), STEP))
        return pltpu.make_async_copy(states_ref.at[where], held_ref.at[where], load_sem.at[h * LOADS + i])

    def remote(src, dst, send, recv, peer):
        return pltpu.make_async_remote_copy(
            src_ref=src, dst_ref=dst, send_sem=send, recv_sem=recv, device_id=peer, device_id_type=MESH
        )

    def to_core(i):
        return remote(
            part.at[1 - upper, :, cols(i)], from_core.at[:, cols(i)], sent.at[0], core_recv.at[i], core_peer
        )

    def to_chip(rows, i):
        tile_at = (rows, cols(i))
        which = i + CHUNKS * (rows is near)
        return remote(chip_sum.at[tile_at], from_chip.at[tile_at], sent.at[0], chip_recv.at[which], chip_peer)

    def edge_cols(m):
        return slice(m * width, (m + 1) * width)

    def to_edge(m, k):
        peer = {"grp": edge_chips[k] * 2 + upper, "slab": beyond}
        out = edge_out.at[:, edge_cols(m)]
        return remote(out, edge_in.at[chip, :, edge_cols(m)], sent.at[1], edge_recv.at[2 * m + chip], peer)

    def from_edge(m, k):
        out = edge_out.at[:, edge_cols(m)]
        return remote(out, edge_in.at[k, :, edge_cols(m)], sent.at[1], edge_recv.at[2 * m + k], core_peer)

    def shifted(i):
        return pl.ds(pl.multiple_of(i * width + LANES, LANES), width)

    def to_inner(i):
        return remote(
            dens.at[far, shifted(i)], inner_in.at[:, shifted(i)], sent.at[1], inner_recv.at[i], core_peer
        )

    def own_rows():
        return pl.ds(pl.multiple_of(upper * half, half), half)

    near_out = pl.ds(pl.multiple_of(upper * 24, 8), 8)
    far_out = pl.ds(pl.multiple_of(8 + upper * 8, 8), 8)

    def to_pot(i):
        start, count = PARTS[i]
        where = pot_ref.at[near_out, pl.ds(start * LANES, count * LANES)]
        return remote(where, where, sent.at[1], pot_recv.at[i], core_peer)

    def to_pot_far():
        where = pot_ref.at[far_out, :]
        return remote(where, where, sent.at[1], pot_recv.at[len(PARTS)], core_peer)

    barrier = pltpu.get_barrier_semaphore()

    def greet(peer):
        pl.semaphore_signal(barrier, inc=1, device_id=peer, device_id_type=MESH)

    @pl.when(upper == 0)
    def _():
        greet(chip_peer)
        greet({"grp": 0, "slab": beyond})
        greet({"grp": 2, "slab": beyond})

    @pl.when(upper == 1)
    def _():
        greet(core_peer)
        greet(cross_peer)
        greet({"grp": 0, "slab": beyond})
        greet({"grp": 2, "slab": beyond})

    occ_copy = pltpu.make_async_copy(occ_hbm, occ_ref, misc_sem.at[0])
    occ_copy.start()
    for i in range(LOADS):
        load(1, i).start()
    core_copy = pltpu.make_async_copy(core_ref.at[own_rows(), :], core_half, misc_sem.at[1])
    core_copy.start()
    for i in range(LOADS):
        load(0, i).start()

    occ_copy.wait()
    weights = [
        occ_ref[s].astype(jnp.float32) * (valence_norm / (OCC_DEN * s_dev * 4))
        for s in range(s_dev)
    ]

    def density_part(h, i):
        def tile_step(t, carry):
            load(h, i * (width // STEP) + t).wait()
            lanes = pl.ds(pl.multiple_of(i * width + t * STEP, STEP), STEP)
            total = jnp.zeros((half, STEP), jnp.float32)
            for s in range(s_dev):
                wide = held_ref[s, h * half : (h + 1) * half, lanes].astype(jnp.float32)
                total = total + (wide * weights[s]) * wide
            part[h, :, lanes] = total
            return carry

        lax.fori_loop(0, width // STEP, tile_step, 0)

    first_rows = lax.broadcasted_iota(jnp.int32, (8, LANES), 0) < 4
    with_core = (1 - chip).astype(jnp.float32)
    is_low = upper == 0

    def sum_chip(i):
        to_core(i).wait_recv()
        chip_sum[:, cols(i)] = (part[upper, :, cols(i)] + from_core[:, cols(i)]) + with_core * core_half[:, cols(i)]

    def pack(m):
        edge_rows = pl.ds(pl.multiple_of(upper * 8, 8), 8)
        for t in range(width // LANES):
            here = 2 * m * width + t * LANES
            front = chip_sum[edge_rows, here : here + LANES]
            back = chip_sum[edge_rows, here + width : here + width + LANES]
            front_turned, back_turned = pltpu.roll(front, 4, 0), pltpu.roll(back, 4, 0)
            low_edge = jnp.where(first_rows, front, back_turned)
            high_edge = jnp.where(first_rows, front_turned, back)
            edge_out[:, m * width + t * LANES : m * width + (t + 1) * LANES] = jnp.where(is_low, low_edge, high_edge)

    def send_edges(m):
        for k in range(2):
            to_edge(m, k).start()

    def meet_slabs():
        @pl.when(upper == 1)
        def _():
            pl.semaphore_wait(barrier, 4)
            pl.semaphore_signal(slab_sem, inc=1, device_id=core_peer, device_id_type=MESH)

        @pl.when(upper == 0)
        def _():
            pl.semaphore_wait(slab_sem, 1)

    def sum_and_send(m):
        for i in (2 * m, 2 * m + 1):
            sum_chip(i)
        pack(m)

        @pl.when(jnp.logical_not(wrapped))
        def _():
            if m == 0:
                meet_slabs()
            send_edges(m)

        @pl.when(jnp.logical_not(rushed))
        def _():
            for i in (2 * m, 2 * m + 1):
                to_chip(far, i).start()

        if m == 1:

            @pl.when(rushed)
            def _():
                for i in range(CHUNKS):
                    to_chip(far, i).start()

            for i in range(CHUNKS):
                to_chip(near, i).start()

    for i in range(CHUNKS):
        density_part(1, i)
        if i == GATE:

            @pl.when(upper == 0)
            def _():
                pl.semaphore_wait(barrier, 3)
                pl.semaphore_signal(group_sem, inc=1, device_id=core_peer, device_id_type=MESH)
                for j in range(GATE):
                    to_core(j).start()

        if i >= GATE:

            @pl.when(upper == 0)
            def _():
                to_core(i).start()

    core_copy.wait()
    for i in range(CHUNKS):
        if i < 2:
            @pl.when(upper == 1)
            def _():
                if i == 0:
                    pl.semaphore_wait(group_sem, 1)
                sum_and_send(i)
        density_part(0, i)

        @pl.when(upper == 1)
        def _():
            to_core(i).start()

    @pl.when(upper == 0)
    def _():
        for m in range(2):
            sum_and_send(m)

    @pl.when(wrapped)
    def _():
        meet_slabs()
        for m in range(2):
            send_edges(m)

    lane = lax.broadcasted_iota(jnp.int32, (1, LANES), 1)
    inner = lane % NY
    low = lane < NY
    row = lax.broadcasted_iota(jnp.int32, (8, LANES), 0)
    own_four = jnp.where(is_low, row, 7 - row) < 4
    own_two = jnp.where(is_low, row, 7 - row) < 2

    tiles = width // LANES

    def at(j):
        return slice(j * LANES, (j + 1) * LANES)

    def total(rows, i):
        to_chip(rows, i).wait_recv()
        dens[rows, shifted(i)] = chip_sum[rows, cols(i)] + from_chip[rows, cols(i)]

    def flows(fields, turned, j):
        centre = fields[j]
        grad_x = along_x(fields[j - 1], turned[j - 1], turned[j], fields[j + 1], turned[j + 1], low)
        grad_y = along_y(centre, turned[j], inner)
        grad_z = along_z(centre)
        sigma = grad_x * grad_x + grad_y * grad_y + grad_z * grad_z
        root = jnp.exp2(jnp.log2(centre) * (-1.0 / 3.0))
        root2 = root * root
        root4 = root2 * root2
        share = 1.0 / (1.0 + u_scale * (sigma * (root4 * root4)))
        flow = flow_scale * (root4 * (share * share))
        d_dens = (slope_scale * (centre * root2)) * (
            (1.0 + kappa) + share * (2.0 * kappa * share - 3.0 * kappa)
        )
        return flow * grad_x, flow * grad_y, flow * grad_z, d_dens

    def first_pass(start, count):
        where = [at(t % n_tiles + 1) for t in range(start - 1, start + count + 1)]
        fields = [jnp.concatenate([dens[:, w], inner_in[:, w]], axis=0) for w in where]
        turned = [swap_halves(f) for f in fields]
        for j in range(1, count + 1):
            part_x, part_y, part_z, d_dens = flows(fields, turned, j)
            part_y = part_y[:half]
            rest = d_dens[:half] - along_y(part_y, swap_halves(part_y), inner)
            flow_x[:, where[j]] = part_x[:half]
            local[:, where[j]] = rest - along_z(part_z)[:half]
            near_rest[:, where[j]] = jnp.where(is_low, rest[:8], rest[8:])
            near_z[:, where[j]] = jnp.where(is_low, part_z[:8], part_z[8:half])

    def second_pass(start, count):
        where = [at(t % n_tiles + 1) for t in range(start - 1, start + count + 1)]
        fields = [jnp.where(own_four, outer[:, w], pltpu.roll(dens[near, w], 4, 0)) for w in where]
        turned = [swap_halves(f) for f in fields]
        for j in range(1, count + 1):
            part_x, part_y, part_z, d_dens = flows(fields, turned, j)
            rest = d_dens - along_y(part_y, swap_halves(part_y), inner)
            rest = jnp.where(own_two, pltpu.roll(rest, 4, 0), near_rest[:, where[j]])
            old_z = near_z[:, where[j]]
            row_z = jnp.where(
                first_rows,
                pltpu.roll(jnp.where(is_low, part_z, old_z), 6, 0),
                pltpu.roll(jnp.where(is_low, old_z, part_z), 2, 0),
            )
            div_z = along_z(row_z)
            div_z = jnp.where(is_low, pltpu.roll(div_z, 6, 0), pltpu.roll(div_z, 2, 0))
            local[near, where[j]] = jnp.where(own_four, rest - div_z, local[near, where[j]])
            flow_x[near, where[j]] = jnp.where(own_two, pltpu.roll(part_x, 4, 0), flow_x[near, where[j]])

    def finish(rows, out_rows, start, count):
        where = [at(t % n_tiles + 1) for t in range(start - 1, start + count + 1)]
        fields = [flow_x[rows, w] for w in where]
        turned = [swap_halves(f) for f in fields]
        for j in range(1, count + 1):
            div_x = along_x(fields[j - 1], turned[j - 1], turned[j], fields[j + 1], turned[j + 1], low)
            pot_ref[out_rows, at((start + j - 1) % n_tiles)] = local[rows, where[j]] - div_x

    def unpack(m):
        for k in range(2):
            from_edge(m, k).wait_recv()
        for t in range(tiles):
            both = edge_in[0, :, at(m * tiles + t)] + edge_in[1, :, at(m * tiles + t)]
            turned = pltpu.roll(both, 4, 0)
            outer[:, at(2 * m * tiles + t + 1)] = jnp.where(first_rows, both, turned)
            outer[:, at((2 * m + 1) * tiles + t + 1)] = jnp.where(first_rows, turned, both)

    for i in range(CHUNKS):
        total(far, i)
        to_inner(i).start()
    for i in range(CHUNKS):
        total(near, i)
        to_inner(i).wait_recv()
        if i == 0:
            first_pass(1, tiles - 2)
        elif i < CHUNKS - 1:
            first_pass(i * tiles - 1, tiles)
        else:
            first_pass(i * tiles - 1, tiles + 2)
    finish(far, far_out, 0, n_tiles)
    to_pot_far().start()
    unpack(0)
    second_pass(1, 2 * tiles - 2)
    finish(near, near_out, *PARTS[0])
    to_pot(0).start()
    unpack(1)
    second_pass(2 * tiles - 1, 2 * tiles + 2)
    for i in (1, 2):
        finish(near, near_out, *PARTS[i])
        to_pot(i).start()
    for i in range(len(PARTS)):
        to_pot(i).wait_recv()
    to_pot_far().wait_recv()
    for k in range(2):
        remote(part, part, sent.at[k], edge_recv.at[0], core_peer).wait_send()


def apply_kernel(held_ref, pot_ref, applied_ref, out_ref, staged, store_sem, pot_sem):
    s_dev, planes, cells = held_ref.shape
    width = cells // STORES
    pot_copy = pltpu.make_async_copy(pot_ref, out_ref, pot_sem)
    pot_copy.start()

    def store(i):
        cols = pl.ds(i * width, width)
        return pltpu.make_async_copy(staged.at[:, :, cols], applied_ref.at[:, :, cols], store_sem.at[i])

    for i in range(STORES):
        cols = pl.ds(i * width, width)
        pot = pot_ref[:, cols].astype(jnp.bfloat16)

        def state_step(s, carry):
            staged[s, :, cols] = held_ref[s, :, cols] * pot
            return carry

        lax.fori_loop(0, s_dev, state_step, 0, unroll=8)
        store(i).start()
    for i in range(STORES):
        store(i).wait()
    pot_copy.wait()


def body(slabs, states, core_density, occupancy):
    s_dev, planes, cells = states.shape
    half = planes // 2
    vmem = pl.BlockSpec(memory_space=pltpu.VMEM)
    hbm = pl.BlockSpec(memory_space=pltpu.HBM)
    states = pltpu.with_memory_space_constraint(states, pltpu.HBM)
    core_density = pltpu.with_memory_space_constraint(core_density, pltpu.HBM)
    occupancy = pltpu.with_memory_space_constraint(occupancy, pltpu.HBM)

    def rows(count):
        return pltpu.VMEM((count, cells), jnp.float32)

    def wide(count):
        return pltpu.VMEM((count, cells + 2 * LANES), jnp.float32)

    def sems(count):
        return pltpu.SemaphoreType.DMA((count,))

    held, pot = pl.pallas_call(
        functools.partial(potential_kernel, slabs),
        out_shape=(
            pltpu.VMEM((s_dev, planes, cells), jnp.bfloat16),
            pltpu.VMEM((planes, cells), jnp.float32),
        ),
        in_specs=[hbm, hbm, hbm],
        out_specs=(vmem, vmem),
        scratch_shapes=[
            pltpu.SMEM((s_dev,), jnp.int32),
            pltpu.VMEM((2, half, cells), jnp.float32),
            rows(half),
            rows(half),
            rows(half),
            rows(half),
            wide(half),
            wide(8),
            pltpu.VMEM((8, cells // 2), jnp.float32),
            pltpu.VMEM((2, 8, cells // 2), jnp.float32),
            wide(8),
            wide(half),
            wide(half),
            wide(8),
            wide(8),
            sems(2 * LOADS),
            sems(2),
            pltpu.SemaphoreType.REGULAR,
            pltpu.SemaphoreType.REGULAR,
        ]
        + [sems(2), sems(CHUNKS), sems(2 * CHUNKS), sems(CHUNKS), sems(4), sems(len(PARTS) + 1)],
        compiler_params=pltpu.CompilerParams(
            collective_id=0, has_side_effects=True, vmem_limit_bytes=24 * 1024 * 1024
        ),
        name="potential",
    )(occupancy, states, core_density)
    return pl.pallas_call(
        apply_kernel,
        out_shape=(
            jax.ShapeDtypeStruct((s_dev, planes, cells), jnp.bfloat16),
            jax.ShapeDtypeStruct((planes, cells), jnp.float32),
        ),
        in_specs=[vmem, vmem],
        out_specs=(hbm, hbm),
        scratch_shapes=[
            pltpu.VMEM((s_dev, planes, cells), jnp.bfloat16),
            sems(STORES),
            pltpu.SemaphoreType.DMA,
        ],
        compiler_params=pltpu.CompilerParams(vmem_limit_bytes=32 * 1024 * 1024),
        name="apply",
    )(held, pot)


def solution(mesh):
    placed = (P("grp", "slab", None), P("slab", None), P("grp"))
    return jax.shard_map(
        functools.partial(body, mesh.shape["slab"]),
        mesh=mesh,
        in_specs=placed,
        out_specs=(P("grp", "slab", None), P("slab", None)),
        check_vma=False,
    )
```

```python
import functools
import math

import jax
import jax.numpy as jnp
from jax import lax
from jax.experimental import pallas as pl
from jax.experimental.pallas import tpu as pltpu
from jax.sharding import PartitionSpec as P

MESH = pl.DeviceIdType.MESH

NX = 64
NY = 64
OCC_DEN = 8
LANES = 128

grid_step = 0.5
valence_norm = 0.04

kappa = 0.804
mu = 0.2195149727645171
exchange = -0.75 * (3.0 / math.pi) ** (1.0 / 3.0)
reduced_scale = 4.0 * (3.0 * math.pi**2) ** (2.0 / 3.0)
stencil_scale = 1.0 / (12.0 * grid_step)
u_scale = mu / kappa / reduced_scale * stencil_scale * stencil_scale
flow_scale = 2.0 * exchange * mu / reduced_scale * stencil_scale * stencil_scale
slope_scale = exchange * 4.0 / 3.0

CHUNKS = 4
STEP = 4 * LANES
LOADS = 8
GATE = 1
PARTS = ((2, 12), (14, 18), (0, 2))
STORES = 8


def stencil(before2, before1, after1, after2):
    return (before2 - after2) + 8.0 * (after1 - before1)


def swap_halves(tile):
    return pltpu.roll(tile, 64, 1)


def along_y(tile, swapped, inner):
    before2 = pltpu.roll(jnp.where(inner >= NY - 2, swapped, tile), 2, 1)
    before1 = pltpu.roll(jnp.where(inner >= NY - 1, swapped, tile), 1, 1)
    after1 = pltpu.roll(jnp.where(inner < 1, swapped, tile), LANES - 1, 1)
    after2 = pltpu.roll(jnp.where(inner < 2, swapped, tile), LANES - 2, 1)
    return stencil(before2, before1, after1, after2)


def along_x(left, left_swapped, swapped, right, right_swapped, low):
    before1 = jnp.where(low, left_swapped, swapped)
    after1 = jnp.where(low, swapped, right_swapped)
    return stencil(left, before1, after1, right)


def along_z(tile):
    rows = tile.shape[0]
    return stencil(
        pltpu.roll(tile, 2, 0),
        pltpu.roll(tile, 1, 0),
        pltpu.roll(tile, rows - 1, 0),
        pltpu.roll(tile, rows - 2, 0),
    )


def potential_kernel(
    slabs,
    occ_hbm,
    states_ref,
    core_ref,
    held_ref,
    pot_ref,
    occ_ref,
    part,
    from_core,
    chip_sum,
    from_chip,
    core_half,
    dens,
    inner_in,
    edge_out,
    edge_in,
    outer,
    flow_x,
    local,
    near_rest,
    near_z,
    load_sem,
    misc_sem,
    group_sem,
    slab_sem,
    sent,
    core_recv,
    chip_recv,
    inner_recv,
    edge_recv,
    pot_recv,
):
    s_dev, planes, cells = states_ref.shape
    half = planes // 2
    width = cells // CHUNKS
    n_tiles = cells // LANES

    grp = lax.axis_index("grp")
    slab = lax.axis_index("slab")
    chip = grp // 2
    upper = 1 - grp % 2
    core_peer = {"grp": chip * 2 + upper, "slab": slab}
    chip_peer = {"grp": (1 - chip) * 2 + 1 - upper, "slab": slab}
    cross_peer = {"grp": (1 - chip) * 2 + upper, "slab": slab}
    beyond = (slab + slabs - 1 + 2 * upper) % slabs
    wrapped = slab % 8 == 0
    rushed = (slab % 8 == 7) & (upper == 1)
    edge_chips = (0, 1)

    near = pl.ds(pl.multiple_of(upper * 8, 8), 8)
    far = pl.ds(pl.multiple_of((1 - upper) * 8, 8), 8)

    def cols(i):
        return pl.ds(pl.multiple_of(i * width, LANES), width)

    def load(h, i):
        where = (slice(None), pl.ds(h * half, half), pl.ds(pl.multiple_of(i * STEP, STEP), STEP))
        return pltpu.make_async_copy(states_ref.at[where], held_ref.at[where], load_sem.at[h * LOADS + i])

    def remote(src, dst, send, recv, peer):
        return pltpu.make_async_remote_copy(
            src_ref=src, dst_ref=dst, send_sem=send, recv_sem=recv, device_id=peer, device_id_type=MESH
        )

    def to_core(i):
        return remote(
            part.at[1 - upper, :, cols(i)], from_core.at[:, cols(i)], sent.at[0], core_recv.at[i], core_peer
        )

    def to_chip(rows, i):
        tile_at = (rows, cols(i))
        which = i + CHUNKS * (rows is near)
        return remote(chip_sum.at[tile_at], from_chip.at[tile_at], sent.at[0], chip_recv.at[which], chip_peer)

    def edge_cols(m):
        return slice(m * width, (m + 1) * width)

    def to_edge(m, k):
        peer = {"grp": edge_chips[k] * 2 + upper, "slab": beyond}
        out = edge_out.at[:, edge_cols(m)]
        return remote(out, edge_in.at[chip, :, edge_cols(m)], sent.at[1], edge_recv.at[2 * m + chip], peer)

    def from_edge(m, k):
        out = edge_out.at[:, edge_cols(m)]
        return remote(out, edge_in.at[k, :, edge_cols(m)], sent.at[1], edge_recv.at[2 * m + k], core_peer)

    def shifted(i):
        return pl.ds(pl.multiple_of(i * width + LANES, LANES), width)

    def to_inner(i):
        return remote(
            dens.at[far, shifted(i)], inner_in.at[:, shifted(i)], sent.at[1], inner_recv.at[i], core_peer
        )

    def own_rows():
        return pl.ds(pl.multiple_of(upper * half, half), half)

    near_out = pl.ds(pl.multiple_of(upper * 24, 8), 8)
    far_out = pl.ds(pl.multiple_of(8 + upper * 8, 8), 8)

    def to_pot(i):
        start, count = PARTS[i]
        where = pot_ref.at[near_out, pl.ds(start * LANES, count * LANES)]
        return remote(where, where, sent.at[1], pot_recv.at[i], core_peer)

    def to_pot_far():
        where = pot_ref.at[far_out, :]
        return remote(where, where, sent.at[1], pot_recv.at[len(PARTS)], core_peer)

    barrier = pltpu.get_barrier_semaphore()

    def greet(peer):
        pl.semaphore_signal(barrier, inc=1, device_id=peer, device_id_type=MESH)

    @pl.when(upper == 0)
    def _():
        greet(chip_peer)
        greet({"grp": 0, "slab": beyond})
        greet({"grp": 2, "slab": beyond})

    @pl.when(upper == 1)
    def _():
        greet(core_peer)
        greet(cross_peer)
        greet({"grp": 0, "slab": beyond})
        greet({"grp": 2, "slab": beyond})

    occ_copy = pltpu.make_async_copy(occ_hbm, occ_ref, misc_sem.at[0])
    occ_copy.start()
    for i in range(LOADS):
        load(1, i).start()
    core_copy = pltpu.make_async_copy(core_ref.at[own_rows(), :], core_half, misc_sem.at[1])
    core_copy.start()
    for i in range(LOADS):
        load(0, i).start()

    occ_copy.wait()
    weights = [
        occ_ref[s].astype(jnp.float32) * (valence_norm / (OCC_DEN * s_dev * 4))
        for s in range(s_dev)
    ]

    def density_part(h, i):
        def tile_step(t, carry):
            load(h, i * (width // STEP) + t).wait()
            lanes = pl.ds(pl.multiple_of(i * width + t * STEP, STEP), STEP)
            total = jnp.zeros((half, STEP), jnp.float32)
            for s in range(s_dev):
                wide = held_ref[s, h * half : (h + 1) * half, lanes].astype(jnp.float32)
                total = total + (wide * weights[s]) * wide
            part[h, :, lanes] = total
            return carry

        lax.fori_loop(0, width // STEP, tile_step, 0)

    first_rows = lax.broadcasted_iota(jnp.int32, (8, LANES), 0) < 4
    with_core = (1 - chip).astype(jnp.float32)
    is_low = upper == 0

    def sum_chip(i):
        to_core(i).wait_recv()
        chip_sum[:, cols(i)] = (part[upper, :, cols(i)] + from_core[:, cols(i)]) + with_core * core_half[:, cols(i)]

    def pack(m):
        edge_rows = pl.ds(pl.multiple_of(upper * 8, 8), 8)
        for t in range(width // LANES):
            here = 2 * m * width + t * LANES
            front = chip_sum[edge_rows, here : here + LANES]
            back = chip_sum[edge_rows, here + width : here + width + LANES]
            front_turned, back_turned = pltpu.roll(front, 4, 0), pltpu.roll(back, 4, 0)
            low_edge = jnp.where(first_rows, front, back_turned)
            high_edge = jnp.where(first_rows, front_turned, back)
            edge_out[:, m * width + t * LANES : m * width + (t + 1) * LANES] = jnp.where(is_low, low_edge, high_edge)

    def send_edges(m):
        for k in range(2):
            to_edge(m, k).start()

    def meet_slabs():
        @pl.when(upper == 1)
        def _():
            pl.semaphore_wait(barrier, 4)
            pl.semaphore_signal(slab_sem, inc=1, device_id=core_peer, device_id_type=MESH)

        @pl.when(upper == 0)
        def _():
            pl.semaphore_wait(slab_sem, 1)

    def sum_and_send(m):
        for i in (2 * m, 2 * m + 1):
            sum_chip(i)
        pack(m)

        @pl.when(jnp.logical_not(wrapped))
        def _():
            if m == 0:
                meet_slabs()
            send_edges(m)

        @pl.when(jnp.logical_not(rushed))
        def _():
            for i in (2 * m, 2 * m + 1):
                to_chip(far, i).start()

        if m == 1:

            @pl.when(rushed)
            def _():
                for i in range(CHUNKS):
                    to_chip(far, i).start()

            for i in range(CHUNKS):
                to_chip(near, i).start()

    for i in range(CHUNKS):
        density_part(1, i)
        if i == GATE:

            @pl.when(upper == 0)
            def _():
                pl.semaphore_wait(barrier, 3)
                pl.semaphore_signal(group_sem, inc=1, device_id=core_peer, device_id_type=MESH)
                for j in range(GATE):
                    to_core(j).start()

        if i >= GATE:

            @pl.when(upper == 0)
            def _():
                to_core(i).start()

    core_copy.wait()
    for i in range(CHUNKS):
        if i == 0:
            @pl.when(upper == 1)
            def _():
                pl.semaphore_wait(group_sem, 1)
                for m in range(2):
                    sum_and_send(m)
        density_part(0, i)

        @pl.when(upper == 1)
        def _():
            to_core(i).start()

    @pl.when(upper == 0)
    def _():
        for m in range(2):
            sum_and_send(m)

    @pl.when(wrapped)
    def _():
        meet_slabs()
        for m in range(2):
            send_edges(m)

    lane = lax.broadcasted_iota(jnp.int32, (1, LANES), 1)
    inner = lane % NY
    low = lane < NY
    row = lax.broadcasted_iota(jnp.int32, (8, LANES), 0)
    own_four = jnp.where(is_low, row, 7 - row) < 4
    own_two = jnp.where(is_low, row, 7 - row) < 2

    tiles = width // LANES

    def at(j):
        return slice(j * LANES, (j + 1) * LANES)

    def total(rows, i):
        to_chip(rows, i).wait_recv()
        dens[rows, shifted(i)] = chip_sum[rows, cols(i)] + from_chip[rows, cols(i)]

    def flows(fields, turned, j):
        centre = fields[j]
        grad_x = along_x(fields[j - 1], turned[j - 1], turned[j], fields[j + 1], turned[j + 1], low)
        grad_y = along_y(centre, turned[j], inner)
        grad_z = along_z(centre)
        sigma = grad_x * grad_x + grad_y * grad_y + grad_z * grad_z
        root = jnp.exp2(jnp.log2(centre) * (-1.0 / 3.0))
        root2 = root * root
        root4 = root2 * root2
        share = 1.0 / (1.0 + u_scale * (sigma * (root4 * root4)))
        flow = flow_scale * (root4 * (share * share))
        d_dens = (slope_scale * (centre * root2)) * (
            (1.0 + kappa) + share * (2.0 * kappa * share - 3.0 * kappa)
        )
        return flow * grad_x, flow * grad_y, flow * grad_z, d_dens

    def first_pass(start, count):
        where = [at(t % n_tiles + 1) for t in range(start - 1, start + count + 1)]
        fields = [jnp.concatenate([dens[:, w], inner_in[:, w]], axis=0) for w in where]
        turned = [swap_halves(f) for f in fields]
        for j in range(1, count + 1):
            part_x, part_y, part_z, d_dens = flows(fields, turned, j)
            part_y = part_y[:half]
            rest = d_dens[:half] - along_y(part_y, swap_halves(part_y), inner)
            flow_x[:, where[j]] = part_x[:half]
            local[:, where[j]] = rest - along_z(part_z)[:half]
            near_rest[:, where[j]] = jnp.where(is_low, rest[:8], rest[8:])
            near_z[:, where[j]] = jnp.where(is_low, part_z[:8], part_z[8:half])

    def second_pass(start, count):
        where = [at(t % n_tiles + 1) for t in range(start - 1, start + count + 1)]
        fields = [jnp.where(own_four, outer[:, w], pltpu.roll(dens[near, w], 4, 0)) for w in where]
        turned = [swap_halves(f) for f in fields]
        for j in range(1, count + 1):
            part_x, part_y, part_z, d_dens = flows(fields, turned, j)
            rest = d_dens - along_y(part_y, swap_halves(part_y), inner)
            rest = jnp.where(own_two, pltpu.roll(rest, 4, 0), near_rest[:, where[j]])
            old_z = near_z[:, where[j]]
            row_z = jnp.where(
                first_rows,
                pltpu.roll(jnp.where(is_low, part_z, old_z), 6, 0),
                pltpu.roll(jnp.where(is_low, old_z, part_z), 2, 0),
            )
            div_z = along_z(row_z)
            div_z = jnp.where(is_low, pltpu.roll(div_z, 6, 0), pltpu.roll(div_z, 2, 0))
            local[near, where[j]] = jnp.where(own_four, rest - div_z, local[near, where[j]])
            flow_x[near, where[j]] = jnp.where(own_two, pltpu.roll(part_x, 4, 0), flow_x[near, where[j]])

    def finish(rows, out_rows, start, count):
        where = [at(t % n_tiles + 1) for t in range(start - 1, start + count + 1)]
        fields = [flow_x[rows, w] for w in where]
        turned = [swap_halves(f) for f in fields]
        for j in range(1, count + 1):
            div_x = along_x(fields[j - 1], turned[j - 1], turned[j], fields[j + 1], turned[j + 1], low)
            pot_ref[out_rows, at((start + j - 1) % n_tiles)] = local[rows, where[j]] - div_x

    def unpack(m):
        for k in range(2):
            from_edge(m, k).wait_recv()
        for t in range(tiles):
            both = edge_in[0, :, at(m * tiles + t)] + edge_in[1, :, at(m * tiles + t)]
            turned = pltpu.roll(both, 4, 0)
            outer[:, at(2 * m * tiles + t + 1)] = jnp.where(first_rows, both, turned)
            outer[:, at((2 * m + 1) * tiles + t + 1)] = jnp.where(first_rows, turned, both)

    for i in range(CHUNKS):
        total(far, i)
        to_inner(i).start()
    for i in range(CHUNKS):
        total(near, i)
        to_inner(i).wait_recv()
        if i == 0:
            first_pass(1, tiles - 2)
        elif i < CHUNKS - 1:
            first_pass(i * tiles - 1, tiles)
        else:
            first_pass(i * tiles - 1, tiles + 2)
    finish(far, far_out, 0, n_tiles)
    to_pot_far().start()
    unpack(0)
    second_pass(1, 2 * tiles - 2)
    finish(near, near_out, *PARTS[0])
    to_pot(0).start()
    unpack(1)
    second_pass(2 * tiles - 1, 2 * tiles + 2)
    for i in (1, 2):
        finish(near, near_out, *PARTS[i])
        to_pot(i).start()
    for i in range(len(PARTS)):
        to_pot(i).wait_recv()
    to_pot_far().wait_recv()
    for k in range(2):
        remote(part, part, sent.at[k], edge_recv.at[0], core_peer).wait_send()


def apply_kernel(held_ref, pot_ref, applied_ref, out_ref, staged, store_sem, pot_sem):
    s_dev, planes, cells = held_ref.shape
    width = cells // STORES
    pot_copy = pltpu.make_async_copy(pot_ref, out_ref, pot_sem)
    pot_copy.start()

    def store(i):
        cols = pl.ds(i * width, width)
        return pltpu.make_async_copy(staged.at[:, :, cols], applied_ref.at[:, :, cols], store_sem.at[i])

    for i in range(STORES):
        cols = pl.ds(i * width, width)
        pot = pot_ref[:, cols].astype(jnp.bfloat16)

        def state_step(s, carry):
            staged[s, :, cols] = held_ref[s, :, cols] * pot
            return carry

        lax.fori_loop(0, s_dev, state_step, 0, unroll=8)
        store(i).start()
    for i in range(STORES):
        store(i).wait()
    pot_copy.wait()


def body(slabs, states, core_density, occupancy):
    s_dev, planes, cells = states.shape
    half = planes // 2
    vmem = pl.BlockSpec(memory_space=pltpu.VMEM)
    hbm = pl.BlockSpec(memory_space=pltpu.HBM)
    states = pltpu.with_memory_space_constraint(states, pltpu.HBM)
    core_density = pltpu.with_memory_space_constraint(core_density, pltpu.HBM)
    occupancy = pltpu.with_memory_space_constraint(occupancy, pltpu.HBM)

    def rows(count):
        return pltpu.VMEM((count, cells), jnp.float32)

    def wide(count):
        return pltpu.VMEM((count, cells + 2 * LANES), jnp.float32)

    def sems(count):
        return pltpu.SemaphoreType.DMA((count,))

    held, pot = pl.pallas_call(
        functools.partial(potential_kernel, slabs),
        out_shape=(
            pltpu.VMEM((s_dev, planes, cells), jnp.bfloat16),
            pltpu.VMEM((planes, cells), jnp.float32),
        ),
        in_specs=[hbm, hbm, hbm],
        out_specs=(vmem, vmem),
        scratch_shapes=[
            pltpu.SMEM((s_dev,), jnp.int32),
            pltpu.VMEM((2, half, cells), jnp.float32),
            rows(half),
            rows(half),
            rows(half),
            rows(half),
            wide(half),
            wide(8),
            pltpu.VMEM((8, cells // 2), jnp.float32),
            pltpu.VMEM((2, 8, cells // 2), jnp.float32),
            wide(8),
            wide(half),
            wide(half),
            wide(8),
            wide(8),
            sems(2 * LOADS),
            sems(2),
            pltpu.SemaphoreType.REGULAR,
            pltpu.SemaphoreType.REGULAR,
        ]
        + [sems(2), sems(CHUNKS), sems(2 * CHUNKS), sems(CHUNKS), sems(4), sems(len(PARTS) + 1)],
        compiler_params=pltpu.CompilerParams(
            collective_id=0, has_side_effects=True, vmem_limit_bytes=24 * 1024 * 1024
        ),
        name="potential",
    )(occupancy, states, core_density)
    return pl.pallas_call(
        apply_kernel,
        out_shape=(
            jax.ShapeDtypeStruct((s_dev, planes, cells), jnp.bfloat16),
            jax.ShapeDtypeStruct((planes, cells), jnp.float32),
        ),
        in_specs=[vmem, vmem],
        out_specs=(hbm, hbm),
        scratch_shapes=[
            pltpu.VMEM((s_dev, planes, cells), jnp.bfloat16),
            sems(STORES),
            pltpu.SemaphoreType.DMA,
        ],
        compiler_params=pltpu.CompilerParams(vmem_limit_bytes=32 * 1024 * 1024),
        name="apply",
    )(held, pot)


def solution(mesh):
    placed = (P("grp", "slab", None), P("slab", None), P("grp"))
    return jax.shard_map(
        functools.partial(body, mesh.shape["slab"]),
        mesh=mesh,
        in_specs=placed,
        out_specs=(P("grp", "slab", None), P("slab", None)),
        check_vma=False,
    )
```

```python
import functools
import math

import jax
import jax.numpy as jnp
from jax import lax
from jax.experimental import pallas as pl
from jax.experimental.pallas import tpu as pltpu
from jax.sharding import PartitionSpec as P

MESH = pl.DeviceIdType.MESH

NX = 64
NY = 64
OCC_DEN = 8
LANES = 128

grid_step = 0.5
valence_norm = 0.04

kappa = 0.804
mu = 0.2195149727645171
exchange = -0.75 * (3.0 / math.pi) ** (1.0 / 3.0)
reduced_scale = 4.0 * (3.0 * math.pi**2) ** (2.0 / 3.0)
stencil_scale = 1.0 / (12.0 * grid_step)
u_scale = mu / kappa / reduced_scale * stencil_scale * stencil_scale
flow_scale = 2.0 * exchange * mu / reduced_scale * stencil_scale * stencil_scale
slope_scale = exchange * 4.0 / 3.0

CHUNKS = 4
STEP = 4 * LANES
LOADS = 8
GATE = 1
PARTS = ((2, 12), (14, 18), (0, 2))
STORES = 8


def stencil(before2, before1, after1, after2):
    return (before2 - after2) + 8.0 * (after1 - before1)


def swap_halves(tile):
    return pltpu.roll(tile, 64, 1)


def along_y(tile, swapped, inner):
    before2 = pltpu.roll(jnp.where(inner >= NY - 2, swapped, tile), 2, 1)
    before1 = pltpu.roll(jnp.where(inner >= NY - 1, swapped, tile), 1, 1)
    after1 = pltpu.roll(jnp.where(inner < 1, swapped, tile), LANES - 1, 1)
    after2 = pltpu.roll(jnp.where(inner < 2, swapped, tile), LANES - 2, 1)
    return stencil(before2, before1, after1, after2)


def along_x(left, left_swapped, swapped, right, right_swapped, low):
    before1 = jnp.where(low, left_swapped, swapped)
    after1 = jnp.where(low, swapped, right_swapped)
    return stencil(left, before1, after1, right)


def along_z(tile):
    rows = tile.shape[0]
    return stencil(
        pltpu.roll(tile, 2, 0),
        pltpu.roll(tile, 1, 0),
        pltpu.roll(tile, rows - 1, 0),
        pltpu.roll(tile, rows - 2, 0),
    )


def potential_kernel(
    slabs,
    occ_hbm,
    states_ref,
    core_ref,
    held_ref,
    pot_ref,
    occ_ref,
    part,
    from_core,
    chip_sum,
    from_chip,
    core_half,
    dens,
    inner_in,
    edge_out,
    edge_in,
    outer,
    flow_x,
    local,
    near_rest,
    near_z,
    load_sem,
    misc_sem,
    group_sem,
    slab_sem,
    sent,
    core_recv,
    chip_recv,
    inner_recv,
    edge_recv,
    pot_recv,
):
    s_dev, planes, cells = states_ref.shape
    half = planes // 2
    width = cells // CHUNKS
    n_tiles = cells // LANES

    grp = lax.axis_index("grp")
    slab = lax.axis_index("slab")
    chip = grp // 2
    upper = 1 - grp % 2
    core_peer = {"grp": chip * 2 + upper, "slab": slab}
    chip_peer = {"grp": (1 - chip) * 2 + 1 - upper, "slab": slab}
    cross_peer = {"grp": (1 - chip) * 2 + upper, "slab": slab}
    beyond = (slab + slabs - 1 + 2 * upper) % slabs
    wrapped = slab % 8 == 0
    rushed = (slab % 8 == 7) & (upper == 1)
    edge_chips = (0, 1)

    near = pl.ds(pl.multiple_of(upper * 8, 8), 8)
    far = pl.ds(pl.multiple_of((1 - upper) * 8, 8), 8)

    def cols(i):
        return pl.ds(pl.multiple_of(i * width, LANES), width)

    def load(h, i):
        span = STEP if h == 1 else width
        where = (slice(None), pl.ds(h * half, half), pl.ds(pl.multiple_of(i * span, STEP), span))
        return pltpu.make_async_copy(states_ref.at[where], held_ref.at[where], load_sem.at[h * CHUNKS + i])

    def remote(src, dst, send, recv, peer):
        return pltpu.make_async_remote_copy(
            src_ref=src, dst_ref=dst, send_sem=send, recv_sem=recv, device_id=peer, device_id_type=MESH
        )

    def to_core(i):
        return remote(
            part.at[1 - upper, :, cols(i)], from_core.at[:, cols(i)], sent.at[0], core_recv.at[i], core_peer
        )

    def to_chip(rows, i):
        tile_at = (rows, cols(i))
        which = i + CHUNKS * (rows is near)
        return remote(chip_sum.at[tile_at], from_chip.at[tile_at], sent.at[0], chip_recv.at[which], chip_peer)

    def edge_cols(m):
        return slice(m * width, (m + 1) * width)

    def to_edge(m, k):
        peer = {"grp": edge_chips[k] * 2 + upper, "slab": beyond}
        out = edge_out.at[:, edge_cols(m)]
        return remote(out, edge_in.at[chip, :, edge_cols(m)], sent.at[1], edge_recv.at[2 * m + chip], peer)

    def from_edge(m, k):
        out = edge_out.at[:, edge_cols(m)]
        return remote(out, edge_in.at[k, :, edge_cols(m)], sent.at[1], edge_recv.at[2 * m + k], core_peer)

    def shifted(i):
        return pl.ds(pl.multiple_of(i * width + LANES, LANES), width)

    def to_inner(i):
        return remote(
            dens.at[far, shifted(i)], inner_in.at[:, shifted(i)], sent.at[1], inner_recv.at[i], core_peer
        )

    def own_rows():
        return pl.ds(pl.multiple_of(upper * half, half), half)

    near_out = pl.ds(pl.multiple_of(upper * 24, 8), 8)
    far_out = pl.ds(pl.multiple_of(8 + upper * 8, 8), 8)

    def to_pot(i):
        start, count = PARTS[i]
        where = pot_ref.at[near_out, pl.ds(start * LANES, count * LANES)]
        return remote(where, where, sent.at[1], pot_recv.at[i], core_peer)

    def to_pot_far():
        where = pot_ref.at[far_out, :]
        return remote(where, where, sent.at[1], pot_recv.at[len(PARTS)], core_peer)

    barrier = pltpu.get_barrier_semaphore()

    def greet(peer):
        pl.semaphore_signal(barrier, inc=1, device_id=peer, device_id_type=MESH)

    @pl.when(upper == 0)
    def _():
        greet(chip_peer)
        greet({"grp": 0, "slab": beyond})
        greet({"grp": 2, "slab": beyond})

    @pl.when(upper == 1)
    def _():
        greet(core_peer)
        greet(cross_peer)
        greet({"grp": 0, "slab": beyond})
        greet({"grp": 2, "slab": beyond})

    occ_copy = pltpu.make_async_copy(occ_hbm, occ_ref, misc_sem.at[0])
    occ_copy.start()
    for i in range(LOADS):
        load(1, i).start()
    core_copy = pltpu.make_async_copy(core_ref.at[own_rows(), :], core_half, misc_sem.at[1])
    core_copy.start()
    for i in range(CHUNKS):
        load(0, i).start()

    occ_copy.wait()
    weights = [
        occ_ref[s].astype(jnp.float32) * (valence_norm / (OCC_DEN * s_dev * 4))
        for s in range(s_dev)
    ]

    def density_part(h, i):
        if h == 0:
            load(0, i).wait()

        def tile_step(t, carry):
            if h == 1:
                load(1, i * (width // STEP) + t).wait()
            lanes = pl.ds(pl.multiple_of(i * width + t * STEP, STEP), STEP)
            total = jnp.zeros((half, STEP), jnp.float32)
            for s in range(s_dev):
                wide = held_ref[s, h * half : (h + 1) * half, lanes].astype(jnp.float32)
                total = total + (wide * weights[s]) * wide
            part[h, :, lanes] = total
            return carry

        lax.fori_loop(0, width // STEP, tile_step, 0)

    first_rows = lax.broadcasted_iota(jnp.int32, (8, LANES), 0) < 4
    with_core = (1 - chip).astype(jnp.float32)
    is_low = upper == 0

    def sum_chip(i):
        to_core(i).wait_recv()
        chip_sum[:, cols(i)] = (part[upper, :, cols(i)] + from_core[:, cols(i)]) + with_core * core_half[:, cols(i)]

    def pack(m):
        edge_rows = pl.ds(pl.multiple_of(upper * 8, 8), 8)
        for t in range(width // LANES):
            here = 2 * m * width + t * LANES
            front = chip_sum[edge_rows, here : here + LANES]
            back = chip_sum[edge_rows, here + width : here + width + LANES]
            front_turned, back_turned = pltpu.roll(front, 4, 0), pltpu.roll(back, 4, 0)
            low_edge = jnp.where(first_rows, front, back_turned)
            high_edge = jnp.where(first_rows, front_turned, back)
            edge_out[:, m * width + t * LANES : m * width + (t + 1) * LANES] = jnp.where(is_low, low_edge, high_edge)

    def send_edges(m):
        for k in range(2):
            to_edge(m, k).start()

    def meet_slabs():
        @pl.when(upper == 1)
        def _():
            pl.semaphore_wait(barrier, 4)
            pl.semaphore_signal(slab_sem, inc=1, device_id=core_peer, device_id_type=MESH)

        @pl.when(upper == 0)
        def _():
            pl.semaphore_wait(slab_sem, 1)

    def sum_and_send(m):
        for i in (2 * m, 2 * m + 1):
            sum_chip(i)
        pack(m)

        @pl.when(jnp.logical_not(wrapped))
        def _():
            if m == 0:
                meet_slabs()
            send_edges(m)

        @pl.when(jnp.logical_not(rushed))
        def _():
            for i in (2 * m, 2 * m + 1):
                to_chip(far, i).start()

        if m == 1:

            @pl.when(rushed)
            def _():
                for i in range(CHUNKS):
                    to_chip(far, i).start()

            for i in range(CHUNKS):
                to_chip(near, i).start()

    for i in range(CHUNKS):
        density_part(1, i)
        if i == GATE:

            @pl.when(upper == 0)
            def _():
                pl.semaphore_wait(barrier, 3)
                pl.semaphore_signal(group_sem, inc=1, device_id=core_peer, device_id_type=MESH)
                for j in range(GATE):
                    to_core(j).start()

        if i >= GATE:

            @pl.when(upper == 0)
            def _():
                to_core(i).start()

    core_copy.wait()
    for i in range(CHUNKS):
        if i == 0:
            @pl.when(upper == 1)
            def _():
                pl.semaphore_wait(group_sem, 1)
                for m in range(2):
                    sum_and_send(m)
        density_part(0, i)

        @pl.when(upper == 1)
        def _():
            to_core(i).start()

    @pl.when(upper == 0)
    def _():
        for m in range(2):
            sum_and_send(m)

    @pl.when(wrapped)
    def _():
        meet_slabs()
        for m in range(2):
            send_edges(m)

    lane = lax.broadcasted_iota(jnp.int32, (1, LANES), 1)
    inner = lane % NY
    low = lane < NY
    row = lax.broadcasted_iota(jnp.int32, (8, LANES), 0)
    own_four = jnp.where(is_low, row, 7 - row) < 4
    own_two = jnp.where(is_low, row, 7 - row) < 2

    tiles = width // LANES

    def at(j):
        return slice(j * LANES, (j + 1) * LANES)

    def total(rows, i):
        to_chip(rows, i).wait_recv()
        dens[rows, shifted(i)] = chip_sum[rows, cols(i)] + from_chip[rows, cols(i)]

    def flows(fields, turned, j):
        centre = fields[j]
        grad_x = along_x(fields[j - 1], turned[j - 1], turned[j], fields[j + 1], turned[j + 1], low)
        grad_y = along_y(centre, turned[j], inner)
        grad_z = along_z(centre)
        sigma = grad_x * grad_x + grad_y * grad_y + grad_z * grad_z
        root = jnp.exp2(jnp.log2(centre) * (-1.0 / 3.0))
        root2 = root * root
        root4 = root2 * root2
        share = 1.0 / (1.0 + u_scale * (sigma * (root4 * root4)))
        flow = flow_scale * (root4 * (share * share))
        d_dens = (slope_scale * (centre * root2)) * (
            (1.0 + kappa) + share * (2.0 * kappa * share - 3.0 * kappa)
        )
        return flow * grad_x, flow * grad_y, flow * grad_z, d_dens

    def first_pass(start, count):
        where = [at(t % n_tiles + 1) for t in range(start - 1, start + count + 1)]
        fields = [jnp.concatenate([dens[:, w], inner_in[:, w]], axis=0) for w in where]
        turned = [swap_halves(f) for f in fields]
        for j in range(1, count + 1):
            part_x, part_y, part_z, d_dens = flows(fields, turned, j)
            part_y = part_y[:half]
            rest = d_dens[:half] - along_y(part_y, swap_halves(part_y), inner)
            flow_x[:, where[j]] = part_x[:half]
            local[:, where[j]] = rest - along_z(part_z)[:half]
            near_rest[:, where[j]] = jnp.where(is_low, rest[:8], rest[8:])
            near_z[:, where[j]] = jnp.where(is_low, part_z[:8], part_z[8:half])

    def second_pass(start, count):
        where = [at(t % n_tiles + 1) for t in range(start - 1, start + count + 1)]
        fields = [jnp.where(own_four, outer[:, w], pltpu.roll(dens[near, w], 4, 0)) for w in where]
        turned = [swap_halves(f) for f in fields]
        for j in range(1, count + 1):
            part_x, part_y, part_z, d_dens = flows(fields, turned, j)
            rest = d_dens - along_y(part_y, swap_halves(part_y), inner)
            rest = jnp.where(own_two, pltpu.roll(rest, 4, 0), near_rest[:, where[j]])
            old_z = near_z[:, where[j]]
            row_z = jnp.where(
                first_rows,
                pltpu.roll(jnp.where(is_low, part_z, old_z), 6, 0),
                pltpu.roll(jnp.where(is_low, old_z, part_z), 2, 0),
            )
            div_z = along_z(row_z)
            div_z = jnp.where(is_low, pltpu.roll(div_z, 6, 0), pltpu.roll(div_z, 2, 0))
            local[near, where[j]] = jnp.where(own_four, rest - div_z, local[near, where[j]])
            flow_x[near, where[j]] = jnp.where(own_two, pltpu.roll(part_x, 4, 0), flow_x[near, where[j]])

    def finish(rows, out_rows, start, count):
        where = [at(t % n_tiles + 1) for t in range(start - 1, start + count + 1)]
        fields = [flow_x[rows, w] for w in where]
        turned = [swap_halves(f) for f in fields]
        for j in range(1, count + 1):
            div_x = along_x(fields[j - 1], turned[j - 1], turned[j], fields[j + 1], turned[j + 1], low)
            pot_ref[out_rows, at((start + j - 1) % n_tiles)] = local[rows, where[j]] - div_x

    def unpack(m):
        for k in range(2):
            from_edge(m, k).wait_recv()
        for t in range(tiles):
            both = edge_in[0, :, at(m * tiles + t)] + edge_in[1, :, at(m * tiles + t)]
            turned = pltpu.roll(both, 4, 0)
            outer[:, at(2 * m * tiles + t + 1)] = jnp.where(first_rows, both, turned)
            outer[:, at((2 * m + 1) * tiles + t + 1)] = jnp.where(first_rows, turned, both)

    for i in range(CHUNKS):
        total(far, i)
        to_inner(i).start()
    for i in range(CHUNKS):
        total(near, i)
        to_inner(i).wait_recv()
        if i == 0:
            first_pass(1, tiles - 2)
        elif i < CHUNKS - 1:
            first_pass(i * tiles - 1, tiles)
        else:
            first_pass(i * tiles - 1, tiles + 2)
    finish(far, far_out, 0, n_tiles)
    to_pot_far().start()
    unpack(0)
    second_pass(1, 2 * tiles - 2)
    finish(near, near_out, *PARTS[0])
    to_pot(0).start()
    unpack(1)
    second_pass(2 * tiles - 1, 2 * tiles + 2)
    finish(near, near_out, PARTS[1][0], PARTS[1][1] + PARTS[2][1])
    for i in (1, 2):
        to_pot(i).start()
    for i in range(len(PARTS)):
        to_pot(i).wait_recv()
    to_pot_far().wait_recv()
    for k in range(2):
        remote(part, part, sent.at[k], edge_recv.at[0], core_peer).wait_send()


def apply_kernel(held_ref, pot_ref, applied_ref, out_ref, staged, store_sem, pot_sem):
    s_dev, planes, cells = held_ref.shape
    width = cells // STORES
    pot_copy = pltpu.make_async_copy(pot_ref, out_ref, pot_sem)
    pot_copy.start()

    def store(i):
        cols = pl.ds(i * width, width)
        return pltpu.make_async_copy(staged.at[:, :, cols], applied_ref.at[:, :, cols], store_sem.at[i])

    for i in range(STORES):
        cols = pl.ds(i * width, width)
        pot = pot_ref[:, cols].astype(jnp.bfloat16)

        def state_step(s, carry):
            staged[s, :, cols] = held_ref[s, :, cols] * pot
            return carry

        lax.fori_loop(0, s_dev, state_step, 0, unroll=8)
        store(i).start()
    for i in range(STORES):
        store(i).wait()
    pot_copy.wait()


def body(slabs, states, core_density, occupancy):
    s_dev, planes, cells = states.shape
    half = planes // 2
    vmem = pl.BlockSpec(memory_space=pltpu.VMEM)
    hbm = pl.BlockSpec(memory_space=pltpu.HBM)
    states = pltpu.with_memory_space_constraint(states, pltpu.HBM)
    core_density = pltpu.with_memory_space_constraint(core_density, pltpu.HBM)
    occupancy = pltpu.with_memory_space_constraint(occupancy, pltpu.HBM)

    def rows(count):
        return pltpu.VMEM((count, cells), jnp.float32)

    def wide(count):
        return pltpu.VMEM((count, cells + 2 * LANES), jnp.float32)

    def sems(count):
        return pltpu.SemaphoreType.DMA((count,))

    held, pot = pl.pallas_call(
        functools.partial(potential_kernel, slabs),
        out_shape=(
            pltpu.VMEM((s_dev, planes, cells), jnp.bfloat16),
            pltpu.VMEM((planes, cells), jnp.float32),
        ),
        in_specs=[hbm, hbm, hbm],
        out_specs=(vmem, vmem),
        scratch_shapes=[
            pltpu.SMEM((s_dev,), jnp.int32),
            pltpu.VMEM((2, half, cells), jnp.float32),
            rows(half),
            rows(half),
            rows(half),
            rows(half),
            wide(half),
            wide(8),
            pltpu.VMEM((8, cells // 2), jnp.float32),
            pltpu.VMEM((2, 8, cells // 2), jnp.float32),
            wide(8),
            wide(half),
            wide(half),
            wide(8),
            wide(8),
            sems(LOADS + CHUNKS),
            sems(2),
            pltpu.SemaphoreType.REGULAR,
            pltpu.SemaphoreType.REGULAR,
        ]
        + [sems(2), sems(CHUNKS), sems(2 * CHUNKS), sems(CHUNKS), sems(4), sems(len(PARTS) + 1)],
        compiler_params=pltpu.CompilerParams(
            collective_id=0, has_side_effects=True, vmem_limit_bytes=24 * 1024 * 1024
        ),
        name="potential",
    )(occupancy, states, core_density)
    return pl.pallas_call(
        apply_kernel,
        out_shape=(
            jax.ShapeDtypeStruct((s_dev, planes, cells), jnp.bfloat16),
            jax.ShapeDtypeStruct((planes, cells), jnp.float32),
        ),
        in_specs=[vmem, vmem],
        out_specs=(hbm, hbm),
        scratch_shapes=[
            pltpu.VMEM((s_dev, planes, cells), jnp.bfloat16),
            sems(STORES),
            pltpu.SemaphoreType.DMA,
        ],
        compiler_params=pltpu.CompilerParams(vmem_limit_bytes=32 * 1024 * 1024),
        name="apply",
    )(held, pot)


def solution(mesh):
    placed = (P("grp", "slab", None), P("slab", None), P("grp"))
    return jax.shard_map(
        functools.partial(body, mesh.shape["slab"]),
        mesh=mesh,
        in_specs=placed,
        out_specs=(P("grp", "slab", None), P("slab", None)),
        check_vma=False,
    )
```

```python
import functools
import math

import jax
import jax.numpy as jnp
from jax import lax
from jax.experimental import pallas as pl
from jax.experimental.pallas import tpu as pltpu
from jax.sharding import PartitionSpec as P

MESH = pl.DeviceIdType.MESH

NX = 64
NY = 64
OCC_DEN = 8
LANES = 128

grid_step = 0.5
valence_norm = 0.04

kappa = 0.804
mu = 0.2195149727645171
exchange = -0.75 * (3.0 / math.pi) ** (1.0 / 3.0)
reduced_scale = 4.0 * (3.0 * math.pi**2) ** (2.0 / 3.0)
stencil_scale = 1.0 / (12.0 * grid_step)
u_scale = mu / kappa / reduced_scale * stencil_scale * stencil_scale
flow_scale = 2.0 * exchange * mu / reduced_scale * stencil_scale * stencil_scale
slope_scale = exchange * 4.0 / 3.0

CHUNKS = 4
STEP = 4 * LANES
LOADS = 8
GATE = 1
PARTS = ((2, 12), (14, 18), (0, 2))
STORES = 4


def stencil(before2, before1, after1, after2):
    return (before2 - after2) + 8.0 * (after1 - before1)


def swap_halves(tile):
    return pltpu.roll(tile, 64, 1)


def along_y(tile, swapped, inner):
    before2 = pltpu.roll(jnp.where(inner >= NY - 2, swapped, tile), 2, 1)
    before1 = pltpu.roll(jnp.where(inner >= NY - 1, swapped, tile), 1, 1)
    after1 = pltpu.roll(jnp.where(inner < 1, swapped, tile), LANES - 1, 1)
    after2 = pltpu.roll(jnp.where(inner < 2, swapped, tile), LANES - 2, 1)
    return stencil(before2, before1, after1, after2)


def along_x(left, left_swapped, swapped, right, right_swapped, low):
    before1 = jnp.where(low, left_swapped, swapped)
    after1 = jnp.where(low, swapped, right_swapped)
    return stencil(left, before1, after1, right)


def along_z(tile):
    rows = tile.shape[0]
    return stencil(
        pltpu.roll(tile, 2, 0),
        pltpu.roll(tile, 1, 0),
        pltpu.roll(tile, rows - 1, 0),
        pltpu.roll(tile, rows - 2, 0),
    )


def potential_kernel(
    slabs,
    occ_hbm,
    states_ref,
    core_ref,
    held_ref,
    pot_ref,
    occ_ref,
    part,
    from_core,
    chip_sum,
    from_chip,
    core_half,
    dens,
    inner_in,
    edge_out,
    edge_in,
    outer,
    flow_x,
    local,
    near_rest,
    near_z,
    load_sem,
    misc_sem,
    group_sem,
    slab_sem,
    sent,
    core_recv,
    chip_recv,
    inner_recv,
    edge_recv,
    pot_recv,
):
    s_dev, planes, cells = states_ref.shape
    half = planes // 2
    width = cells // CHUNKS
    n_tiles = cells // LANES

    grp = lax.axis_index("grp")
    slab = lax.axis_index("slab")
    chip = grp // 2
    upper = 1 - grp % 2
    core_peer = {"grp": chip * 2 + upper, "slab": slab}
    chip_peer = {"grp": (1 - chip) * 2 + 1 - upper, "slab": slab}
    cross_peer = {"grp": (1 - chip) * 2 + upper, "slab": slab}
    beyond = (slab + slabs - 1 + 2 * upper) % slabs
    wrapped = slab % 8 == 0
    rushed = (slab % 8 == 7) & (upper == 1)
    edge_chips = (0, 1)

    near = pl.ds(pl.multiple_of(upper * 8, 8), 8)
    far = pl.ds(pl.multiple_of((1 - upper) * 8, 8), 8)

    def cols(i):
        return pl.ds(pl.multiple_of(i * width, LANES), width)

    def load(h, i):
        span = STEP if h == 1 else width
        where = (slice(None), pl.ds(h * half, half), pl.ds(pl.multiple_of(i * span, STEP), span))
        return pltpu.make_async_copy(states_ref.at[where], held_ref.at[where], load_sem.at[h * CHUNKS + i])

    def remote(src, dst, send, recv, peer):
        return pltpu.make_async_remote_copy(
            src_ref=src, dst_ref=dst, send_sem=send, recv_sem=recv, device_id=peer, device_id_type=MESH
        )

    def to_core(i):
        return remote(
            part.at[1 - upper, :, cols(i)], from_core.at[:, cols(i)], sent.at[0], core_recv.at[i], core_peer
        )

    def to_chip(rows, i):
        tile_at = (rows, cols(i))
        which = i + CHUNKS * (rows is near)
        return remote(chip_sum.at[tile_at], from_chip.at[tile_at], sent.at[0], chip_recv.at[which], chip_peer)

    def edge_cols(m):
        return slice(m * width, (m + 1) * width)

    def to_edge(m, k):
        peer = {"grp": edge_chips[k] * 2 + upper, "slab": beyond}
        out = edge_out.at[:, edge_cols(m)]
        return remote(out, edge_in.at[chip, :, edge_cols(m)], sent.at[1], edge_recv.at[2 * m + chip], peer)

    def from_edge(m, k):
        out = edge_out.at[:, edge_cols(m)]
        return remote(out, edge_in.at[k, :, edge_cols(m)], sent.at[1], edge_recv.at[2 * m + k], core_peer)

    def shifted(i):
        return pl.ds(pl.multiple_of(i * width + LANES, LANES), width)

    def to_inner(i):
        return remote(
            dens.at[far, shifted(i)], inner_in.at[:, shifted(i)], sent.at[1], inner_recv.at[i], core_peer
        )

    def own_rows():
        return pl.ds(pl.multiple_of(upper * half, half), half)

    near_out = pl.ds(pl.multiple_of(upper * 24, 8), 8)
    far_out = pl.ds(pl.multiple_of(8 + upper * 8, 8), 8)

    def to_pot(i):
        start, count = PARTS[i]
        where = pot_ref.at[near_out, pl.ds(start * LANES, count * LANES)]
        return remote(where, where, sent.at[1], pot_recv.at[i], core_peer)

    def to_pot_far():
        where = pot_ref.at[far_out, :]
        return remote(where, where, sent.at[1], pot_recv.at[len(PARTS)], core_peer)

    barrier = pltpu.get_barrier_semaphore()

    def greet(peer):
        pl.semaphore_signal(barrier, inc=1, device_id=peer, device_id_type=MESH)

    @pl.when(upper == 0)
    def _():
        greet(chip_peer)
        greet({"grp": 0, "slab": beyond})
        greet({"grp": 2, "slab": beyond})

    @pl.when(upper == 1)
    def _():
        greet(core_peer)
        greet(cross_peer)
        greet({"grp": 0, "slab": beyond})
        greet({"grp": 2, "slab": beyond})

    occ_copy = pltpu.make_async_copy(occ_hbm, occ_ref, misc_sem.at[0])
    occ_copy.start()
    for i in range(LOADS):
        load(1, i).start()
    core_copy = pltpu.make_async_copy(core_ref.at[own_rows(), :], core_half, misc_sem.at[1])
    core_copy.start()
    for i in range(CHUNKS):
        load(0, i).start()

    occ_copy.wait()
    weights = [
        occ_ref[s].astype(jnp.float32) * (valence_norm / (OCC_DEN * s_dev * 4))
        for s in range(s_dev)
    ]

    def density_part(h, i):
        if h == 0:
            load(0, i).wait()

        def tile_step(t, carry):
            if h == 1:
                load(1, i * (width // STEP) + t).wait()
            lanes = pl.ds(pl.multiple_of(i * width + t * STEP, STEP), STEP)
            total = jnp.zeros((half, STEP), jnp.float32)
            for s in range(s_dev):
                wide = held_ref[s, h * half : (h + 1) * half, lanes].astype(jnp.float32)
                total = total + (wide * weights[s]) * wide
            part[h, :, lanes] = total
            return carry

        lax.fori_loop(0, width // STEP, tile_step, 0)

    first_rows = lax.broadcasted_iota(jnp.int32, (8, LANES), 0) < 4
    with_core = (1 - chip).astype(jnp.float32)
    is_low = upper == 0

    def sum_chip(i):
        to_core(i).wait_recv()
        chip_sum[:, cols(i)] = (part[upper, :, cols(i)] + from_core[:, cols(i)]) + with_core * core_half[:, cols(i)]

    def pack(m):
        edge_rows = pl.ds(pl.multiple_of(upper * 8, 8), 8)
        for t in range(width // LANES):
            here = 2 * m * width + t * LANES
            front = chip_sum[edge_rows, here : here + LANES]
            back = chip_sum[edge_rows, here + width : here + width + LANES]
            front_turned, back_turned = pltpu.roll(front, 4, 0), pltpu.roll(back, 4, 0)
            low_edge = jnp.where(first_rows, front, back_turned)
            high_edge = jnp.where(first_rows, front_turned, back)
            edge_out[:, m * width + t * LANES : m * width + (t + 1) * LANES] = jnp.where(is_low, low_edge, high_edge)

    def send_edges(m):
        for k in range(2):
            to_edge(m, k).start()

    def meet_slabs():
        @pl.when(upper == 1)
        def _():
            pl.semaphore_wait(barrier, 4)
            pl.semaphore_signal(slab_sem, inc=1, device_id=core_peer, device_id_type=MESH)

        @pl.when(upper == 0)
        def _():
            pl.semaphore_wait(slab_sem, 1)

    def sum_and_send(m):
        for i in (2 * m, 2 * m + 1):
            sum_chip(i)
        pack(m)

        @pl.when(jnp.logical_not(wrapped))
        def _():
            if m == 0:
                meet_slabs()
            send_edges(m)

        @pl.when(jnp.logical_not(rushed))
        def _():
            for i in (2 * m, 2 * m + 1):
                to_chip(far, i).start()

        if m == 1:

            @pl.when(rushed)
            def _():
                for i in range(CHUNKS):
                    to_chip(far, i).start()

            for i in range(CHUNKS):
                to_chip(near, i).start()

    for i in range(CHUNKS):
        density_part(1, i)
        if i == GATE:

            @pl.when(upper == 0)
            def _():
                pl.semaphore_wait(barrier, 3)
                pl.semaphore_signal(group_sem, inc=1, device_id=core_peer, device_id_type=MESH)
                for j in range(GATE):
                    to_core(j).start()

        if i >= GATE:

            @pl.when(upper == 0)
            def _():
                to_core(i).start()

    core_copy.wait()
    for i in range(CHUNKS):
        if i == 0:
            @pl.when(upper == 1)
            def _():
                pl.semaphore_wait(group_sem, 1)
                for m in range(2):
                    sum_and_send(m)
        density_part(0, i)

        @pl.when(upper == 1)
        def _():
            to_core(i).start()

    @pl.when(upper == 0)
    def _():
        for m in range(2):
            sum_and_send(m)

    @pl.when(wrapped)
    def _():
        meet_slabs()
        for m in range(2):
            send_edges(m)

    lane = lax.broadcasted_iota(jnp.int32, (1, LANES), 1)
    inner = lane % NY
    low = lane < NY
    row = lax.broadcasted_iota(jnp.int32, (8, LANES), 0)
    own_four = jnp.where(is_low, row, 7 - row) < 4
    own_two = jnp.where(is_low, row, 7 - row) < 2

    tiles = width // LANES

    def at(j):
        return slice(j * LANES, (j + 1) * LANES)

    def total(rows, i):
        to_chip(rows, i).wait_recv()
        dens[rows, shifted(i)] = chip_sum[rows, cols(i)] + from_chip[rows, cols(i)]

    def flows(fields, turned, j):
        centre = fields[j]
        grad_x = along_x(fields[j - 1], turned[j - 1], turned[j], fields[j + 1], turned[j + 1], low)
        grad_y = along_y(centre, turned[j], inner)
        grad_z = along_z(centre)
        sigma = grad_x * grad_x + grad_y * grad_y + grad_z * grad_z
        root = jnp.exp2(jnp.log2(centre) * (-1.0 / 3.0))
        root2 = root * root
        root4 = root2 * root2
        share = 1.0 / (1.0 + u_scale * (sigma * (root4 * root4)))
        flow = flow_scale * (root4 * (share * share))
        d_dens = (slope_scale * (centre * root2)) * (
            (1.0 + kappa) + share * (2.0 * kappa * share - 3.0 * kappa)
        )
        return flow * grad_x, flow * grad_y, flow * grad_z, d_dens

    def first_pass(start, count):
        where = [at(t % n_tiles + 1) for t in range(start - 1, start + count + 1)]
        fields = [jnp.concatenate([dens[:, w], inner_in[:, w]], axis=0) for w in where]
        turned = [swap_halves(f) for f in fields]
        for j in range(1, count + 1):
            part_x, part_y, part_z, d_dens = flows(fields, turned, j)
            part_y = part_y[:half]
            rest = d_dens[:half] - along_y(part_y, swap_halves(part_y), inner)
            flow_x[:, where[j]] = part_x[:half]
            local[:, where[j]] = rest - along_z(part_z)[:half]
            near_rest[:, where[j]] = jnp.where(is_low, rest[:8], rest[8:])
            near_z[:, where[j]] = jnp.where(is_low, part_z[:8], part_z[8:half])

    def second_pass(start, count):
        where = [at(t % n_tiles + 1) for t in range(start - 1, start + count + 1)]
        fields = [jnp.where(own_four, outer[:, w], pltpu.roll(dens[near, w], 4, 0)) for w in where]
        turned = [swap_halves(f) for f in fields]
        for j in range(1, count + 1):
            part_x, part_y, part_z, d_dens = flows(fields, turned, j)
            rest = d_dens - along_y(part_y, swap_halves(part_y), inner)
            rest = jnp.where(own_two, pltpu.roll(rest, 4, 0), near_rest[:, where[j]])
            old_z = near_z[:, where[j]]
            row_z = jnp.where(
                first_rows,
                pltpu.roll(jnp.where(is_low, part_z, old_z), 6, 0),
                pltpu.roll(jnp.where(is_low, old_z, part_z), 2, 0),
            )
            div_z = along_z(row_z)
            div_z = jnp.where(is_low, pltpu.roll(div_z, 6, 0), pltpu.roll(div_z, 2, 0))
            local[near, where[j]] = jnp.where(own_four, rest - div_z, local[near, where[j]])
            flow_x[near, where[j]] = jnp.where(own_two, pltpu.roll(part_x, 4, 0), flow_x[near, where[j]])

    def finish(rows, out_rows, start, count):
        where = [at(t % n_tiles + 1) for t in range(start - 1, start + count + 1)]
        fields = [flow_x[rows, w] for w in where]
        turned = [swap_halves(f) for f in fields]
        for j in range(1, count + 1):
            div_x = along_x(fields[j - 1], turned[j - 1], turned[j], fields[j + 1], turned[j + 1], low)
            pot_ref[out_rows, at((start + j - 1) % n_tiles)] = local[rows, where[j]] - div_x

    def unpack(m):
        for k in range(2):
            from_edge(m, k).wait_recv()
        for t in range(tiles):
            both = edge_in[0, :, at(m * tiles + t)] + edge_in[1, :, at(m * tiles + t)]
            turned = pltpu.roll(both, 4, 0)
            outer[:, at(2 * m * tiles + t + 1)] = jnp.where(first_rows, both, turned)
            outer[:, at((2 * m + 1) * tiles + t + 1)] = jnp.where(first_rows, turned, both)

    for i in range(CHUNKS):
        total(far, i)
        to_inner(i).start()
    for i in range(CHUNKS):
        total(near, i)
        to_inner(i).wait_recv()
        if i == 0:
            first_pass(1, tiles - 2)
        elif i < CHUNKS - 1:
            first_pass(i * tiles - 1, tiles)
        else:
            first_pass(i * tiles - 1, tiles + 2)
    finish(far, far_out, 0, n_tiles)
    to_pot_far().start()
    unpack(0)
    second_pass(1, 2 * tiles - 2)
    finish(near, near_out, *PARTS[0])
    to_pot(0).start()
    unpack(1)
    second_pass(2 * tiles - 1, 2 * tiles + 2)
    finish(near, near_out, PARTS[1][0], PARTS[1][1] + PARTS[2][1])
    for i in (1, 2):
        to_pot(i).start()
    for i in range(len(PARTS)):
        to_pot(i).wait_recv()
    to_pot_far().wait_recv()
    for k in range(2):
        remote(part, part, sent.at[k], edge_recv.at[0], core_peer).wait_send()


def apply_kernel(held_ref, pot_ref, applied_ref, out_ref, staged, store_sem, pot_sem):
    s_dev, planes, cells = held_ref.shape
    width = cells // STORES
    pot_copy = pltpu.make_async_copy(pot_ref, out_ref, pot_sem)
    pot_copy.start()

    def store(i):
        cols = pl.ds(i * width, width)
        return pltpu.make_async_copy(staged.at[:, :, cols], applied_ref.at[:, :, cols], store_sem.at[i])

    for i in range(STORES):
        cols = pl.ds(i * width, width)
        pot = pot_ref[:, cols].astype(jnp.bfloat16)

        def state_step(s, carry):
            staged[s, :, cols] = held_ref[s, :, cols] * pot
            return carry

        lax.fori_loop(0, s_dev, state_step, 0, unroll=8)
        store(i).start()
    for i in range(STORES):
        store(i).wait()
    pot_copy.wait()


def body(slabs, states, core_density, occupancy):
    s_dev, planes, cells = states.shape
    half = planes // 2
    vmem = pl.BlockSpec(memory_space=pltpu.VMEM)
    hbm = pl.BlockSpec(memory_space=pltpu.HBM)
    states = pltpu.with_memory_space_constraint(states, pltpu.HBM)
    core_density = pltpu.with_memory_space_constraint(core_density, pltpu.HBM)
    occupancy = pltpu.with_memory_space_constraint(occupancy, pltpu.HBM)

    def rows(count):
        return pltpu.VMEM((count, cells), jnp.float32)

    def wide(count):
        return pltpu.VMEM((count, cells + 2 * LANES), jnp.float32)

    def sems(count):
        return pltpu.SemaphoreType.DMA((count,))

    held, pot = pl.pallas_call(
        functools.partial(potential_kernel, slabs),
        out_shape=(
            pltpu.VMEM((s_dev, planes, cells), jnp.bfloat16),
            pltpu.VMEM((planes, cells), jnp.float32),
        ),
        in_specs=[hbm, hbm, hbm],
        out_specs=(vmem, vmem),
        scratch_shapes=[
            pltpu.SMEM((s_dev,), jnp.int32),
            pltpu.VMEM((2, half, cells), jnp.float32),
            rows(half),
            rows(half),
            rows(half),
            rows(half),
            wide(half),
            wide(8),
            pltpu.VMEM((8, cells // 2), jnp.float32),
            pltpu.VMEM((2, 8, cells // 2), jnp.float32),
            wide(8),
            wide(half),
            wide(half),
            wide(8),
            wide(8),
            sems(LOADS + CHUNKS),
            sems(2),
            pltpu.SemaphoreType.REGULAR,
            pltpu.SemaphoreType.REGULAR,
        ]
        + [sems(2), sems(CHUNKS), sems(2 * CHUNKS), sems(CHUNKS), sems(4), sems(len(PARTS) + 1)],
        compiler_params=pltpu.CompilerParams(
            collective_id=0, has_side_effects=True, vmem_limit_bytes=24 * 1024 * 1024
        ),
        name="potential",
    )(occupancy, states, core_density)
    return pl.pallas_call(
        apply_kernel,
        out_shape=(
            jax.ShapeDtypeStruct((s_dev, planes, cells), jnp.bfloat16),
            jax.ShapeDtypeStruct((planes, cells), jnp.float32),
        ),
        in_specs=[vmem, vmem],
        out_specs=(hbm, hbm),
        scratch_shapes=[
            pltpu.VMEM((s_dev, planes, cells), jnp.bfloat16),
            sems(STORES),
            pltpu.SemaphoreType.DMA,
        ],
        compiler_params=pltpu.CompilerParams(vmem_limit_bytes=32 * 1024 * 1024),
        name="apply",
    )(held, pot)


def solution(mesh):
    placed = (P("grp", "slab", None), P("slab", None), P("grp"))
    return jax.shard_map(
        functools.partial(body, mesh.shape["slab"]),
        mesh=mesh,
        in_specs=placed,
        out_specs=(P("grp", "slab", None), P("slab", None)),
        check_vma=False,
    )
```
